128 devices in a mesh: dom: 8 (over z, core), orient: 16 (over y, x).
Axes of the slice: x: 4, y: 4, z: 4, core: 2. Of those that a mesh axis runs over, the one named last changes fastest.
Arguments:
- images: bfloat16 [2048, 2, 4096], P(('dom', 'orient'))
- references: bfloat16 [512, 2, 4096], P('orient'), as said below
- noise_weight: float32 [4096], replicated, may hold values from 0.5 to 2
- candidate_ids: int32 [2048, 16, 8], P(('dom', 'orient')), may hold values from 0 to 31, as said below
- candidate_mask: int32 [2048, 16, 8], P(('dom', 'orient')), may hold values from 0 to 1, as said below
- shifts: int32 [25, 2], replicated, may hold values from -4 to 4
Outputs:
- image_sums: float32 [512, 2, 4096], P('orient', None, 'dom')
- totals: float32 [512], P('orient')
- log_evidence: float32 [2048], P(('dom', 'orient'))
The draws below stay inside these ranges and needn't reach their ends.
Inputs may be any that keep to these rules, and one draw needn't show every extreme that they name: `references`: fourier coefficients of the projections. Slot c of owner j for particle p names orientation j * 32 + candidate_ids[p, j, c]; names may repeat and then count once per valid slot. `candidate_mask`: 1 marks a valid slot; every particle has at least one valid slot.
All inputs are finite; a program needn't handle non-finite values.
Results may differ from the reference program's by a relative error of at most 0.0028.
Values may be sent and summed in bfloat16 or wider, within the bound.
No kernel may reach another device: no remote copies, remote signals or barrier semaphores. Data moves between devices by JAX's collectives and lax.ppermute only.
A program may use at most 192 MiB of HBM per device.

```python
import math
import jax
import jax.numpy as jnp
from jax import lax

GRID = 64
K = 4096
BOX = 400
NTRANS = 25
CAP = 8
O_DEV = 32
P_SIZE = 2048
O = 512
N_ORIENT = 16


def shared_draw(key):
    subkeys = jax.random.split(key, 7)
    ref_values = jnp.clip(0.03 * jax.random.normal(subkeys[0], (O, 2, K), jnp.float32), -0.2, 0.2)
    first_owner = jax.random.randint(subkeys[1], (P_SIZE,), 0, N_ORIENT)
    second_owner = jax.random.randint(subkeys[2], (P_SIZE,), 0, N_ORIENT)
    offset = jax.random.randint(subkeys[3], (), 0, N_ORIENT)
    home_owner = (jnp.minimum(first_owner, second_owner) + offset) % N_ORIENT
    local_ids = jax.random.randint(subkeys[4], (P_SIZE, N_ORIENT, CAP), 0, O_DEV)
    dice_roll = jax.random.randint(subkeys[5], (P_SIZE, N_ORIENT, CAP), 0, 10)
    owner_index = jnp.arange(N_ORIENT, dtype=jnp.int32)[None, :, None]
    home_cell = home_owner[:, None, None]
    distance = jnp.minimum((owner_index - home_cell) % N_ORIENT, (home_cell - owner_index) % N_ORIENT)
    slot_index = jnp.arange(CAP, dtype=jnp.int32)[None, None, :]
    valid = jnp.where(distance <= 1, dice_roll < 9, dice_roll < 3) | (distance == 0) & (slot_index < 2)
    valid_mask = valid.astype(jnp.int32)
    shift_values = jax.random.randint(subkeys[6], (NTRANS, 2), -4, 5)
    return (ref_values, local_ids, valid_mask, shift_values)


def draw_images(key, part):
    key = jax.random.fold_in(key, 11)
    values = jnp.clip(jax.random.normal(key, (P_SIZE, 2, K), jnp.float32), -6.0, 6.0)
    return jnp.clip(values, -16.0, 16.0).astype(jnp.bfloat16)


def draw_references(key, part):
    return shared_draw(key)[0].astype(jnp.bfloat16)


def draw_candidate_ids(key, part):
    return shared_draw(key)[1]


def draw_candidate_mask(key, part):
    return shared_draw(key)[2]


def draw_shifts(key, part):
    return shared_draw(key)[3]


def setup_inputs(seed: int = 0) -> dict:
    keys = jax.random.split(jax.random.key(seed), 7)
    images = draw_images(jax.random.fold_in(keys[6], 71), 0)
    references = draw_references(jax.random.fold_in(keys[6], 71), 0)
    noise_weight = jnp.clip(jnp.exp(jax.random.uniform(keys[2], (K,), jnp.float32, math.log(0.5), math.log(2.0))), 0.5, 2.0)
    candidate_ids = draw_candidate_ids(jax.random.fold_in(keys[6], 71), 0)
    candidate_mask = draw_candidate_mask(jax.random.fold_in(keys[6], 71), 0)
    shifts = draw_shifts(jax.random.fold_in(keys[6], 71), 0)
    return {"images": images, "references": references, "noise_weight": noise_weight, "candidate_ids": candidate_ids, "candidate_mask": candidate_mask, "shifts": shifts}


def phase_table(shifts):
    coefficient = jnp.arange(GRID * GRID, dtype=jnp.int32)
    row_freq = coefficient // GRID - GRID // 2
    col_freq = coefficient % GRID - GRID // 2
    phase_turns = row_freq[None, :] * shifts[:, 0:1] + col_freq[None, :] * shifts[:, 1:2]
    angles = phase_turns.astype(jnp.float32) * (2.0 * math.pi / BOX)
    return jnp.cos(angles), jnp.sin(angles)


def shift_images(images, cosine_table, sine_table):
    real_part = images[:, 0, :].astype(jnp.float32)[:, None, :]
    imag_part = images[:, 1, :].astype(jnp.float32)[:, None, :]
    moved_real = real_part * cosine_table[None] - imag_part * sine_table[None]
    moved_imag = real_part * sine_table[None] + imag_part * cosine_table[None]
    return jnp.stack([moved_real, moved_imag], axis=2).astype(jnp.bfloat16)


def weighted_refs(references, noise_weight):
    ref_values = references.astype(jnp.float32)
    scaled = (ref_values * noise_weight[None, None, :]).astype(jnp.bfloat16)
    half_norm = 0.5 * jnp.sum(noise_weight[None, None, :] * ref_values * ref_values, axis=(1, 2))
    return scaled, half_norm


def contract_cols(left, right):
    return lax.dot_general(left, right, (((1,), (1,)), ((), ())), preferred_element_type=jnp.float32)


def contract_rows(left, right):
    return lax.dot_general(left, right, (((0,), (0,)), ((), ())), preferred_element_type=jnp.float32)


def candidate_counts(global_ids, marks, number):
    matches = global_ids[:, :, None] == jnp.arange(number, dtype=jnp.int32)[None, None, :]
    return jnp.sum(jnp.where(matches, marks[:, :, None], 0), axis=1).astype(jnp.float32)


def posterior(scores, counts):
    usable = (counts > 0)[:, None, :]
    highest = jnp.max(jnp.where(usable, scores, jnp.float32(-1e30)), axis=(1, 2))
    terms = jnp.where(usable, counts[:, None, :] * jnp.exp(scores - highest[:, None, None]), jnp.float32(0.0))
    return highest, jnp.sum(terms, axis=(1, 2))


def weights_from(scores, counts, evidence):
    usable = (counts > 0)[:, None, :]
    values = jnp.where(usable, counts[:, None, :] * jnp.exp(scores - evidence[:, None, None]), jnp.float32(0.0))
    return values.astype(jnp.bfloat16)


def reference(images, references, noise_weight, candidate_ids, candidate_mask, shifts):
    cosine_table, sine_table = phase_table(shifts)
    scaled, half_norm = weighted_refs(references, noise_weight)
    scaled_flat = scaled.reshape(O, 2 * K)
    owner_base = (jnp.arange(N_ORIENT, dtype=jnp.int32) * O_DEV)[None, :, None]
    global_ids = (candidate_ids + owner_base).reshape(P_SIZE, N_ORIENT * CAP)
    marks = candidate_mask.reshape(P_SIZE, N_ORIENT * CAP)
    block_rows = math.gcd(P_SIZE, 128)

    def accumulate(running, offset):
        image_sums, totals = running
        portion = lax.dynamic_slice_in_dim(images, offset, block_rows, 0)
        shifted = shift_images(portion, cosine_table, sine_table).reshape(block_rows * NTRANS, 2 * K)
        scores = contract_cols(shifted, scaled_flat).reshape(block_rows, NTRANS, O) - half_norm[None, None, :]
        counts = candidate_counts(lax.dynamic_slice_in_dim(global_ids, offset, block_rows, 0),
                                  lax.dynamic_slice_in_dim(marks, offset, block_rows, 0), O)
        highest, summed = posterior(scores, counts)
        evidence = highest + jnp.log(summed)
        flat_weights = weights_from(scores, counts, evidence).reshape(block_rows * NTRANS, O)
        image_sums = image_sums + contract_rows(flat_weights, shifted)
        totals = totals + jnp.sum(flat_weights.astype(jnp.float32), axis=0)
        return (image_sums, totals), evidence

    block_starts = jnp.arange(P_SIZE // block_rows, dtype=jnp.int32) * block_rows
    start_state = (jnp.zeros((O, 2 * K), jnp.float32), jnp.zeros((O,), jnp.float32))
    (image_sums, totals), evidence = lax.scan(accumulate, start_state, block_starts)
    return image_sums.reshape(O, 2, K), totals, evidence.reshape(P_SIZE)
```

```python
import math

import jax
import jax.numpy as jnp
from jax import lax
from jax.experimental import pallas as pl
from jax.experimental.pallas import tpu as pltpu
from jax.sharding import PartitionSpec as P

GRID = 64
K = 4096
BOX = 400
NTRANS = 25
CAP = 8
ZN = 4
YN = 4
XN = 4
DOM = 8
PART = 16
KS = K // DOM
K2 = 2 * KS
EXT = 128
KE = K2 + EXT
SLOTS = 128
OD = 32
YB = XN * OD
TC = 5
STEPS = NTRANS // TC
HALF = ZN * PART
ROWS = TC * HALF
BF = jnp.bfloat16
F32 = jnp.float32
VMEM_LIMIT = 56 * 1024 * 1024


def nt(left, right):
    return lax.dot_general(
        left, right, (((1,), (1,)), ((), ())), preferred_element_type=F32
    )


def tn(left, right):
    return lax.dot_general(
        left, right, (((0,), (0,)), ((), ())), preferred_element_type=F32
    )


def params():
    return pltpu.CompilerParams(vmem_limit_bytes=VMEM_LIMIT)


def lanes(shape):
    return lax.broadcasted_iota(jnp.int32, shape, len(shape) - 1)


def split3(value):
    high = value.astype(BF)
    rest = value - high.astype(F32)
    mid = rest.astype(BF)
    low = (rest - mid.astype(F32)).astype(BF)
    return high.astype(F32), mid.astype(F32), low.astype(F32)


def refs_kernel(refs_ref, noise_ref, out_ref):
    d = lax.axis_index("dom")
    span = pl.ds(pl.multiple_of(d * KS, KS), KS)
    noise = noise_ref[:, span]
    total = jnp.zeros((OD, 1), F32)
    for part in range(2):
        values = refs_ref[:, part, span].astype(F32)
        out_ref[:, part * KS : (part + 1) * KS] = (values * noise).astype(BF)
        total = total + jnp.sum(noise * values * values, axis=1, keepdims=True)
    high, mid, low = split3(0.5 * total)
    lane = lanes((OD, EXT))
    packed = jnp.where(lane == 0, high, jnp.where(lane == 1, mid, jnp.where(lane == 2, low, 0.0)))
    out_ref[:, K2:] = packed.astype(BF)


def images_kernel(images_ref, code_ref, far_ref, near_ref):
    d = lax.axis_index("dom")
    z = d // 2
    core = d % 2
    code = code_ref[...].astype(F32).astype(BF)
    for rc, out_ref in ((0, near_ref), (1, far_ref)):
        for rz in range(ZN):
            zz = lax.rem(z + rz, ZN)
            cc = core if rc == 0 else 1 - core
            span = pl.ds(pl.multiple_of((zz * 2 + cc) * KS, KS), KS)
            for part in range(2):
                out_ref[rz, :, part * KS : (part + 1) * KS] = images_ref[:, part, span]
            out_ref[rz, :, K2:] = code


def slots_kernel(code_ref, inv_ref, count_ref):
    code = code_ref[...]
    rows = code.shape[0]
    lane = lanes((rows, SLOTS))
    for block in range(YN):
        inverse = jnp.zeros((rows, YB), jnp.int32)
        count = jnp.zeros((rows, YB), F32)
        for c in range(CAP):
            where_slot = (block * XN + lane // OD) * CAP + c
            seen = jnp.take_along_axis(code, where_slot, axis=1, mode="promise_in_bounds")
            match = seen == (lane % OD + OD)
            count = count + jnp.where(match, 1.0, 0.0)
            inverse = jnp.where(match, where_slot, inverse)
        inv_ref[:, block * YB : (block + 1) * YB] = inverse
        count_ref[:, block * YB : (block + 1) * YB] = count


def scores_kernel(rc, *refs):
    imgs = refs[0:ZN]
    refs_in = refs[ZN : ZN + YN]
    cos_ref, sin_ref = refs[ZN + YN : ZN + YN + 2]
    slot_ref, shift_ref = refs[ZN + YN + 2 : ZN + YN + 4]
    weight_ref, norm_ref, index_ref, value_ref = refs[ZN + YN + 4 :]
    step = pl.program_id(0)

    @pl.when(step == 0)
    def _():
        lane8 = lanes((8, EXT))
        ones = jnp.where(lane8 < 3, 1.0, 0.0).astype(BF)
        for y in range(YN):
            weight_ref[y * YB : (y + 1) * YB, :] = refs_in[y][:, :K2]
            norm_ref[:, y * YB : (y + 1) * YB] = nt(ones, refs_in[y][:, K2:])
        lane = lanes((HALF, SLOTS))
        for rz in range(ZN):
            rows = slice(rz * PART, (rz + 1) * PART)
            value_ref[rows, :] = imgs[rz][rc, :, :K2].astype(F32)
            index_ref[rows, :] = imgs[rz][rc, :, K2:].astype(F32).astype(jnp.int32)
        code = index_ref[...]
        local = jnp.where(code >= OD, code - OD, code)
        index_ref[...] = ((lane // CAP) % XN) * OD + local

    real = value_ref[:, :KS]
    imag = value_ref[:, KS:]
    for t in range(TC):
        row = step * TC + t
        cosine = cos_ref[pl.ds(row, 1), :]
        sine = sin_ref[pl.ds(row, 1), :]
        shift_ref[t, :, :KS] = (real * cosine - imag * sine).astype(BF)
        shift_ref[t, :, KS:] = (real * sine + imag * cosine).astype(BF)
    lane = lanes((HALF, SLOTS))
    index = index_ref[...]
    scores = nt(shift_ref[...].reshape(ROWS, K2), weight_ref[...])
    for t in range(TC):
        found = jnp.zeros((HALF, SLOTS), F32)
        for y in range(YN):
            span = slice(y * YB, (y + 1) * YB)
            block = scores[t * HALF : (t + 1) * HALF, span] - norm_ref[0:1, span]
            picked = jnp.take_along_axis(block, index, axis=1, mode="promise_in_bounds")
            found = jnp.where(lane // OD == y, picked, found)
        slot_ref[:, t] = found.reshape(ZN, PART, SLOTS)


def posterior_kernel(own_ref, one_ref, two_ref, three_ref, code_ref, weight_ref, evidence_ref):
    valid = code_ref[...] >= OD
    scores = own_ref[...] + one_ref[...] + two_ref[...] + three_ref[...]
    masked = jnp.where(valid[None], scores, -1e30)
    highest = jnp.max(jnp.max(masked, axis=0), axis=1, keepdims=True)
    terms = jnp.where(valid[None], jnp.exp(scores - highest[None]), 0.0)
    summed = jnp.sum(jnp.sum(terms, axis=0), axis=1, keepdims=True)
    evidence = highest + jnp.log(summed)
    weights = jnp.where(valid[None], jnp.exp(scores - evidence[None]), 0.0)
    weight_ref[...] = weights.astype(BF)
    evidence_ref[...] = jnp.broadcast_to(evidence, evidence_ref.shape)


def sums_kernel(near_ref, far_ref, near_shift, far_shift, inv_ref, count_ref, *refs):
    outs = refs[:XN]
    acc_ref, dense_ref, shift_ref = refs[XN:]
    step = pl.program_id(0)

    @pl.when(step == 0)
    def _():
        acc_ref[...] = jnp.zeros_like(acc_ref)

    for rc, (slot_ref, moved_ref) in enumerate(((near_ref, near_shift), (far_ref, far_shift))):
        for t in range(TC):
            slot = slot_ref[:, t].reshape(HALF, SLOTS).astype(F32)
            rows = slice(t * HALF, (t + 1) * HALF)
            particles = slice(rc * HALF, (rc + 1) * HALF)
            for y in range(YN):
                span = slice(y * YB, (y + 1) * YB)
                picked = jnp.take_along_axis(
                    slot, inv_ref[particles, span], axis=1, mode="promise_in_bounds"
                )
                dense_ref[rows, span] = (picked * count_ref[particles, span]).astype(BF)
        shift_ref[:, :K2] = moved_ref[...].reshape(ROWS, K2)
        shift_ref[:, K2:] = jnp.ones((ROWS, EXT), BF)
        acc_ref[...] += tn(dense_ref[...], shift_ref[...])

    @pl.when(step == STEPS - 1)
    def _():
        lane = lanes((OD, EXT))
        for y in range(YN):
            for x in range(XN):
                rows = slice((y * XN + x) * OD, (y * XN + x + 1) * OD)
                block = acc_ref[rows, :]
                total = block[:, K2:]
                high = total.astype(BF).astype(F32)
                packed = jnp.where(lane == 0, high, jnp.where(lane == 1, total - high, 0.0))
                outs[x][y, :, :K2] = block[:, :K2].astype(outs[x].dtype)
                outs[x][y, :, K2:] = packed.astype(outs[x].dtype)


def merge_kernel(own_ref, one_ref, two_ref, three_ref, *outs):
    lane = lanes((OD, EXT))
    for y in range(YN):
        block = own_ref[y]
        for other in (one_ref, two_ref, three_ref):
            block = block + other[y].astype(F32)
        total = jnp.sum(block[:, K2:], axis=1, keepdims=True)
        high = total.astype(BF).astype(F32)
        packed = jnp.where(lane == 0, high, jnp.where(lane == 1, total - high, 0.0))
        outs[y][:, :K2] = block[:, :K2].astype(outs[y].dtype)
        outs[y][:, K2:] = packed.astype(outs[y].dtype)


def final_kernel(own_ref, one_ref, two_ref, three_ref, sum_ref, total_ref):
    block = own_ref[...]
    for other in (one_ref, two_ref, three_ref):
        block = block + other[...].astype(F32)
    sum_ref[:, 0, :] = block[:, :KS]
    sum_ref[:, 1, :] = block[:, KS:K2]
    total = jnp.sum(block[:, K2:], axis=1, keepdims=True)
    total_ref[...] = jnp.broadcast_to(total, total_ref.shape)


def shape(dims, dtype):
    return jax.ShapeDtypeStruct(dims, dtype)


def dom_core():
    return [(d, d ^ 1) for d in range(DOM)]


def dom_z(step):
    return [(d, (d + 2 * step) % DOM) for d in range(DOM)]


def orient_x(step):
    return [(y * XN + x, y * XN + (x + step) % XN) for y in range(YN) for x in range(XN)]


def orient_y(step):
    return [(y * XN + x, ((y + step) % YN) * XN + x) for y in range(YN) for x in range(XN)]


ORDER = (2, 1, 3)


def phase_tables(shifts, d):
    coefficient = d * KS + jnp.arange(KS, dtype=jnp.int32)
    row_freq = coefficient // GRID - GRID // 2
    col_freq = coefficient % GRID - GRID // 2
    phase_turns = row_freq[None, :] * shifts[:, 0:1] + col_freq[None, :] * shifts[:, 1:2]
    angles = phase_turns.astype(F32) * (2.0 * math.pi / BOX)
    return jnp.cos(angles), jnp.sin(angles)


def gather_references(scaled):
    blocks = {0: scaled}
    for step in ORDER:
        blocks[(-step) % XN] = lax.ppermute(scaled, "orient", orient_x(step))
    line = jnp.concatenate([blocks[x] for x in range(XN)], axis=0)
    lines = {0: line}
    for step in ORDER:
        lines[(-step) % YN] = lax.ppermute(line, "orient", orient_y(step))
    return [lines[y] for y in range(YN)]


def trade_images(far, near):
    other = lax.ppermute(far, "dom", dom_core())
    both = jnp.stack([near, other], axis=1)
    pieces = {0: both[0]}
    for step in ORDER:
        pieces[(-step) % ZN] = lax.ppermute(both[step], "dom", dom_z(step))
    return [pieces[rz] for rz in range(ZN)]


def score_half(rc, pieces, lines, cosine, sine):
    whole = lambda dims: pl.BlockSpec(dims, lambda i: (0,) * len(dims))
    return pl.pallas_call(
        lambda *refs: scores_kernel(rc, *refs),
        grid=(STEPS,),
        in_specs=[whole((2, PART, KE))] * ZN + [whole((YB, KE))] * YN + [whole((NTRANS, KS))] * 2,
        out_specs=[
            pl.BlockSpec((ZN, TC, PART, SLOTS), lambda i: (0, i, 0, 0)),
            pl.BlockSpec((TC, HALF, K2), lambda i: (i, 0, 0)),
        ],
        out_shape=[
            shape((ZN, NTRANS, PART, SLOTS), F32),
            shape((NTRANS, HALF, K2), BF),
        ],
        scratch_shapes=[
            pltpu.VMEM((YN * YB, K2), BF),
            pltpu.VMEM((8, YN * YB), F32),
            pltpu.VMEM((HALF, SLOTS), jnp.int32),
            pltpu.VMEM((HALF, K2), F32),
        ],
        compiler_params=params(),
        cost_estimate=pl.CostEstimate(
            flops=2 * NTRANS * HALF * K2 * YN * YB, bytes_accessed=6 * 2**20, transcendentals=0
        ),
        name="scores",
    )(*pieces, *lines, cosine, sine)


def shards(images, references, noise_weight, candidate_ids, candidate_mask, shifts):
    d = lax.axis_index("dom")
    j = lax.axis_index("orient")
    scaled = pl.pallas_call(
        refs_kernel, out_shape=shape((OD, KE), BF), compiler_params=params(), name="scale"
    )(references, noise_weight.reshape(1, K))
    lines = gather_references(scaled)

    code = jnp.where(candidate_mask > 0, candidate_ids + OD, candidate_ids)
    code = code.reshape(PART, YN, XN, CAP)
    code = jnp.roll(code, -(j // XN), axis=1)
    code = jnp.roll(code, -(j % XN), axis=2).reshape(PART, SLOTS)
    far, near = pl.pallas_call(
        images_kernel,
        out_shape=[shape((ZN, PART, KE), BF)] * 2,
        compiler_params=params(),
        name="cut_images",
    )(images, code)
    pieces = trade_images(far, near)
    cosine, sine = phase_tables(shifts, d)

    group = jnp.concatenate(
        [pieces[rz][rc, :, K2:].astype(jnp.int32) for rc in range(2) for rz in range(ZN)], axis=0
    )
    inverse, counts = pl.pallas_call(
        slots_kernel,
        out_shape=[shape((2 * HALF, YN * YB), jnp.int32), shape((2 * HALF, YN * YB), F32)],
        compiler_params=params(),
        name="slot_map",
    )(group)

    far_slots, far_shift = score_half(1, pieces, lines, cosine, sine)
    partner = lax.ppermute(far_slots, "dom", dom_core())
    near_slots, near_shift = score_half(0, pieces, lines, cosine, sine)
    slots = near_slots + partner
    arrived = [lax.ppermute(slots[step], "dom", dom_z(step)) for step in ORDER]
    weights, evidence = pl.pallas_call(
        posterior_kernel,
        out_shape=[shape((NTRANS, PART, SLOTS), BF), shape((PART, SLOTS), F32)],
        compiler_params=params(),
        name="posterior",
    )(slots[0], *arrived, code)

    mine = {0: weights}
    for step in ORDER:
        mine[(-step) % ZN] = lax.ppermute(weights, "dom", dom_z(step))
    near_weights = jnp.stack([mine[rz] for rz in range(ZN)], axis=0)
    far_weights = lax.ppermute(near_weights, "dom", dom_core())

    outs = pl.pallas_call(
        sums_kernel,
        grid=(STEPS,),
        in_specs=[pl.BlockSpec((ZN, TC, PART, SLOTS), lambda i: (0, i, 0, 0))] * 2
        + [pl.BlockSpec((TC, HALF, K2), lambda i: (i, 0, 0))] * 2
        + [pl.BlockSpec((2 * HALF, YN * YB), lambda i: (0, 0))] * 2,
        out_specs=[pl.BlockSpec((YN, OD, KE), lambda i: (0, 0, 0))] * XN,
        out_shape=[shape((YN, OD, KE), F32 if x == 0 else BF) for x in range(XN)],
        scratch_shapes=[
            pltpu.VMEM((YN * YB, KE), F32),
            pltpu.VMEM((ROWS, YN * YB), BF),
            pltpu.VMEM((ROWS, KE), BF),
        ],
        compiler_params=params(),
        cost_estimate=pl.CostEstimate(
            flops=4 * NTRANS * HALF * K2 * YN * YB, bytes_accessed=10 * 2**20, transcendentals=0
        ),
        name="weighted_sums",
    )(near_weights, far_weights, near_shift, far_shift, inverse, counts)
    along_x = [lax.ppermute(outs[step], "orient", orient_x(step)) for step in ORDER]
    rows = pl.pallas_call(
        merge_kernel,
        out_shape=[shape((OD, KE), F32 if y == 0 else BF) for y in range(YN)],
        compiler_params=params(),
        name="merge_x",
    )(outs[0], *along_x)
    along_y = [lax.ppermute(rows[step], "orient", orient_y(step)) for step in ORDER]
    image_sums, totals = pl.pallas_call(
        final_kernel,
        out_shape=[shape((OD, 2, KS), F32), shape((OD, EXT), F32)],
        compiler_params=params(),
        name="merge_y",
    )(rows[0], *along_y)
    return image_sums, totals[:, 0], evidence[:, 0]


def solution(mesh):
    return jax.shard_map(
        shards,
        mesh=mesh,
        in_specs=(
            P(("dom", "orient"), None, None),
            P("orient", None, None),
            P(),
            P(("dom", "orient"), None, None),
            P(("dom", "orient"), None, None),
            P(),
        ),
        out_specs=(P("orient", None, "dom"), P("orient"), P(("dom", "orient"))),
        check_vma=False,
    )
```

```python
import math

import jax
import jax.numpy as jnp
from jax import lax
from jax.experimental import pallas as pl
from jax.experimental.pallas import tpu as pltpu
from jax.sharding import PartitionSpec as P

GRID = 64
K = 4096
BOX = 400
NTRANS = 25
CAP = 8
ZN = 4
YN = 4
XN = 4
DOM = 8
PART = 16
KS = K // DOM
K2 = 2 * KS
EXT = 128
KE = K2 + EXT
SLOTS = 128
OD = 32
YB = XN * OD
TC = 5
STEPS = NTRANS // TC
HALF = ZN * PART
ROWS = TC * HALF
BF = jnp.bfloat16
F32 = jnp.float32
BLOCK = 128
OWNERS = YN * XN
INSIDE = pl.BlockSpec(memory_space=pltpu.VMEM)


def nt(left, right):
    return lax.dot_general(
        left, right, (((1,), (1,)), ((), ())), preferred_element_type=F32
    )


def tn(left, right):
    return lax.dot_general(
        left, right, (((0,), (0,)), ((), ())), preferred_element_type=F32
    )


def params(mib=16):
    return pltpu.CompilerParams(vmem_limit_bytes=mib * 1024 * 1024)


def lanes(shape):
    return lax.broadcasted_iota(jnp.int32, shape, len(shape) - 1)


def split3(value):
    high = value.astype(BF)
    rest = value - high.astype(F32)
    mid = rest.astype(BF)
    low = (rest - mid.astype(F32)).astype(BF)
    return high, mid, low


def pack2(total, lane):
    high = total.astype(BF).astype(F32)
    return jnp.where(lane == 0, high, jnp.where(lane == 1, total - high, 0.0))


def refs_kernel(refs_ref, noise_ref, out_ref, slice_ref, sem):
    d = lax.axis_index("dom")
    span = pl.ds(pl.multiple_of(d * KS, KS), KS)
    copy = pltpu.make_async_copy(refs_ref.at[:, :, span], slice_ref, sem)
    copy.start()
    noise = noise_ref[:, span]
    copy.wait()
    total = jnp.zeros((OD, 1), F32)
    for part in range(2):
        values = slice_ref[:, part, :].astype(F32)
        out_ref[:, part * KS : (part + 1) * KS] = (values * noise).astype(BF)
        total = total + jnp.sum(noise * values * values, axis=1, keepdims=True)
    high, mid, low = split3(0.5 * total)
    lane = lanes((OD, EXT))
    packed = jnp.where(
        lane == 0,
        high.astype(F32),
        jnp.where(lane == 1, mid.astype(F32), jnp.where(lane == 2, low.astype(F32), 0.0)),
    )
    out_ref[:, K2:] = packed.astype(BF)


def images_kernel(images_ref, ids_ref, mask_ref, far_ref, near_ref, code_ref):
    d = lax.axis_index("dom")
    j = lax.axis_index("orient")
    z = d // 2
    core = lax.rem(d, 2)
    marked = jnp.where(mask_ref[...] > 0, ids_ref[...] + OD, ids_ref[...])
    flat = jnp.concatenate([marked[:, c, :] for c in range(CAP)], axis=1)
    lane = lanes((PART, SLOTS))
    owner = lane % OWNERS
    y = (owner // XN + j // XN) % YN
    x = (owner % XN + lax.rem(j, XN)) % XN
    source = (lane // OWNERS) * OWNERS + y * XN + x
    turned = jnp.take_along_axis(flat, source, axis=1, mode="promise_in_bounds")
    code_ref[...] = turned
    code = turned.astype(F32).astype(BF)
    for rc, out_ref in ((0, near_ref), (1, far_ref)):
        for rz in range(ZN):
            zz = lax.rem(z + rz, ZN)
            cc = core if rc == 0 else 1 - core
            span = pl.ds(pl.multiple_of((zz * 2 + cc) * KS, KS), KS)
            for part in range(2):
                out_ref[rz, :, part * KS : (part + 1) * KS] = images_ref[:, part, span]
            out_ref[rz, :, K2:] = code


def slots_kernel(p0_ref, p1_ref, p2_ref, p3_ref, inv_ref, count_ref):
    lane = lanes((HALF, SLOTS))
    for rc in range(2):
        code = jnp.concatenate(
            [ref[rc, :, K2:].astype(F32) for ref in (p0_ref, p1_ref, p2_ref, p3_ref)], axis=0
        ).astype(jnp.int32)
        rows = slice(rc * HALF, (rc + 1) * HALF)
        for block in range(YN):
            inverse = jnp.zeros((HALF, YB), jnp.int32)
            count = jnp.zeros((HALF, YB), F32)
            for c in range(CAP):
                where_slot = c * OWNERS + block * XN + lane // OD
                seen = jnp.take_along_axis(code, where_slot, axis=1, mode="promise_in_bounds")
                match = seen == (lane % OD + OD)
                count = count + jnp.where(match, 1.0, 0.0)
                inverse = jnp.where(match, where_slot, inverse)
            inv_ref[rows, block * YB : (block + 1) * YB] = inverse
            count_ref[rows, block * YB : (block + 1) * YB] = count


def scores_kernel(rc, *refs):
    imgs = refs[0:ZN]
    refs_in = refs[ZN : ZN + YN]
    cos_ref, sin_ref = refs[ZN + YN : ZN + YN + 2]
    outs = refs[ZN + YN + 2 : ZN + YN + 2 + (ZN if rc == 0 else 1)]
    weight_ref, shift_ref = refs[-2:]
    lane8 = lanes((8, EXT))
    ones = jnp.where(lane8 < 3, 1.0, 0.0).astype(BF)
    norms = []
    for y in range(YN):
        weight_ref[y * YB : (y + 1) * YB, :] = refs_in[y][:, :K2]
        norms.append(nt(ones, refs_in[y][:, K2:])[0:1])
    lane = lanes((HALF, SLOTS))
    code = jnp.concatenate([ref[rc, :, K2:].astype(F32) for ref in imgs], axis=0).astype(jnp.int32)
    index = (lane % XN) * OD + code % OD
    line = (lane % OWNERS) // XN
    value = jnp.concatenate([ref[rc, :, :K2].astype(F32) for ref in imgs], axis=0)
    real = value[:, :KS]
    imag = value[:, KS:]
    for step in range(STEPS):
        base = step * ROWS
        for t in range(TC):
            row = step * TC + t
            cosine = cos_ref[row : row + 1, :]
            sine = sin_ref[row : row + 1, :]
            rows = slice(base + t * HALF, base + (t + 1) * HALF)
            shift_ref[rows, :KS] = (real * cosine - imag * sine).astype(BF)
            shift_ref[rows, KS:] = (real * sine + imag * cosine).astype(BF)
        scores = nt(shift_ref[base : base + ROWS, :], weight_ref[...])
        for t in range(TC):
            found = jnp.zeros((HALF, SLOTS), F32)
            for y in range(YN):
                span = slice(y * YB, (y + 1) * YB)
                block = scores[t * HALF : (t + 1) * HALF, span] - norms[y]
                picked = jnp.take_along_axis(block, index, axis=1, mode="promise_in_bounds")
                found = jnp.where(line == y, picked, found)
            if rc == 0:
                for rz in range(ZN):
                    outs[rz][step * TC + t] = found[rz * PART : (rz + 1) * PART, :]
            else:
                outs[0][:, step * TC + t] = found.reshape(ZN, PART, SLOTS)


def add_kernel(partner_ref, *refs):
    for rz in range(ZN):
        refs[ZN + rz][...] = refs[rz][...] + partner_ref[rz]


def posterior_kernel(own_ref, one_ref, two_ref, three_ref, code_ref, weight_ref, evidence_ref):
    valid = code_ref[...] >= OD
    scores = own_ref[...] + one_ref[...] + two_ref[...] + three_ref[...]
    masked = jnp.where(valid[None], scores, -1e30)
    highest = jnp.max(jnp.max(masked, axis=0), axis=1, keepdims=True)
    terms = jnp.where(valid[None], jnp.exp(scores - highest[None]), 0.0)
    summed = jnp.sum(jnp.sum(terms, axis=0), axis=1, keepdims=True)
    evidence = highest + jnp.log(summed)
    weights = jnp.where(valid[None], jnp.exp(scores - evidence[None]), 0.0)
    weight_ref[...] = weights.astype(BF)
    evidence_ref[...] = jnp.broadcast_to(evidence, evidence_ref.shape)


def sums_kernel(near_ref, far_ref, *refs):
    imgs = refs[:ZN]
    cos_ref, sin_ref, inv_ref, count_ref = refs[ZN : ZN + 4]
    outs = refs[ZN + 4 : ZN + 4 + XN]
    dense_ref, shift_ref = refs[ZN + 4 + XN :]
    gathered = []
    for rc, slot_ref in enumerate((near_ref, far_ref)):
        particles = slice(rc * HALF, (rc + 1) * HALF)
        for y in range(YN):
            span = slice(y * YB, (y + 1) * YB)
            inverse = inv_ref[particles, span]
            count = count_ref[particles, span]
            total = jnp.zeros((HALF, YB), F32)
            for t in range(NTRANS):
                slot = slot_ref[:, t].reshape(HALF, SLOTS).astype(F32)
                picked = jnp.take_along_axis(slot, inverse, axis=1, mode="promise_in_bounds")
                weight = (picked * count).astype(BF)
                start = (2 * t + rc) * HALF
                dense_ref[start : start + HALF, span] = weight
                total = total + weight.astype(F32)
            gathered.append(total)
    lane = lanes((OD, EXT))
    ones = jnp.ones((HALF, EXT), BF)
    for y in range(YN):
        total = jnp.zeros((YB, EXT), F32)
        for rc in range(2):
            for term in split3(gathered[rc * YN + y]):
                total = total + tn(term, ones)
        for x in range(XN):
            packed = pack2(total[x * OD : (x + 1) * OD, :], lane)
            outs[x][y, :, K2:] = packed.astype(outs[x].dtype)
    for block in range(KS // BLOCK):
        low = slice(block * BLOCK, (block + 1) * BLOCK)
        high = slice(KS + block * BLOCK, KS + (block + 1) * BLOCK)
        real = jnp.concatenate(
            [ref[rc, :, low].astype(F32) for rc in range(2) for ref in imgs], axis=0
        )
        imag = jnp.concatenate(
            [ref[rc, :, high].astype(F32) for rc in range(2) for ref in imgs], axis=0
        )
        for t in range(NTRANS):
            cosine = cos_ref[t : t + 1, low]
            sine = sin_ref[t : t + 1, low]
            rows = slice(2 * t * HALF, 2 * (t + 1) * HALF)
            shift_ref[rows, :BLOCK] = (real * cosine - imag * sine).astype(BF)
            shift_ref[rows, BLOCK:] = (real * sine + imag * cosine).astype(BF)
        sums = tn(dense_ref[...], shift_ref[...])
        for y in range(YN):
            for x in range(XN):
                rows = slice((y * XN + x) * OD, (y * XN + x + 1) * OD)
                outs[x][y, :, low] = sums[rows, :BLOCK].astype(outs[x].dtype)
                outs[x][y, :, high] = sums[rows, BLOCK:].astype(outs[x].dtype)


def merge_kernel(own_ref, one_ref, two_ref, three_ref, *outs):
    lane = lanes((OD, EXT))
    for y in range(YN):
        block = own_ref[y]
        for other in (one_ref, two_ref, three_ref):
            block = block + other[y].astype(F32)
        total = jnp.sum(block[:, K2:], axis=1, keepdims=True)
        outs[y][:, :K2] = block[:, :K2].astype(outs[y].dtype)
        outs[y][:, K2:] = pack2(total, lane).astype(outs[y].dtype)


def final_kernel(own_ref, one_ref, two_ref, three_ref, sum_ref, total_ref):
    block = own_ref[...]
    for other in (one_ref, two_ref, three_ref):
        block = block + other[...].astype(F32)
    sum_ref[:, 0, :] = block[:, :KS]
    sum_ref[:, 1, :] = block[:, KS:K2]
    ones = jnp.ones((8, EXT), BF)
    row = jnp.zeros((8, OD), F32)
    for term in split3(block[:, K2:]):
        row = row + nt(ones, term)
    total_ref[...] = row[0:1]


def shape(dims, dtype):
    return jax.ShapeDtypeStruct(dims, dtype)


def dom_core():
    return [(d, d ^ 1) for d in range(DOM)]


def dom_z(step):
    return [(d, (d + 2 * step) % DOM) for d in range(DOM)]


def orient_x(step):
    return [(y * XN + x, y * XN + (x + step) % XN) for y in range(YN) for x in range(XN)]


def orient_y(step):
    return [(y * XN + x, ((y + step) % YN) * XN + x) for y in range(YN) for x in range(XN)]


ORDER = (2, 1, 3)


def phase_tables(shifts, d):
    coefficient = d * KS + jnp.arange(KS, dtype=jnp.int32)
    row_freq = coefficient // GRID - GRID // 2
    col_freq = coefficient % GRID - GRID // 2
    phase_turns = row_freq[None, :] * shifts[:, 0:1] + col_freq[None, :] * shifts[:, 1:2]
    angles = phase_turns.astype(F32) * (2.0 * math.pi / BOX)
    return jnp.cos(angles), jnp.sin(angles)


def gather_references(scaled):
    blocks = {0: scaled}
    for step in ORDER:
        blocks[(-step) % XN] = lax.ppermute(scaled, "orient", orient_x(step))
    line = jnp.concatenate([blocks[x] for x in range(XN)], axis=0)
    lines = {0: line}
    for step in ORDER:
        lines[(-step) % YN] = lax.ppermute(line, "orient", orient_y(step))
    return [lines[y] for y in range(YN)]


def trade_images(far, near):
    other = lax.ppermute(far, "dom", dom_core())
    both = jnp.stack([near, other], axis=1)
    pieces = {0: both[0]}
    for step in ORDER:
        pieces[(-step) % ZN] = lax.ppermute(both[step], "dom", dom_z(step))
    return [pieces[rz] for rz in range(ZN)]


def cost(flops, moved):
    return pl.CostEstimate(flops=flops, bytes_accessed=moved, transcendentals=0)


def inside(kernel, arguments, out_shape, name, flops=0, scratch=(), mib=16):
    single = not isinstance(out_shape, list)
    return pl.pallas_call(
        kernel,
        in_specs=[INSIDE] * len(arguments),
        out_specs=INSIDE if single else [INSIDE] * len(out_shape),
        out_shape=out_shape,
        scratch_shapes=list(scratch),
        compiler_params=params(mib),
        cost_estimate=cost(flops, 2**20),
        name=name,
    )(*arguments)


def score_half(rc, pieces, lines, cosine, sine):
    part = shape((NTRANS, PART, SLOTS), F32)
    return inside(
        lambda *refs: scores_kernel(rc, *refs),
        [*pieces, *lines, cosine, sine],
        [part] * ZN if rc == 0 else [shape((ZN, NTRANS, PART, SLOTS), F32)],
        "scores",
        flops=2 * NTRANS * HALF * K2 * YN * YB,
        scratch=[
            pltpu.VMEM((YN * YB, K2), BF),
            pltpu.VMEM((NTRANS * HALF, K2), BF),
        ],
    )


def shards(images, references, noise_weight, candidate_ids, candidate_mask, shifts):
    d = lax.axis_index("dom")
    scaled = pl.pallas_call(
        refs_kernel,
        in_specs=[pl.BlockSpec(memory_space=pl.ANY), INSIDE],
        out_specs=INSIDE,
        out_shape=shape((OD, KE), BF),
        scratch_shapes=[pltpu.VMEM((OD, 2, KS), BF), pltpu.SemaphoreType.DMA],
        compiler_params=params(4),
        name="scale",
    )(references, noise_weight.reshape(1, K))
    lines = gather_references(scaled)

    far, near, code = pl.pallas_call(
        images_kernel,
        out_specs=[INSIDE] * 3,
        out_shape=[shape((ZN, PART, KE), BF)] * 2 + [shape((PART, SLOTS), jnp.int32)],
        compiler_params=params(8),
        name="cut_images",
    )(images, jnp.swapaxes(candidate_ids, 1, 2), jnp.swapaxes(candidate_mask, 1, 2))
    pieces = trade_images(far, near)
    cosine, sine = phase_tables(shifts, d)
    inverse, counts = inside(
        slots_kernel,
        pieces,
        [shape((2 * HALF, YN * YB), jnp.int32), shape((2 * HALF, YN * YB), F32)],
        "slot_map",
    )
    cosine, sine, inverse, counts = lax.optimization_barrier((cosine, sine, inverse, counts))

    (far_slots,) = score_half(1, pieces, lines, cosine, sine)
    partner = lax.ppermute(far_slots, "dom", dom_core())
    near_slots = score_half(0, pieces, lines, cosine, sine)
    part = shape((NTRANS, PART, SLOTS), F32)
    slots = inside(add_kernel, [partner, *near_slots], [part] * ZN, "add_cores")
    arrived = [lax.ppermute(slots[step], "dom", dom_z(step)) for step in ORDER]
    weights, evidence = inside(
        posterior_kernel,
        [slots[0], *arrived, code],
        [shape((NTRANS, PART, SLOTS), BF), shape((PART, SLOTS), F32)],
        "posterior",
    )

    mine = {0: weights}
    for step in ORDER:
        mine[(-step) % ZN] = lax.ppermute(weights, "dom", dom_z(step))
    near_weights = jnp.stack([mine[rz] for rz in range(ZN)], axis=0)
    far_weights = lax.ppermute(near_weights, "dom", dom_core())

    outs = inside(
        sums_kernel,
        [near_weights, far_weights, *pieces, cosine, sine, inverse, counts],
        [shape((YN, OD, KE), F32 if x == 0 else BF) for x in range(XN)],
        "weighted_sums",
        flops=4 * NTRANS * HALF * K2 * YN * YB,
        scratch=[
            pltpu.VMEM((2 * NTRANS * HALF, YN * YB), BF),
            pltpu.VMEM((2 * NTRANS * HALF, 2 * BLOCK), BF),
        ],
        mib=24,
    )
    along_x = [lax.ppermute(outs[step], "orient", orient_x(step)) for step in ORDER]
    rows = inside(
        merge_kernel,
        [outs[0], *along_x],
        [shape((OD, KE), F32 if y == 0 else BF) for y in range(YN)],
        "merge_x",
    )
    along_y = [lax.ppermute(rows[step], "orient", orient_y(step)) for step in ORDER]
    image_sums, totals = inside(
        final_kernel,
        [rows[0], *along_y],
        [shape((OD, 2, KS), F32), shape((1, OD), F32)],
        "merge_y",
    )
    return image_sums, totals.reshape(OD), evidence[:, 0]


def solution(mesh):
    return jax.shard_map(
        shards,
        mesh=mesh,
        in_specs=(
            P(("dom", "orient"), None, None),
            P("orient", None, None),
            P(),
            P(("dom", "orient"), None, None),
            P(("dom", "orient"), None, None),
            P(),
        ),
        out_specs=(P("orient", None, "dom"), P("orient"), P(("dom", "orient"))),
        check_vma=False,
    )
```

```python
import math

import jax
import jax.numpy as jnp
from jax import lax
from jax.experimental import pallas as pl
from jax.experimental.pallas import tpu as pltpu
from jax.sharding import PartitionSpec as P

GRID = 64
K = 4096
BOX = 400
NTRANS = 25
CAP = 8
ZN = 4
YN = 4
XN = 4
DOM = 8
PART = 16
KS = K // DOM
K2 = 2 * KS
EXT = 128
KE = K2 + EXT
SLOTS = 128
OD = 32
YB = XN * OD
TC = 5
STEPS = NTRANS // TC
HALF = ZN * PART
ROWS = TC * HALF
BF = jnp.bfloat16
F32 = jnp.float32
BLOCK = 256
OWNERS = YN * XN
INSIDE = pl.BlockSpec(memory_space=pltpu.VMEM)


def nt(left, right):
    return lax.dot_general(
        left, right, (((1,), (1,)), ((), ())), preferred_element_type=F32
    )


def tn(left, right):
    return lax.dot_general(
        left, right, (((0,), (0,)), ((), ())), preferred_element_type=F32
    )


def params(mib=16):
    return pltpu.CompilerParams(vmem_limit_bytes=mib * 1024 * 1024)


def lanes(shape):
    return lax.broadcasted_iota(jnp.int32, shape, len(shape) - 1)


def split3(value):
    high = value.astype(BF)
    rest = value - high.astype(F32)
    mid = rest.astype(BF)
    low = (rest - mid.astype(F32)).astype(BF)
    return high, mid, low


def pack2(total, lane):
    high = total.astype(BF).astype(F32)
    return jnp.where(lane == 0, high, jnp.where(lane == 1, total - high, 0.0))


def refs_kernel(refs_ref, noise_ref, out_ref, slice_ref, sem):
    d = lax.axis_index("dom")
    span = pl.ds(pl.multiple_of(d * KS, KS), KS)
    copy = pltpu.make_async_copy(refs_ref.at[:, :, span], slice_ref, sem)
    copy.start()
    noise = noise_ref[:, span]
    copy.wait()
    total = jnp.zeros((OD, 1), F32)
    for part in range(2):
        values = slice_ref[:, part, :].astype(F32)
        out_ref[:, part * KS : (part + 1) * KS] = (values * noise).astype(BF)
        total = total + jnp.sum(noise * values * values, axis=1, keepdims=True)
    high, mid, low = split3(0.5 * total)
    lane = lanes((OD, EXT))
    packed = jnp.where(
        lane == 0,
        high.astype(F32),
        jnp.where(lane == 1, mid.astype(F32), jnp.where(lane == 2, low.astype(F32), 0.0)),
    )
    out_ref[:, K2:] = packed.astype(BF)


def images_kernel(images_ref, ids_ref, mask_ref, far_ref, near_ref, code_ref):
    d = lax.axis_index("dom")
    z = d // 2
    core = lax.rem(d, 2)
    marked = jnp.where(mask_ref[...] > 0, ids_ref[...] + OD, ids_ref[...])
    flat = jnp.concatenate([marked[:, c, :] for c in range(CAP)], axis=1)
    code_ref[...] = flat
    code = flat.astype(F32).astype(BF)
    for rc, out_ref in ((0, near_ref), (1, far_ref)):
        for rz in range(ZN):
            zz = lax.rem(z + rz, ZN)
            cc = core if rc == 0 else 1 - core
            span = pl.ds(pl.multiple_of((zz * 2 + cc) * KS, KS), KS)
            for part in range(2):
                out_ref[rz, :, part * KS : (part + 1) * KS] = images_ref[:, part, span]
            out_ref[rz, :, K2:] = code


def slots_kernel(p0_ref, p1_ref, p2_ref, p3_ref, near_inv, near_count, far_inv, far_count):
    lane = lanes((HALF, SLOTS))
    for rc in range(2):
        code = jnp.concatenate(
            [ref[rc, :, K2:].astype(F32) for ref in (p0_ref, p1_ref, p2_ref, p3_ref)], axis=0
        ).astype(jnp.int32)
        inv_ref, count_ref = ((near_inv, near_count), (far_inv, far_count))[rc]
        for block in range(YN):
            inverse = jnp.zeros((HALF, YB), jnp.int32)
            count = jnp.zeros((HALF, YB), F32)
            for c in range(CAP):
                where_slot = c * OWNERS + block * XN + lane // OD
                seen = jnp.take_along_axis(code, where_slot, axis=1, mode="promise_in_bounds")
                match = seen == (lane % OD + OD)
                count = count + jnp.where(match, 1.0, 0.0)
                inverse = jnp.where(match, where_slot, inverse)
            inv_ref[:, block * YB : (block + 1) * YB] = inverse
            count_ref[:, block * YB : (block + 1) * YB] = count


def scores_kernel(rc, *refs):
    imgs = refs[0:ZN]
    refs_in = refs[ZN : ZN + YN]
    cos_ref, sin_ref = refs[ZN + YN : ZN + YN + 2]
    shift_ref = refs[ZN + YN + 2]
    outs = refs[ZN + YN + 3 : -1]
    weight_ref = refs[-1]
    core = lax.rem(lax.axis_index("dom"), 2)
    j = lax.axis_index("orient")
    lane8 = lanes((8, EXT))
    ones = jnp.where(lane8 < 3, 1.0, 0.0).astype(BF)
    norms = []
    for y in range(YN):
        weight_ref[y * YB : (y + 1) * YB, :] = refs_in[y][:, :K2]
        norms.append(nt(ones, refs_in[y][:, K2:])[0:1])
    lane = lanes((HALF, SLOTS))
    code = jnp.concatenate([ref[rc, :, K2:].astype(F32) for ref in imgs], axis=0).astype(jnp.int32)
    owner = lane % OWNERS
    along_y = (owner // XN + YN - j // XN) % YN
    along_x = (owner % XN + XN - lax.rem(j, XN)) % XN
    line = jnp.where(core == 0, along_y, along_x)
    index = jnp.where(core == 0, along_x, along_y) * OD + code % OD
    value = jnp.concatenate([ref[rc, :, :K2].astype(F32) for ref in imgs], axis=0)
    real = value[:, :KS]
    imag = value[:, KS:]
    for step in range(STEPS):
        base = step * ROWS
        for t in range(TC):
            row = step * TC + t
            cosine = cos_ref[row : row + 1, :]
            sine = sin_ref[row : row + 1, :]
            rows = slice(base + t * HALF, base + (t + 1) * HALF)
            shift_ref[rows, :KS] = (real * cosine - imag * sine).astype(BF)
            shift_ref[rows, KS:] = (real * sine + imag * cosine).astype(BF)
        scores = nt(shift_ref[base : base + ROWS, :], weight_ref[...])
        for t in range(TC):
            found = jnp.zeros((HALF, SLOTS), F32)
            for y in range(YN):
                span = slice(y * YB, (y + 1) * YB)
                block = scores[t * HALF : (t + 1) * HALF, span] - norms[y]
                picked = jnp.take_along_axis(block, index, axis=1, mode="promise_in_bounds")
                found = jnp.where(line == y, picked, found)
            if rc == 0:
                for rz in range(ZN):
                    outs[rz][step * TC + t] = found[rz * PART : (rz + 1) * PART, :]
            else:
                outs[0][:, step * TC + t] = found.reshape(ZN, PART, SLOTS)


def add_kernel(partner_ref, *refs):
    for rz in range(ZN):
        refs[ZN + rz][...] = refs[rz][...] + partner_ref[rz]


def posterior_kernel(own_ref, one_ref, two_ref, three_ref, code_ref, weight_ref, evidence_ref):
    valid = code_ref[...] >= OD
    scores = own_ref[...] + one_ref[...] + two_ref[...] + three_ref[...]
    masked = jnp.where(valid[None], scores, -1e30)
    highest = jnp.max(jnp.max(masked, axis=0), axis=1, keepdims=True)
    terms = jnp.where(valid[None], jnp.exp(scores - highest[None]), 0.0)
    summed = jnp.sum(jnp.sum(terms, axis=0), axis=1, keepdims=True)
    evidence = highest + jnp.log(summed)
    weights = jnp.where(valid[None], jnp.exp(scores - evidence[None]), 0.0)
    weight_ref[...] = weights.astype(BF)
    evidence_ref[...] = jnp.broadcast_to(evidence, evidence_ref.shape)


def dense_rows(slots, inv_ref, count_ref, dense_ref):
    column = []
    ones = jnp.ones((HALF, EXT), BF)
    for y in range(YN):
        span = slice(y * YB, (y + 1) * YB)
        inverse = inv_ref[:, span]
        count = count_ref[:, span]
        total = jnp.zeros((HALF, YB), F32)
        for t in range(NTRANS):
            picked = jnp.take_along_axis(slots[t], inverse, axis=1, mode="promise_in_bounds")
            weight = (picked * count).astype(BF)
            dense_ref[t * HALF : (t + 1) * HALF, span] = weight
            total = total + weight.astype(F32)
        summed = jnp.zeros((YB, EXT), F32)
        for term in split3(total):
            summed = summed + tn(term, ones)
        column.append(summed)
    return column


def near_kernel(s0_ref, s1_ref, s2_ref, s3_ref, shift_ref, inv_ref, count_ref, acc_ref, dense_ref):
    parts = (s0_ref, s1_ref, s2_ref, s3_ref)
    slots = [
        jnp.concatenate([ref[t].astype(F32) for ref in parts], axis=0) for t in range(NTRANS)
    ]
    column = dense_rows(slots, inv_ref, count_ref, dense_ref)
    for y in range(YN):
        acc_ref[y * YB : (y + 1) * YB, K2:] = column[y]
    for block in range(K2 // BLOCK):
        span = slice(block * BLOCK, (block + 1) * BLOCK)
        acc_ref[:, span] = tn(dense_ref[...], shift_ref[:, span])


def far_kernel(slot_ref, shift_ref, inv_ref, count_ref, acc_ref, out_ref, dense_ref):
    slots = [slot_ref[:, t].reshape(HALF, SLOTS).astype(F32) for t in range(NTRANS)]
    column = dense_rows(slots, inv_ref, count_ref, dense_ref)
    lane = lanes((YB, EXT))
    for y in range(YN):
        total = acc_ref[y * YB : (y + 1) * YB, K2:] + column[y]
        packed = pack2(total, lane).astype(BF)
        out_ref[y * XN : (y + 1) * XN, :, K2:] = packed.reshape(XN, OD, EXT)
    for block in range(K2 // BLOCK):
        span = slice(block * BLOCK, (block + 1) * BLOCK)
        sums = acc_ref[:, span] + tn(dense_ref[...], shift_ref[:, span])
        out_ref[:, :, span] = sums.astype(BF).reshape(OWNERS, OD, BLOCK)


def final_kernel(parts_ref, sum_ref, total_ref):
    block = parts_ref[0].astype(F32)
    for source in range(1, OWNERS):
        block = block + parts_ref[source].astype(F32)
    sum_ref[:, 0, :] = block[:, :KS]
    sum_ref[:, 1, :] = block[:, KS:K2]
    ones = jnp.ones((8, EXT), BF)
    row = jnp.zeros((8, OD), F32)
    for term in split3(block[:, K2:]):
        row = row + nt(ones, term)
    total_ref[...] = row[0:1]


def shape(dims, dtype):
    return jax.ShapeDtypeStruct(dims, dtype)


def dom_core():
    return [(d, d ^ 1) for d in range(DOM)]


def dom_z(step):
    return [(d, (d + 2 * step) % DOM) for d in range(DOM)]


def mixed(step, first):
    pairs = []
    for d in range(DOM):
        for y in range(YN):
            for x in range(XN):
                if (d % 2 == 0) == first:
                    target = y * XN + (x + step) % XN
                else:
                    target = ((y + step) % YN) * XN + x
                pairs.append((d * OWNERS + y * XN + x, d * OWNERS + target))
    return pairs


ORDER = (2, 1, 3)


def phase_tables(shifts, d):
    coefficient = d * KS + jnp.arange(KS, dtype=jnp.int32)
    row_freq = coefficient // GRID - GRID // 2
    col_freq = coefficient % GRID - GRID // 2
    phase_turns = row_freq[None, :] * shifts[:, 0:1] + col_freq[None, :] * shifts[:, 1:2]
    angles = phase_turns.astype(F32) * (2.0 * math.pi / BOX)
    return jnp.cos(angles), jnp.sin(angles)


def gather_references(scaled):
    blocks = {0: scaled}
    for step in ORDER:
        blocks[(-step) % XN] = lax.ppermute(scaled, ("dom", "orient"), mixed(step, True))
    line = jnp.concatenate([blocks[x] for x in range(XN)], axis=0)
    lines = {0: line}
    for step in ORDER:
        lines[(-step) % YN] = lax.ppermute(line, ("dom", "orient"), mixed(step, False))
    return [lines[y] for y in range(YN)]


def trade_images(far, near):
    other = lax.ppermute(far, "dom", dom_core())
    both = jnp.stack([near, other], axis=1)
    pieces = {0: both[0]}
    for step in ORDER:
        pieces[(-step) % ZN] = lax.ppermute(both[step], "dom", dom_z(step))
    return [pieces[rz] for rz in range(ZN)]


def cost(flops, moved):
    return pl.CostEstimate(flops=flops, bytes_accessed=moved, transcendentals=0)


def inside(kernel, arguments, out_shape, name, flops=0, scratch=(), mib=16):
    single = not isinstance(out_shape, list)
    return pl.pallas_call(
        kernel,
        in_specs=[INSIDE] * len(arguments),
        out_specs=INSIDE if single else [INSIDE] * len(out_shape),
        out_shape=out_shape,
        scratch_shapes=list(scratch),
        compiler_params=params(mib),
        cost_estimate=cost(flops, 2**20),
        name=name,
    )(*arguments)


def score_half(rc, pieces, lines, cosine, sine):
    part = shape((NTRANS, PART, SLOTS), F32)
    return inside(
        lambda *refs: scores_kernel(rc, *refs),
        [*pieces, *lines, cosine, sine],
        [shape((NTRANS * HALF, K2), BF)]
        + ([part] * ZN if rc == 0 else [shape((ZN, NTRANS, PART, SLOTS), F32)]),
        "scores",
        flops=2 * NTRANS * HALF * K2 * YN * YB,
        scratch=[pltpu.VMEM((YN * YB, K2), BF)],
    )


def shards(images, references, noise_weight, candidate_ids, candidate_mask, shifts):
    d = lax.axis_index("dom")
    scaled = pl.pallas_call(
        refs_kernel,
        in_specs=[pl.BlockSpec(memory_space=pl.ANY), INSIDE],
        out_specs=INSIDE,
        out_shape=shape((OD, KE), BF),
        scratch_shapes=[pltpu.VMEM((OD, 2, KS), BF), pltpu.SemaphoreType.DMA],
        compiler_params=params(4),
        name="scale",
    )(references, noise_weight.reshape(1, K))
    lines = gather_references(scaled)

    far, near, code = pl.pallas_call(
        images_kernel,
        out_specs=[INSIDE] * 3,
        out_shape=[shape((ZN, PART, KE), BF)] * 2 + [shape((PART, SLOTS), jnp.int32)],
        compiler_params=params(8),
        name="cut_images",
    )(images, jnp.swapaxes(candidate_ids, 1, 2), jnp.swapaxes(candidate_mask, 1, 2))
    pieces = trade_images(far, near)
    cosine, sine = phase_tables(shifts, d)
    near_inv, near_count, far_inv, far_count = inside(
        slots_kernel,
        pieces,
        [shape((HALF, YN * YB), jnp.int32), shape((HALF, YN * YB), F32)] * 2,
        "slot_map",
    )
    cosine, near_inv, near_count, far_inv, far_count = lax.optimization_barrier(
        (cosine, near_inv, near_count, far_inv, far_count)
    )

    far_shift, far_slots = score_half(1, pieces, lines, cosine, sine)
    partner = lax.ppermute(far_slots, "dom", dom_core())
    near_shift, *near_slots = score_half(0, pieces, lines, cosine, sine)
    part = shape((NTRANS, PART, SLOTS), F32)
    slots = inside(add_kernel, [partner, *near_slots], [part] * ZN, "add_cores")
    arrived = [lax.ppermute(slots[step], "dom", dom_z(step)) for step in ORDER]
    weights, evidence = inside(
        posterior_kernel,
        [slots[0], *arrived, code],
        [shape((NTRANS, PART, SLOTS), BF), shape((PART, SLOTS), F32)],
        "posterior",
    )

    mine = {0: weights}
    for step in ORDER:
        mine[(-step) % ZN] = lax.ppermute(weights, "dom", dom_z(step))
    near_weights = [mine[rz] for rz in range(ZN)]
    far_weights = lax.ppermute(jnp.stack(near_weights, axis=0), "dom", dom_core())
    dense = pltpu.VMEM((NTRANS * HALF, YN * YB), BF)
    flops = 2 * NTRANS * HALF * K2 * YN * YB
    acc = inside(
        near_kernel,
        [*near_weights, near_shift, near_inv, near_count],
        shape((YN * YB, KE), F32),
        "near_sums",
        flops=flops,
        scratch=[dense],
    )
    sums = inside(
        far_kernel,
        [far_weights, far_shift, far_inv, far_count, acc],
        shape((OWNERS, OD, KE), BF),
        "far_sums",
        flops=flops,
        scratch=[dense],
    )
    parts = lax.all_to_all(sums, "orient", 0, 0, tiled=True)
    image_sums, totals = inside(
        final_kernel,
        [parts],
        [shape((OD, 2, KS), F32), shape((1, OD), F32)],
        "merge",
    )
    return image_sums, totals.reshape(OD), evidence[:, 0]


def solution(mesh):
    return jax.shard_map(
        shards,
        mesh=mesh,
        in_specs=(
            P(("dom", "orient"), None, None),
            P("orient", None, None),
            P(),
            P(("dom", "orient"), None, None),
            P(("dom", "orient"), None, None),
            P(),
        ),
        out_specs=(P("orient", None, "dom"), P("orient"), P(("dom", "orient"))),
        check_vma=False,
    )
```

```python
import math

import jax
import jax.numpy as jnp
from jax import lax
from jax.experimental import pallas as pl
from jax.experimental.pallas import tpu as pltpu
from jax.sharding import PartitionSpec as P

GRID = 64
K = 4096
BOX = 400
NTRANS = 25
CAP = 8
ZN = 4
YN = 4
XN = 4
DOM = 8
PART = 16
KS = K // DOM
K2 = 2 * KS
EXT = 128
KE = K2 + EXT
SLOTS = 128
OD = 32
YB = XN * OD
TC = 5
STEPS = NTRANS // TC
HALF = ZN * PART
ROWS = TC * HALF
BF = jnp.bfloat16
F32 = jnp.float32
BLOCK = 256
OWNERS = YN * XN
INSIDE = pl.BlockSpec(memory_space=pltpu.VMEM)


def nt(left, right):
    return lax.dot_general(
        left, right, (((1,), (1,)), ((), ())), preferred_element_type=F32
    )


def tn(left, right):
    return lax.dot_general(
        left, right, (((0,), (0,)), ((), ())), preferred_element_type=F32
    )


def params(mib=16):
    return pltpu.CompilerParams(vmem_limit_bytes=mib * 1024 * 1024)


def lanes(shape):
    return lax.broadcasted_iota(jnp.int32, shape, len(shape) - 1)


def split3(value):
    high = value.astype(BF)
    rest = value - high.astype(F32)
    mid = rest.astype(BF)
    low = (rest - mid.astype(F32)).astype(BF)
    return high, mid, low


def pack2(total, lane):
    high = total.astype(BF).astype(F32)
    return jnp.where(lane == 0, high, jnp.where(lane == 1, total - high, 0.0))


def prepare_kernel(
    refs_hbm, images_hbm, noise_hbm, ids_hbm, mask_hbm,
    out0, out1, out2, out3, code_ref,
    refs_ref, images_ref, noise_ref, ids_ref, mask_ref, sems,
):
    d = lax.axis_index("dom")
    z = d // 2
    core = lax.rem(d, 2)

    def span(step, rc):
        slot = lax.rem(z + step, ZN) * 2 + (core if rc == 0 else 1 - core)
        return pl.ds(pl.multiple_of(slot * KS, KS), KS)

    copies = [
        pltpu.make_async_copy(noise_hbm, noise_ref, sems.at[0]),
        pltpu.make_async_copy(ids_hbm, ids_ref, sems.at[1]),
        pltpu.make_async_copy(mask_hbm, mask_ref, sems.at[2]),
        pltpu.make_async_copy(images_hbm, images_ref, sems.at[3]),
    ] + [
        pltpu.make_async_copy(refs_hbm.at[:, :, span(step, 0)], refs_ref.at[step], sems.at[4 + step])
        for step in range(ZN)
    ]
    for copy in copies:
        copy.start()
    for copy in copies:
        copy.wait()
    marked = jnp.where(mask_ref[...] > 0, ids_ref[...] + OD, ids_ref[...])
    flat = jnp.concatenate([marked[:, c, :] for c in range(CAP)], axis=1)
    code_ref[...] = flat
    code = flat.astype(F32).astype(BF)
    lane = lanes((OD, EXT))
    for step, out_ref in enumerate((out0, out1, out2, out3)):
        noise = noise_ref[:, span(step, 0)]
        total = jnp.zeros((OD, 1), F32)
        for part in range(2):
            columns = slice(part * KS, (part + 1) * KS)
            values = refs_ref[step, :, part, :].astype(F32)
            out_ref[:OD, columns] = (values * noise).astype(BF)
            total = total + jnp.sum(noise * values * values, axis=1, keepdims=True)
            for rc in range(2):
                rows = slice(OD + rc * PART, OD + (rc + 1) * PART)
                out_ref[rows, columns] = images_ref[:, part, span(step, rc)]
        high, mid, low = [term.astype(F32) for term in split3(0.5 * total)]
        norms = jnp.where(lane == 0, high, jnp.where(lane == 1, mid, jnp.where(lane == 2, low, 0.0)))
        out_ref[:OD, K2:] = norms.astype(BF)
        for rc in range(2):
            out_ref[OD + rc * PART : OD + (rc + 1) * PART, K2:] = code


def gather_kernel(b0_ref, b1_ref, b2_ref, b3_ref, line_ref, far_ref):
    for place, ref in enumerate((b0_ref, b1_ref, b2_ref, b3_ref)):
        line_ref[place * OD : (place + 1) * OD, :] = ref[:OD, :]
        far_ref[place] = ref[OD + PART :, :]


def stack_kernel(s0_ref, s1_ref, s2_ref, s3_ref, out_ref):
    for place, ref in enumerate((s0_ref, s1_ref, s2_ref, s3_ref)):
        out_ref[place] = ref[...]


def first_axis(core, along_x, along_y):
    return jnp.where(core == 0, along_x, along_y)


def slots_kernel(
    shifts_ref, b0_ref, b1_ref, b2_ref, b3_ref, far_ref,
    near_inv, near_count, far_inv, far_count, cos_ref, sin_ref,
):
    d = lax.axis_index("dom")
    core = lax.rem(d, 2)
    j = lax.axis_index("orient")
    coefficient = d * KS + lanes((1, KS))
    row_freq = coefficient // GRID - GRID // 2
    col_freq = coefficient % GRID - GRID // 2
    turns = jnp.concatenate(
        [row_freq * shifts_ref[0, t] + col_freq * shifts_ref[1, t] for t in range(NTRANS)], axis=0
    )
    angles = turns.astype(F32) * (2.0 * math.pi / BOX)
    cos_ref[...] = jnp.cos(angles)
    sin_ref[...] = jnp.sin(angles)
    lane = lanes((HALF, SLOTS))
    near = [ref[OD : OD + PART, K2:] for ref in (b0_ref, b1_ref, b2_ref, b3_ref)]
    far = [far_ref[rz, :, K2:] for rz in range(ZN)]
    outs = ((near, near_inv, near_count), (far, far_inv, far_count))
    for parts, inv_ref, count_ref in outs:
        code = jnp.concatenate([part.astype(F32) for part in parts], axis=0).astype(jnp.int32)
        for block in range(XN):
            along_x = first_axis(core, block, lane // OD)
            along_y = first_axis(core, lane // OD, block)
            owner = ((j // XN + along_y) % YN) * XN + (lax.rem(j, XN) + along_x) % XN
            inverse = jnp.zeros((HALF, YB), jnp.int32)
            count = jnp.zeros((HALF, YB), F32)
            for c in range(CAP):
                where_slot = c * OWNERS + owner
                seen = jnp.take_along_axis(code, where_slot, axis=1, mode="promise_in_bounds")
                match = seen == (lane % OD + OD)
                count = count + jnp.where(match, 1.0, 0.0)
                inverse = jnp.where(match, where_slot, inverse)
            inv_ref[:, block * YB : (block + 1) * YB] = inverse
            count_ref[:, block * YB : (block + 1) * YB] = count


def scores_kernel(rc, *refs):
    if rc == 0:
        images = [ref[OD : OD + PART, :] for ref in refs[:ZN]]
        refs = refs[ZN:]
    else:
        images = [refs[0][rz] for rz in range(ZN)]
        refs = refs[1:]
    refs_in = refs[:YN]
    cos_ref, sin_ref, shift_ref = refs[YN : YN + 3]
    outs = refs[YN + 3 : -1]
    weight_ref = refs[-1]
    core = lax.rem(lax.axis_index("dom"), 2)
    j = lax.axis_index("orient")
    lane8 = lanes((8, EXT))
    ones = jnp.where(lane8 < 3, 1.0, 0.0).astype(BF)
    norms = []
    for y in range(YN):
        weight_ref[y * YB : (y + 1) * YB, :] = refs_in[y][:, :K2]
        norms.append(nt(ones, refs_in[y][:, K2:])[0:1])
    lane = lanes((HALF, SLOTS))
    values = jnp.concatenate([part.astype(F32) for part in images], axis=0)
    code = values[:, K2:].astype(jnp.int32)
    owner = lane % OWNERS
    along_y = (owner // XN + YN - j // XN) % YN
    along_x = (owner % XN + XN - lax.rem(j, XN)) % XN
    line = first_axis(core, along_y, along_x)
    index = first_axis(core, along_x, along_y) * OD + code % OD
    real = values[:, :KS]
    imag = values[:, KS:K2]
    for step in range(STEPS):
        base = step * ROWS
        for t in range(TC):
            row = step * TC + t
            cosine = cos_ref[row : row + 1, :]
            sine = sin_ref[row : row + 1, :]
            rows = slice(base + t * HALF, base + (t + 1) * HALF)
            shift_ref[rows, :KS] = (real * cosine - imag * sine).astype(BF)
            shift_ref[rows, KS:] = (real * sine + imag * cosine).astype(BF)
        scores = nt(shift_ref[base : base + ROWS, :], weight_ref[...])
        for t in range(TC):
            found = jnp.zeros((HALF, SLOTS), F32)
            for y in range(YN):
                span = slice(y * YB, (y + 1) * YB)
                block = scores[t * HALF : (t + 1) * HALF, span] - norms[y]
                picked = jnp.take_along_axis(block, index, axis=1, mode="promise_in_bounds")
                found = jnp.where(line == y, picked, found)
            if rc == 0:
                for rz in range(ZN):
                    outs[rz][step * TC + t] = found[rz * PART : (rz + 1) * PART, :]
            else:
                outs[0][:, step * TC + t] = found.reshape(ZN, PART, SLOTS)


def add_kernel(partner_ref, *refs):
    for rz in range(ZN):
        refs[ZN + rz][...] = refs[rz][...] + partner_ref[rz]


def posterior_kernel(own_ref, one_ref, two_ref, three_ref, code_ref, weight_ref, evidence_ref):
    valid = code_ref[...] >= OD
    scores = own_ref[...] + one_ref[...] + two_ref[...] + three_ref[...]
    masked = jnp.where(valid[None], scores, -1e30)
    highest = jnp.max(jnp.max(masked, axis=0), axis=1, keepdims=True)
    terms = jnp.where(valid[None], jnp.exp(scores - highest[None]), 0.0)
    summed = jnp.sum(jnp.sum(terms, axis=0), axis=1, keepdims=True)
    evidence = highest + jnp.log(summed)
    weights = jnp.where(valid[None], jnp.exp(scores - evidence[None]), 0.0)
    weight_ref[...] = weights.astype(BF)
    evidence_ref[...] = jnp.broadcast_to(evidence, evidence_ref.shape)


def dense_rows(blocks, slots, inv_ref, count_ref, dense_ref):
    column = []
    ones = jnp.ones((HALF, EXT), BF)
    for place, block in enumerate(blocks):
        span = slice(block * YB, (block + 1) * YB)
        inverse = inv_ref[:, span]
        count = count_ref[:, span]
        total = jnp.zeros((HALF, YB), F32)
        for t in range(NTRANS):
            picked = jnp.take_along_axis(slots[t], inverse, axis=1, mode="promise_in_bounds")
            weight = (picked * count).astype(BF)
            dense_ref[t * HALF : (t + 1) * HALF, place * YB : (place + 1) * YB] = weight
            total = total + weight.astype(F32)
        summed = jnp.zeros((YB, EXT), F32)
        for term in split3(total):
            summed = summed + tn(term, ones)
        column.append(summed)
    return column


def near_kernel(s0_ref, s1_ref, s2_ref, s3_ref, shift_ref, inv_ref, count_ref, acc_ref, dense_ref):
    parts = (s0_ref, s1_ref, s2_ref, s3_ref)
    slots = [
        jnp.concatenate([ref[t].astype(F32) for ref in parts], axis=0) for t in range(NTRANS)
    ]
    column = dense_rows(range(XN), slots, inv_ref, count_ref, dense_ref)
    for block in range(XN):
        acc_ref[block * YB : (block + 1) * YB, K2:] = column[block]
    for block in range(K2 // BLOCK):
        span = slice(block * BLOCK, (block + 1) * BLOCK)
        acc_ref[:, span] = tn(dense_ref[...], shift_ref[:, span])


def far_kernel(blocks, slot_ref, shift_ref, inv_ref, count_ref, acc_ref, *refs):
    outs = refs[:-1]
    dense_ref = refs[-1]
    slots = [slot_ref[:, t].reshape(HALF, SLOTS).astype(F32) for t in range(NTRANS)]
    column = dense_rows(blocks, slots, inv_ref, count_ref, dense_ref)
    lane = lanes((YB, EXT))
    for place, block in enumerate(blocks):
        total = acc_ref[block * YB : (block + 1) * YB, K2:] + column[place]
        outs[place][:, K2:] = pack2(total, lane).astype(outs[place].dtype)
    for part in range(K2 // BLOCK):
        span = slice(part * BLOCK, (part + 1) * BLOCK)
        sums = tn(dense_ref[...], shift_ref[:, span])
        for place, block in enumerate(blocks):
            done = acc_ref[block * YB : (block + 1) * YB, span]
            done = done + sums[place * YB : (place + 1) * YB, :]
            outs[place][:, span] = done.astype(outs[place].dtype)


def merge_kernel(own_ref, one_ref, two_ref, three_ref, *outs):
    lane = lanes((OD, EXT))
    for b in range(YN):
        rows = slice(b * OD, (b + 1) * OD)
        block = own_ref[rows, :]
        for other in (one_ref, two_ref, three_ref):
            block = block + other[rows, :].astype(F32)
        total = jnp.sum(block[:, K2:], axis=1, keepdims=True)
        outs[b][:, :K2] = block[:, :K2].astype(outs[b].dtype)
        outs[b][:, K2:] = pack2(total, lane).astype(outs[b].dtype)


def final_kernel(own_ref, one_ref, two_ref, three_ref, sum_ref, total_ref):
    block = own_ref[...]
    for other in (one_ref, two_ref, three_ref):
        block = block + other[...].astype(F32)
    sum_ref[:, 0, :] = block[:, :KS]
    sum_ref[:, 1, :] = block[:, KS:K2]
    ones = jnp.ones((8, EXT), BF)
    row = jnp.zeros((8, OD), F32)
    for term in split3(block[:, K2:]):
        row = row + nt(ones, term)
    total_ref[...] = row[0:1]


def shape(dims, dtype):
    return jax.ShapeDtypeStruct(dims, dtype)


def dom_core():
    return [(d, d ^ 1) for d in range(DOM)]


def turn(step, first, along_z):
    pairs = []
    for d in range(DOM):
        for y in range(YN):
            for x in range(XN):
                target = (d + 2 * step) % DOM if along_z else d
                if (d % 2 == 0) == first:
                    owner = y * XN + (x + step) % XN
                else:
                    owner = ((y + step) % YN) * XN + x
                pairs.append((d * OWNERS + y * XN + x, target * OWNERS + owner))
    return pairs


ORDER = (2, 1, 3)
BOTH = ("dom", "orient")


def diagonal(value, step):
    return lax.ppermute(value, BOTH, turn(step, True, True))


def along_first(value, step):
    return lax.ppermute(value, BOTH, turn(step, True, False))


def along_second(value, step):
    return lax.ppermute(value, BOTH, turn(step, False, False))


def cost(flops, moved):
    return pl.CostEstimate(flops=flops, bytes_accessed=moved, transcendentals=0)


def inside(kernel, arguments, out_shape, name, flops=0, scratch=(), mib=16):
    single = not isinstance(out_shape, list)
    return pl.pallas_call(
        kernel,
        in_specs=[INSIDE] * len(arguments),
        out_specs=INSIDE if single else [INSIDE] * len(out_shape),
        out_shape=out_shape,
        scratch_shapes=list(scratch),
        compiler_params=params(mib),
        cost_estimate=cost(flops, 2**20),
        name=name,
    )(*arguments)


def score_half(rc, images, lines, cosine, sine):
    part = shape((NTRANS, PART, SLOTS), F32)
    return inside(
        lambda *refs: scores_kernel(rc, *refs),
        [*images, *lines, cosine, sine],
        [shape((NTRANS * HALF, K2), BF)]
        + ([part] * ZN if rc == 0 else [shape((ZN, NTRANS, PART, SLOTS), F32)]),
        "scores",
        flops=2 * NTRANS * HALF * K2 * YN * YB,
        scratch=[pltpu.VMEM((YN * YB, K2), BF)],
    )


def prepare(images, references, noise_weight, candidate_ids, candidate_mask):
    return pl.pallas_call(
        prepare_kernel,
        in_specs=[pl.BlockSpec(memory_space=pltpu.HBM)] * 5,
        out_specs=[INSIDE] * 5,
        out_shape=[shape((OD + 2 * PART, KE), BF)] * ZN
        + [shape((PART, SLOTS), jnp.int32)],
        scratch_shapes=[
            pltpu.VMEM((ZN, OD, 2, KS), BF),
            pltpu.VMEM((PART, 2, K), BF),
            pltpu.VMEM((1, K), F32),
            pltpu.VMEM((PART, CAP, OWNERS), jnp.int32),
            pltpu.VMEM((PART, CAP, OWNERS), jnp.int32),
            pltpu.SemaphoreType.DMA((8,)),
        ],
        compiler_params=params(56),
        name="prepare",
    )(
        references,
        images,
        noise_weight.reshape(1, K),
        jnp.swapaxes(candidate_ids, 1, 2),
        jnp.swapaxes(candidate_mask, 1, 2),
    )


def shards(images, references, noise_weight, candidate_ids, candidate_mask, shifts):
    *payload, code = prepare(images, references, noise_weight, candidate_ids, candidate_mask)
    blocks = {0: payload[0]}
    for step in ORDER:
        blocks[(-step) % ZN] = diagonal(payload[step], step)
    blocks = [blocks[rz] for rz in range(ZN)]
    line, far = inside(
        gather_kernel, blocks, [shape((YB, KE), BF), shape((ZN, PART, KE), BF)], "gather"
    )
    lines = {0: line}
    for step in ORDER:
        lines[(-step) % YN] = along_second(line, step)
    lines = [lines[y] for y in range(YN)]
    far = lax.ppermute(far, "dom", dom_core())
    tables = pl.pallas_call(
        slots_kernel,
        in_specs=[pl.BlockSpec(memory_space=pltpu.SMEM)] + [INSIDE] * (ZN + 1),
        out_specs=[INSIDE] * 6,
        out_shape=[shape((HALF, YN * YB), jnp.int32), shape((HALF, YN * YB), F32)] * 2
        + [shape((NTRANS, KS), F32)] * 2,
        compiler_params=params(),
        name="slot_map",
    )(shifts.T, *blocks, far)
    near_inv, near_count, far_inv, far_count, cosine, sine = tables

    far_shift, far_slots = score_half(1, [far], lines, cosine, sine)
    partner = lax.ppermute(far_slots, "dom", dom_core())
    near_shift, *near_slots = score_half(0, blocks, lines, cosine, sine)
    part = shape((NTRANS, PART, SLOTS), F32)
    slots = inside(add_kernel, [partner, *near_slots], [part] * ZN, "add_cores")
    arrived = [diagonal(slots[step], step) for step in ORDER]
    weights, evidence = inside(
        posterior_kernel,
        [slots[0], *arrived, code],
        [shape((NTRANS, PART, SLOTS), BF), shape((PART, SLOTS), F32)],
        "posterior",
    )

    mine = {0: weights}
    for step in ORDER:
        mine[(-step) % ZN] = diagonal(weights, step)
    near_weights = [mine[rz] for rz in range(ZN)]
    stacked = inside(
        stack_kernel, near_weights, shape((ZN, NTRANS, PART, SLOTS), BF), "stack_weights"
    )
    far_weights = lax.ppermute(stacked, "dom", dom_core())
    flops = 2 * NTRANS * HALF * K2 * YN * YB
    acc = inside(
        near_kernel,
        [*near_weights, near_shift, near_inv, near_count],
        shape((YN * YB, KE), F32),
        "near_sums",
        flops=flops,
        scratch=[pltpu.VMEM((NTRANS * HALF, YN * YB), BF)],
    )
    outs = {}
    for targets in ((2, 1), (3, 0)):
        pair = inside(
            lambda *refs, targets=targets: far_kernel(targets, *refs),
            [far_weights, far_shift, far_inv, far_count, acc],
            [shape((YB, KE), F32 if target == 0 else BF) for target in targets],
            "far_sums",
            flops=flops // 2,
            scratch=[pltpu.VMEM((NTRANS * HALF, 2 * YB), BF)],
        )
        outs.update(zip(targets, pair))
    rows = inside(
        merge_kernel,
        [outs[0]] + [along_first(outs[step], step) for step in ORDER],
        [shape((OD, KE), F32 if b == 0 else BF) for b in range(YN)],
        "merge_first",
    )
    image_sums, totals = inside(
        final_kernel,
        [rows[0]] + [along_second(rows[step], step) for step in ORDER],
        [shape((OD, 2, KS), F32), shape((1, OD), F32)],
        "merge_second",
    )
    return image_sums, totals.reshape(OD), evidence[:, 0]


def solution(mesh):
    return jax.shard_map(
        shards,
        mesh=mesh,
        in_specs=(
            P(("dom", "orient"), None, None),
            P("orient", None, None),
            P(),
            P(("dom", "orient"), None, None),
            P(("dom", "orient"), None, None),
            P(),
        ),
        out_specs=(P("orient", None, "dom"), P("orient"), P(("dom", "orient"))),
        check_vma=False,
    )
```

```python
import math

import jax
import jax.numpy as jnp
from jax import lax
from jax.experimental import pallas as pl
from jax.experimental.pallas import tpu as pltpu
from jax.sharding import PartitionSpec as P

GRID = 64
K = 4096
BOX = 400
NTRANS = 25
CAP = 8
ZN = 4
YN = 4
XN = 4
DOM = 8
PART = 16
KS = K // DOM
K2 = 2 * KS
EXT = 128
KE = K2 + EXT
SLOTS = 128
OD = 32
YB = XN * OD
TC = 5
STEPS = NTRANS // TC
HALF = ZN * PART
ROWS = TC * HALF
BF = jnp.bfloat16
F32 = jnp.float32
BLOCK = 256
OWNERS = YN * XN
INSIDE = pl.BlockSpec(memory_space=pltpu.VMEM)


def nt(left, right):
    return lax.dot_general(
        left, right, (((1,), (1,)), ((), ())), preferred_element_type=F32
    )


def tn(left, right):
    return lax.dot_general(
        left, right, (((0,), (0,)), ((), ())), preferred_element_type=F32
    )


def params(mib=16):
    return pltpu.CompilerParams(vmem_limit_bytes=mib * 1024 * 1024)


def lanes(shape):
    return lax.broadcasted_iota(jnp.int32, shape, len(shape) - 1)


def split3(value):
    high = value.astype(BF)
    rest = value - high.astype(F32)
    mid = rest.astype(BF)
    low = (rest - mid.astype(F32)).astype(BF)
    return high, mid, low


def pack2(total, lane):
    high = total.astype(BF).astype(F32)
    return jnp.where(lane == 0, high, jnp.where(lane == 1, total - high, 0.0))


def refs_kernel(refs_hbm, noise_hbm, out_ref, refs_ref, noise_ref, sems):
    d = lax.axis_index("dom")
    span = pl.ds(pl.multiple_of(d * KS, KS), KS)
    copies = [
        pltpu.make_async_copy(refs_hbm.at[:, :, span], refs_ref, sems.at[0]),
        pltpu.make_async_copy(noise_hbm.at[:, span], noise_ref, sems.at[1]),
    ]
    for copy in copies:
        copy.start()
    for copy in copies:
        copy.wait()
    noise = noise_ref[...]
    total = jnp.zeros((OD, 1), F32)
    for part in range(2):
        values = refs_ref[:, part, :].astype(F32)
        out_ref[:, part * KS : (part + 1) * KS] = (values * noise).astype(BF)
        total = total + jnp.sum(noise * values * values, axis=1, keepdims=True)
    high, mid, low = [term.astype(F32) for term in split3(0.5 * total)]
    lane = lanes((OD, EXT))
    norms = jnp.where(lane == 0, high, jnp.where(lane == 1, mid, jnp.where(lane == 2, low, 0.0)))
    out_ref[:, K2:] = norms.astype(BF)


def images_kernel(
    images_hbm, ids_hbm, mask_hbm, o0_ref, o1_ref, o2_ref, o3_ref, code_ref,
    images_ref, ids_ref, mask_ref, sems,
):
    d = lax.axis_index("dom")
    z = d // 2
    core = lax.rem(d, 2)
    copies = [
        pltpu.make_async_copy(images_hbm, images_ref, sems.at[0]),
        pltpu.make_async_copy(ids_hbm, ids_ref, sems.at[1]),
        pltpu.make_async_copy(mask_hbm, mask_ref, sems.at[2]),
    ]
    for copy in copies:
        copy.start()
    for copy in copies:
        copy.wait()
    marked = jnp.where(mask_ref[...] > 0, ids_ref[...] + OD, ids_ref[...])
    flat = jnp.concatenate([marked[:, c, :] for c in range(CAP)], axis=1)
    code_ref[...] = flat
    code = flat.astype(F32).astype(BF)
    for rz, out_ref in enumerate((o0_ref, o1_ref, o2_ref, o3_ref)):
        for rc in range(2):
            slot = lax.rem(z + rz, ZN) * 2 + (core if rc == 0 else 1 - core)
            span = pl.ds(pl.multiple_of(slot * KS, KS), KS)
            for part in range(2):
                out_ref[rc, :, part * KS : (part + 1) * KS] = images_ref[:, part, span]
            out_ref[rc, :, K2:] = code


def gather_kernel(b0_ref, b1_ref, b2_ref, b3_ref, line_ref):
    for place, ref in enumerate((b0_ref, b1_ref, b2_ref, b3_ref)):
        line_ref[place * OD : (place + 1) * OD, :] = ref[...]


def split_kernel(p0_ref, p1_ref, p2_ref, p3_ref, near_ref, far_ref):
    for place, ref in enumerate((p0_ref, p1_ref, p2_ref, p3_ref)):
        near_ref[place] = ref[0]
        far_ref[place] = ref[1]


def stack_kernel(s0_ref, s1_ref, s2_ref, s3_ref, out_ref):
    for place, ref in enumerate((s0_ref, s1_ref, s2_ref, s3_ref)):
        out_ref[place] = ref[...]


def first_axis(core, along_x, along_y):
    return jnp.where(core == 0, along_x, along_y)


def tables_kernel(
    shifts_ref, block_ref, piece_ref, cos_ref, sin_ref, own_block_ref, own_piece_ref
):
    own_block_ref[...] = block_ref[...]
    own_piece_ref[...] = piece_ref[...]
    d = lax.axis_index("dom")
    coefficient = d * KS + lanes((1, KS))
    row_freq = coefficient // GRID - GRID // 2
    col_freq = coefficient % GRID - GRID // 2
    turns = jnp.concatenate(
        [row_freq * shifts_ref[0, t] + col_freq * shifts_ref[1, t] for t in range(NTRANS)], axis=0
    )
    angles = turns.astype(F32) * (2.0 * math.pi / BOX)
    cos_ref[...] = jnp.cos(angles)
    sin_ref[...] = jnp.sin(angles)


def slots_kernel(near_ref, far_ref, near_inv, near_count, far_inv, far_count):
    core = lax.rem(lax.axis_index("dom"), 2)
    j = lax.axis_index("orient")
    lane = lanes((HALF, SLOTS))
    groups = ((near_ref, near_inv, near_count), (far_ref, far_inv, far_count))
    for images_ref, inv_ref, count_ref in groups:
        code = images_ref[:, :, K2:].reshape(HALF, EXT).astype(F32).astype(jnp.int32)
        for block in range(XN):
            along_x = first_axis(core, block, lane // OD)
            along_y = first_axis(core, lane // OD, block)
            owner = ((j // XN + along_y) % YN) * XN + (lax.rem(j, XN) + along_x) % XN
            inverse = jnp.zeros((HALF, YB), jnp.int32)
            count = jnp.zeros((HALF, YB), F32)
            for c in range(CAP):
                where_slot = c * OWNERS + owner
                seen = jnp.take_along_axis(code, where_slot, axis=1, mode="promise_in_bounds")
                match = seen == (lane % OD + OD)
                count = count + jnp.where(match, 1.0, 0.0)
                inverse = jnp.where(match, where_slot, inverse)
            inv_ref[:, block * YB : (block + 1) * YB] = inverse
            count_ref[:, block * YB : (block + 1) * YB] = count


def scores_kernel(rc, *refs):
    images_ref = refs[0]
    refs = refs[1:]
    refs_in = refs[:YN]
    cos_ref, sin_ref, shift_ref = refs[YN : YN + 3]
    outs = refs[YN + 3 : -1]
    weight_ref = refs[-1]
    core = lax.rem(lax.axis_index("dom"), 2)
    j = lax.axis_index("orient")
    lane8 = lanes((8, EXT))
    ones = jnp.where(lane8 < 3, 1.0, 0.0).astype(BF)
    norms = []
    for y in range(YN):
        weight_ref[y * YB : (y + 1) * YB, :] = refs_in[y][:, :K2]
        norms.append(nt(ones, refs_in[y][:, K2:])[0:1])
    lane = lanes((HALF, SLOTS))
    values = images_ref[...].reshape(HALF, KE).astype(F32)
    code = values[:, K2:].astype(jnp.int32)
    owner = lane % OWNERS
    along_y = (owner // XN + YN - j // XN) % YN
    along_x = (owner % XN + XN - lax.rem(j, XN)) % XN
    line = first_axis(core, along_y, along_x)
    index = first_axis(core, along_x, along_y) * OD + code % OD
    real = values[:, :KS]
    imag = values[:, KS:K2]
    for step in range(STEPS):
        base = step * ROWS
        for t in range(TC):
            row = step * TC + t
            cosine = cos_ref[row : row + 1, :]
            sine = sin_ref[row : row + 1, :]
            rows = slice(base + t * HALF, base + (t + 1) * HALF)
            shift_ref[rows, :KS] = (real * cosine - imag * sine).astype(BF)
            shift_ref[rows, KS:] = (real * sine + imag * cosine).astype(BF)
        scores = nt(shift_ref[base : base + ROWS, :], weight_ref[...])
        for t in range(TC):
            found = jnp.zeros((HALF, SLOTS), F32)
            for y in range(YN):
                span = slice(y * YB, (y + 1) * YB)
                block = scores[t * HALF : (t + 1) * HALF, span] - norms[y]
                picked = jnp.take_along_axis(block, index, axis=1, mode="promise_in_bounds")
                found = jnp.where(line == y, picked, found)
            if rc == 0:
                for rz in range(ZN):
                    outs[rz][step * TC + t] = found[rz * PART : (rz + 1) * PART, :]
            else:
                outs[0][:, step * TC + t] = found.reshape(ZN, PART, SLOTS)


def add_kernel(partner_ref, *refs):
    for rz in range(ZN):
        refs[ZN + rz][...] = refs[rz][...] + partner_ref[rz]


def posterior_kernel(own_ref, one_ref, two_ref, three_ref, code_ref, weight_ref, evidence_ref):
    valid = code_ref[...] >= OD
    scores = own_ref[...] + one_ref[...] + two_ref[...] + three_ref[...]
    masked = jnp.where(valid[None], scores, -1e30)
    highest = jnp.max(jnp.max(masked, axis=0), axis=1, keepdims=True)
    terms = jnp.where(valid[None], jnp.exp(scores - highest[None]), 0.0)
    summed = jnp.sum(jnp.sum(terms, axis=0), axis=1, keepdims=True)
    evidence = highest + jnp.log(summed)
    weights = jnp.where(valid[None], jnp.exp(scores - evidence[None]), 0.0)
    weight_ref[...] = weights.astype(BF)
    evidence_ref[...] = jnp.broadcast_to(evidence, evidence_ref.shape)


def dense_rows(blocks, slots, inv_ref, count_ref, dense_ref):
    column = []
    ones = jnp.ones((HALF, EXT), BF)
    for place, block in enumerate(blocks):
        span = slice(block * YB, (block + 1) * YB)
        inverse = inv_ref[:, span]
        count = count_ref[:, span]
        total = jnp.zeros((HALF, YB), F32)
        for t in range(NTRANS):
            picked = jnp.take_along_axis(slots[t], inverse, axis=1, mode="promise_in_bounds")
            weight = (picked * count).astype(BF)
            dense_ref[t * HALF : (t + 1) * HALF, place * YB : (place + 1) * YB] = weight
            total = total + weight.astype(F32)
        summed = jnp.zeros((YB, EXT), F32)
        for term in split3(total):
            summed = summed + tn(term, ones)
        column.append(summed)
    return column


def near_kernel(s0_ref, s1_ref, s2_ref, s3_ref, shift_ref, inv_ref, count_ref, acc_ref, dense_ref):
    parts = (s0_ref, s1_ref, s2_ref, s3_ref)
    slots = [
        jnp.concatenate([ref[t].astype(F32) for ref in parts], axis=0) for t in range(NTRANS)
    ]
    column = dense_rows(range(XN), slots, inv_ref, count_ref, dense_ref)
    for block in range(XN):
        acc_ref[block * YB : (block + 1) * YB, K2:] = column[block]
    for block in range(K2 // BLOCK):
        span = slice(block * BLOCK, (block + 1) * BLOCK)
        acc_ref[:, span] = tn(dense_ref[...], shift_ref[:, span])


def far_kernel(blocks, slot_ref, shift_ref, inv_ref, count_ref, acc_ref, *refs):
    outs = refs[:-1]
    dense_ref = refs[-1]
    slots = [slot_ref[:, t].reshape(HALF, SLOTS).astype(F32) for t in range(NTRANS)]
    column = dense_rows(blocks, slots, inv_ref, count_ref, dense_ref)
    lane = lanes((YB, EXT))
    for place, block in enumerate(blocks):
        total = acc_ref[block * YB : (block + 1) * YB, K2:] + column[place]
        outs[place][:, K2:] = pack2(total, lane).astype(outs[place].dtype)
    for part in range(K2 // BLOCK):
        span = slice(part * BLOCK, (part + 1) * BLOCK)
        sums = tn(dense_ref[...], shift_ref[:, span])
        for place, block in enumerate(blocks):
            done = acc_ref[block * YB : (block + 1) * YB, span]
            done = done + sums[place * YB : (place + 1) * YB, :]
            outs[place][:, span] = done.astype(outs[place].dtype)


def merge_kernel(own_ref, one_ref, two_ref, three_ref, *outs):
    lane = lanes((OD, EXT))
    for b in range(YN):
        rows = slice(b * OD, (b + 1) * OD)
        block = own_ref[rows, :]
        for other in (one_ref, two_ref, three_ref):
            block = block + other[rows, :].astype(F32)
        total = jnp.sum(block[:, K2:], axis=1, keepdims=True)
        outs[b][:, :K2] = block[:, :K2].astype(outs[b].dtype)
        outs[b][:, K2:] = pack2(total, lane).astype(outs[b].dtype)


def final_kernel(own_ref, one_ref, two_ref, three_ref, sum_ref, total_ref):
    block = own_ref[...]
    for other in (one_ref, two_ref, three_ref):
        block = block + other[...].astype(F32)
    sum_ref[:, 0, :] = block[:, :KS]
    sum_ref[:, 1, :] = block[:, KS:K2]
    ones = jnp.ones((8, EXT), BF)
    row = jnp.zeros((8, OD), F32)
    for term in split3(block[:, K2:]):
        row = row + nt(ones, term)
    total_ref[...] = row[0:1]


def shape(dims, dtype):
    return jax.ShapeDtypeStruct(dims, dtype)


def dom_core():
    return [(d, d ^ 1) for d in range(DOM)]


def along_z(value, step):
    return lax.ppermute(value, "dom", [(d, (d + 2 * step) % DOM) for d in range(DOM)])


def turn(step, first):
    pairs = []
    for d in range(DOM):
        for y in range(YN):
            for x in range(XN):
                if (d % 2 == 0) == first:
                    owner = y * XN + (x + step) % XN
                else:
                    owner = ((y + step) % YN) * XN + x
                pairs.append((d * OWNERS + y * XN + x, d * OWNERS + owner))
    return pairs


ORDER = (2, 1, 3)
BOTH = ("dom", "orient")


def along_first(value, step):
    return lax.ppermute(value, BOTH, turn(step, True))


def along_second(value, step):
    return lax.ppermute(value, BOTH, turn(step, False))


def cost(flops, moved):
    return pl.CostEstimate(flops=flops, bytes_accessed=moved, transcendentals=0)


def inside(kernel, arguments, out_shape, name, flops=0, scratch=(), mib=16):
    single = not isinstance(out_shape, list)
    return pl.pallas_call(
        kernel,
        in_specs=[INSIDE] * len(arguments),
        out_specs=INSIDE if single else [INSIDE] * len(out_shape),
        out_shape=out_shape,
        scratch_shapes=list(scratch),
        compiler_params=params(mib),
        cost_estimate=cost(flops, 2**20),
        name=name,
    )(*arguments)


def score_half(rc, images, lines, cosine, sine):
    part = shape((NTRANS, PART, SLOTS), F32)
    return inside(
        lambda *refs: scores_kernel(rc, *refs),
        [images, *lines, cosine, sine],
        [shape((NTRANS * HALF, K2), BF)]
        + ([part] * ZN if rc == 0 else [shape((ZN, NTRANS, PART, SLOTS), F32)]),
        "scores",
        flops=2 * NTRANS * HALF * K2 * YN * YB,
        scratch=[pltpu.VMEM((YN * YB, K2), BF)],
    )


def loader(kernel, arguments, out_shape, scratch, name, kib=56 * 1024):
    single = not isinstance(out_shape, list)
    return pl.pallas_call(
        kernel,
        in_specs=[pl.BlockSpec(memory_space=pl.ANY)] * len(arguments),
        out_specs=INSIDE if single else [INSIDE] * len(out_shape),
        out_shape=out_shape,
        scratch_shapes=scratch + [pltpu.SemaphoreType.DMA((len(arguments),))],
        compiler_params=pltpu.CompilerParams(vmem_limit_bytes=kib * 1024),
        name=name,
    )(*arguments)


def shards(images, references, noise_weight, candidate_ids, candidate_mask, shifts):
    scaled = loader(
        refs_kernel,
        [references, noise_weight.reshape(1, K)],
        shape((OD, KE), BF),
        [pltpu.VMEM((OD, 2, KS), BF), pltpu.VMEM((1, KS), F32)],
        "scale",
    )
    blocks = {}
    for step in ORDER:
        blocks[(-step) % XN] = along_first(scaled, step)
    codes = pltpu.VMEM((PART, CAP, OWNERS), jnp.int32)
    *cuts, code = loader(
        images_kernel,
        [images, jnp.swapaxes(candidate_ids, 1, 2), jnp.swapaxes(candidate_mask, 1, 2)],
        [shape((2, PART, KE), BF)] * ZN + [shape((PART, SLOTS), jnp.int32)],
        [pltpu.VMEM((PART, 2, K), BF), codes, codes],
        "cut_images",
    )
    pieces = {}
    for step in ORDER:
        pieces[(-step) % ZN] = along_z(cuts[step], step)
    cosine, sine, blocks[0], pieces[0] = pl.pallas_call(
        tables_kernel,
        in_specs=[pl.BlockSpec(memory_space=pltpu.SMEM)] + [INSIDE] * 2,
        out_specs=[INSIDE] * 4,
        out_shape=[shape((NTRANS, KS), F32)] * 2
        + [shape((OD, KE), BF), shape((2, PART, KE), BF)],
        compiler_params=params(8),
        name="tables",
    )(shifts.T, scaled, cuts[0])
    line = inside(
        gather_kernel, [blocks[b] for b in range(XN)], shape((YB, KE), BF), "gather"
    )
    lines = {0: line}
    for step in ORDER:
        lines[(-step) % YN] = along_second(line, step)
    lines = [lines[y] for y in range(YN)]
    near, far = inside(
        split_kernel,
        [pieces[rz] for rz in range(ZN)],
        [shape((ZN, PART, KE), BF)] * 2,
        "split_images",
    )
    far = lax.ppermute(far, "dom", dom_core())

    far_shift, far_slots = score_half(1, far, lines, cosine, sine)
    partner = lax.ppermute(far_slots, "dom", dom_core())
    near_shift, *near_slots = score_half(0, near, lines, cosine, sine)
    part = shape((NTRANS, PART, SLOTS), F32)
    slots = inside(add_kernel, [partner, *near_slots], [part] * ZN, "add_cores")
    arrived = [along_z(slots[step], step) for step in ORDER]
    near_inv, near_count, far_inv, far_count = inside(
        slots_kernel,
        [near, far],
        [shape((HALF, YN * YB), jnp.int32), shape((HALF, YN * YB), F32)] * 2,
        "slot_map",
    )
    code, near_inv, near_count, far_inv, far_count = lax.optimization_barrier(
        (code, near_inv, near_count, far_inv, far_count)
    )
    weights, evidence = inside(
        posterior_kernel,
        [slots[0], *arrived, code],
        [shape((NTRANS, PART, SLOTS), BF), shape((PART, SLOTS), F32)],
        "posterior",
    )

    mine = {0: weights}
    for step in ORDER:
        mine[(-step) % ZN] = along_z(weights, step)
    near_weights = [mine[rz] for rz in range(ZN)]
    stacked = inside(
        stack_kernel, near_weights, shape((ZN, NTRANS, PART, SLOTS), BF), "stack_weights"
    )
    far_weights = lax.ppermute(stacked, "dom", dom_core())
    flops = 2 * NTRANS * HALF * K2 * YN * YB
    acc = inside(
        near_kernel,
        [*near_weights, near_shift, near_inv, near_count],
        shape((YN * YB, KE), F32),
        "near_sums",
        flops=flops,
        scratch=[pltpu.VMEM((NTRANS * HALF, YN * YB), BF)],
    )
    outs = {}
    for targets in ((2, 1), (3, 0)):
        pair = inside(
            lambda *refs, targets=targets: far_kernel(targets, *refs),
            [far_weights, far_shift, far_inv, far_count, acc],
            [shape((YB, KE), F32 if target == 0 else BF) for target in targets],
            "far_sums",
            flops=flops // 2,
            scratch=[pltpu.VMEM((NTRANS * HALF, 2 * YB), BF)],
        )
        outs.update(zip(targets, pair))
    rows = inside(
        merge_kernel,
        [outs[0]] + [along_first(outs[step], step) for step in ORDER],
        [shape((OD, KE), F32 if b == 0 else BF) for b in range(YN)],
        "merge_first",
    )
    image_sums, totals = inside(
        final_kernel,
        [rows[0]] + [along_second(rows[step], step) for step in ORDER],
        [shape((OD, 2, KS), F32), shape((1, OD), F32)],
        "merge_second",
    )
    return image_sums, totals.reshape(OD), evidence[:, 0]


def solution(mesh):
    return jax.shard_map(
        shards,
        mesh=mesh,
        in_specs=(
            P(("dom", "orient"), None, None),
            P("orient", None, None),
            P(),
            P(("dom", "orient"), None, None),
            P(("dom", "orient"), None, None),
            P(),
        ),
        out_specs=(P("orient", None, "dom"), P("orient"), P(("dom", "orient"))),
        check_vma=False,
    )
```

```python
import math

import jax
import jax.numpy as jnp
from jax import lax
from jax.experimental import pallas as pl
from jax.experimental.pallas import tpu as pltpu
from jax.sharding import PartitionSpec as P

GRID = 64
K = 4096
BOX = 400
NTRANS = 25
CAP = 8
ZN = 4
YN = 4
XN = 4
DOM = 8
PART = 16
KS = K // DOM
K2 = 2 * KS
EXT = 128
KE = K2 + EXT
SLOTS = 128
OD = 32
YB = XN * OD
TC = 5
STEPS = NTRANS // TC
HALF = ZN * PART
ROWS = TC * HALF
BF = jnp.bfloat16
F32 = jnp.float32
BLOCK = 256
OWNERS = YN * XN
INSIDE = pl.BlockSpec(memory_space=pltpu.VMEM)


def nt(left, right):
    return lax.dot_general(
        left, right, (((1,), (1,)), ((), ())), preferred_element_type=F32
    )


def tn(left, right):
    return lax.dot_general(
        left, right, (((0,), (0,)), ((), ())), preferred_element_type=F32
    )


def params(mib=16):
    return pltpu.CompilerParams(vmem_limit_bytes=mib * 1024 * 1024)


def lanes(shape):
    return lax.broadcasted_iota(jnp.int32, shape, len(shape) - 1)


def split3(value):
    high = value.astype(BF)
    rest = value - high.astype(F32)
    mid = rest.astype(BF)
    low = (rest - mid.astype(F32)).astype(BF)
    return high, mid, low


def pack2(total, lane):
    high = total.astype(BF).astype(F32)
    return jnp.where(lane == 0, high, jnp.where(lane == 1, total - high, 0.0))


def prepare_kernel(
    refs_hbm, noise_hbm, images_hbm, ids_hbm, mask_hbm,
    scaled_ref, o0_ref, o1_ref, o2_ref, o3_ref, code_ref,
    refs_ref, noise_ref, images_ref, ids_ref, mask_ref, sems,
):
    d = lax.axis_index("dom")
    z = d // 2
    core = lax.rem(d, 2)
    span = pl.ds(pl.multiple_of(d * KS, KS), KS)
    copies = [
        pltpu.make_async_copy(refs_hbm.at[:, :, span], refs_ref, sems.at[0]),
        pltpu.make_async_copy(noise_hbm.at[:, span], noise_ref, sems.at[1]),
        pltpu.make_async_copy(images_hbm, images_ref, sems.at[2]),
        pltpu.make_async_copy(ids_hbm, ids_ref, sems.at[3]),
        pltpu.make_async_copy(mask_hbm, mask_ref, sems.at[4]),
    ]
    for copy in copies:
        copy.start()
    for copy in copies[:2]:
        copy.wait()
    noise = noise_ref[...]
    total = jnp.zeros((OD, 1), F32)
    for part in range(2):
        values = refs_ref[:, part, :].astype(F32)
        scaled_ref[:, part * KS : (part + 1) * KS] = (values * noise).astype(BF)
        total = total + jnp.sum(noise * values * values, axis=1, keepdims=True)
    high, mid, low = [term.astype(F32) for term in split3(0.5 * total)]
    lane = lanes((OD, EXT))
    norms = jnp.where(lane == 0, high, jnp.where(lane == 1, mid, jnp.where(lane == 2, low, 0.0)))
    scaled_ref[:, K2:] = norms.astype(BF)
    for copy in copies[2:]:
        copy.wait()
    marked = jnp.where(mask_ref[...] > 0, ids_ref[...] + OD, ids_ref[...])
    flat = jnp.concatenate([marked[:, c, :] for c in range(CAP)], axis=1)
    code_ref[...] = flat
    code = flat.astype(F32).astype(BF)
    for rz, out_ref in enumerate((o0_ref, o1_ref, o2_ref, o3_ref)):
        for rc in range(2):
            slot = lax.rem(z + rz, ZN) * 2 + (core if rc == 0 else 1 - core)
            span = pl.ds(pl.multiple_of(slot * KS, KS), KS)
            for part in range(2):
                out_ref[rc, :, part * KS : (part + 1) * KS] = images_ref[:, part, span]
            out_ref[rc, :, K2:] = code


def gather_kernel(b0_ref, b1_ref, b2_ref, b3_ref, line_ref):
    for place, ref in enumerate((b0_ref, b1_ref, b2_ref, b3_ref)):
        line_ref[place * OD : (place + 1) * OD, :] = ref[...]


def split_kernel(p0_ref, p1_ref, p2_ref, p3_ref, near_ref, far_ref):
    for place, ref in enumerate((p0_ref, p1_ref, p2_ref, p3_ref)):
        near_ref[place] = ref[0]
        far_ref[place] = ref[1]


def stack_kernel(s0_ref, s1_ref, s2_ref, s3_ref, out_ref):
    for place, ref in enumerate((s0_ref, s1_ref, s2_ref, s3_ref)):
        out_ref[place] = ref[...]


def first_axis(core, along_x, along_y):
    return jnp.where(core == 0, along_x, along_y)


def tables_kernel(shifts_ref, cos_ref, sin_ref):
    d = lax.axis_index("dom")
    coefficient = d * KS + lanes((1, KS))
    row_freq = coefficient // GRID - GRID // 2
    col_freq = coefficient % GRID - GRID // 2
    turns = jnp.concatenate(
        [row_freq * shifts_ref[0, t] + col_freq * shifts_ref[1, t] for t in range(NTRANS)], axis=0
    )
    angles = turns.astype(F32) * (2.0 * math.pi / BOX)
    cos_ref[...] = jnp.cos(angles)
    sin_ref[...] = jnp.sin(angles)


def slots_kernel(near_ref, far_ref, near_inv, near_count, far_inv, far_count):
    core = lax.rem(lax.axis_index("dom"), 2)
    j = lax.axis_index("orient")
    lane = lanes((HALF, SLOTS))
    groups = ((near_ref, near_inv, near_count), (far_ref, far_inv, far_count))
    for images_ref, inv_ref, count_ref in groups:
        code = images_ref[:, :, K2:].reshape(HALF, EXT).astype(F32).astype(jnp.int32)
        for block in range(XN):
            along_x = first_axis(core, block, lane // OD)
            along_y = first_axis(core, lane // OD, block)
            owner = ((j // XN + along_y) % YN) * XN + (lax.rem(j, XN) + along_x) % XN
            inverse = jnp.zeros((HALF, YB), jnp.int32)
            count = jnp.zeros((HALF, YB), F32)
            for c in range(CAP):
                where_slot = c * OWNERS + owner
                seen = jnp.take_along_axis(code, where_slot, axis=1, mode="promise_in_bounds")
                match = seen == (lane % OD + OD)
                count = count + jnp.where(match, 1.0, 0.0)
                inverse = jnp.where(match, where_slot, inverse)
            inv_ref[:, block * YB : (block + 1) * YB] = inverse
            count_ref[:, block * YB : (block + 1) * YB] = count


def scores_kernel(rc, *refs):
    images_ref = refs[0]
    refs = refs[1:]
    refs_in = refs[:YN]
    cos_ref, sin_ref, shift_ref = refs[YN : YN + 3]
    outs = refs[YN + 3 : -1]
    weight_ref = refs[-1]
    core = lax.rem(lax.axis_index("dom"), 2)
    j = lax.axis_index("orient")
    lane8 = lanes((8, EXT))
    ones = jnp.where(lane8 < 3, 1.0, 0.0).astype(BF)
    norms = []
    for y in range(YN):
        weight_ref[y * YB : (y + 1) * YB, :] = refs_in[y][:, :K2]
        norms.append(nt(ones, refs_in[y][:, K2:])[0:1])
    lane = lanes((HALF, SLOTS))
    values = images_ref[...].reshape(HALF, KE).astype(F32)
    code = values[:, K2:].astype(jnp.int32)
    owner = lane % OWNERS
    along_y = (owner // XN + YN - j // XN) % YN
    along_x = (owner % XN + XN - lax.rem(j, XN)) % XN
    line = first_axis(core, along_y, along_x)
    index = first_axis(core, along_x, along_y) * OD + code % OD
    real = values[:, :KS]
    imag = values[:, KS:K2]
    for step in range(STEPS):
        base = step * ROWS
        for t in range(TC):
            row = step * TC + t
            cosine = cos_ref[row : row + 1, :]
            sine = sin_ref[row : row + 1, :]
            rows = slice(base + t * HALF, base + (t + 1) * HALF)
            shift_ref[rows, :KS] = (real * cosine - imag * sine).astype(BF)
            shift_ref[rows, KS:] = (real * sine + imag * cosine).astype(BF)
        scores = nt(shift_ref[base : base + ROWS, :], weight_ref[...])
        for t in range(TC):
            found = jnp.zeros((HALF, SLOTS), F32)
            for y in range(YN):
                span = slice(y * YB, (y + 1) * YB)
                block = scores[t * HALF : (t + 1) * HALF, span] - norms[y]
                picked = jnp.take_along_axis(block, index, axis=1, mode="promise_in_bounds")
                found = jnp.where(line == y, picked, found)
            if rc == 0:
                for rz in range(ZN):
                    outs[rz][step * TC + t] = found[rz * PART : (rz + 1) * PART, :]
            else:
                outs[0][:, step * TC + t] = found.reshape(ZN, PART, SLOTS)


def add_kernel(partner_ref, *refs):
    for rz in range(ZN):
        refs[ZN + rz][...] = refs[rz][...] + partner_ref[rz]


def posterior_kernel(own_ref, one_ref, two_ref, three_ref, code_ref, weight_ref, evidence_ref):
    valid = code_ref[...] >= OD
    scores = own_ref[...] + one_ref[...] + two_ref[...] + three_ref[...]
    masked = jnp.where(valid[None], scores, -1e30)
    highest = jnp.max(jnp.max(masked, axis=0), axis=1, keepdims=True)
    terms = jnp.where(valid[None], jnp.exp(scores - highest[None]), 0.0)
    summed = jnp.sum(jnp.sum(terms, axis=0), axis=1, keepdims=True)
    evidence = highest + jnp.log(summed)
    weights = jnp.where(valid[None], jnp.exp(scores - evidence[None]), 0.0)
    weight_ref[...] = weights.astype(BF)
    evidence_ref[...] = jnp.broadcast_to(evidence, evidence_ref.shape)


def dense_rows(blocks, slots, inv_ref, count_ref, dense_ref):
    column = []
    ones = jnp.ones((HALF, EXT), BF)
    for place, block in enumerate(blocks):
        span = slice(block * YB, (block + 1) * YB)
        inverse = inv_ref[:, span]
        count = count_ref[:, span]
        total = jnp.zeros((HALF, YB), F32)
        for t in range(NTRANS):
            picked = jnp.take_along_axis(slots[t], inverse, axis=1, mode="promise_in_bounds")
            weight = (picked * count).astype(BF)
            dense_ref[t * HALF : (t + 1) * HALF, place * YB : (place + 1) * YB] = weight
            total = total + weight.astype(F32)
        summed = jnp.zeros((YB, EXT), F32)
        for term in split3(total):
            summed = summed + tn(term, ones)
        column.append(summed)
    return column


def near_kernel(s0_ref, s1_ref, s2_ref, s3_ref, shift_ref, inv_ref, count_ref, acc_ref, dense_ref):
    parts = (s0_ref, s1_ref, s2_ref, s3_ref)
    slots = [
        jnp.concatenate([ref[t].astype(F32) for ref in parts], axis=0) for t in range(NTRANS)
    ]
    column = dense_rows(range(XN), slots, inv_ref, count_ref, dense_ref)
    for block in range(XN):
        acc_ref[block * YB : (block + 1) * YB, K2:] = column[block]
    for block in range(K2 // BLOCK):
        span = slice(block * BLOCK, (block + 1) * BLOCK)
        acc_ref[:, span] = tn(dense_ref[...], shift_ref[:, span])


def far_kernel(blocks, slot_ref, shift_ref, inv_ref, count_ref, acc_ref, *refs):
    outs = refs[:-1]
    dense_ref = refs[-1]
    slots = [slot_ref[:, t].reshape(HALF, SLOTS).astype(F32) for t in range(NTRANS)]
    column = dense_rows(blocks, slots, inv_ref, count_ref, dense_ref)
    lane = lanes((YB, EXT))
    for place, block in enumerate(blocks):
        total = acc_ref[block * YB : (block + 1) * YB, K2:] + column[place]
        outs[place][:, K2:] = pack2(total, lane).astype(outs[place].dtype)
    for part in range(K2 // BLOCK):
        span = slice(part * BLOCK, (part + 1) * BLOCK)
        sums = tn(dense_ref[...], shift_ref[:, span])
        for place, block in enumerate(blocks):
            done = acc_ref[block * YB : (block + 1) * YB, span]
            done = done + sums[place * YB : (place + 1) * YB, :]
            outs[place][:, span] = done.astype(outs[place].dtype)


def merge_kernel(own_ref, one_ref, two_ref, three_ref, *outs):
    lane = lanes((OD, EXT))
    for b in range(YN):
        rows = slice(b * OD, (b + 1) * OD)
        block = own_ref[rows, :]
        for other in (one_ref, two_ref, three_ref):
            block = block + other[rows, :].astype(F32)
        total = jnp.sum(block[:, K2:], axis=1, keepdims=True)
        outs[b][:, :K2] = block[:, :K2].astype(outs[b].dtype)
        outs[b][:, K2:] = pack2(total, lane).astype(outs[b].dtype)


def final_kernel(own_ref, one_ref, two_ref, three_ref, sum_ref, total_ref):
    block = own_ref[...]
    for other in (one_ref, two_ref, three_ref):
        block = block + other[...].astype(F32)
    sum_ref[:, 0, :] = block[:, :KS]
    sum_ref[:, 1, :] = block[:, KS:K2]
    ones = jnp.ones((8, EXT), BF)
    row = jnp.zeros((8, OD), F32)
    for term in split3(block[:, K2:]):
        row = row + nt(ones, term)
    total_ref[...] = row[0:1]


def shape(dims, dtype):
    return jax.ShapeDtypeStruct(dims, dtype)


def dom_core():
    return [(d, d ^ 1) for d in range(DOM)]


def along_z(value, step):
    return lax.ppermute(value, "dom", [(d, (d + 2 * step) % DOM) for d in range(DOM)])


def turn(step, first):
    pairs = []
    for d in range(DOM):
        for y in range(YN):
            for x in range(XN):
                if (d % 2 == 0) == first:
                    owner = y * XN + (x + step) % XN
                else:
                    owner = ((y + step) % YN) * XN + x
                pairs.append((d * OWNERS + y * XN + x, d * OWNERS + owner))
    return pairs


ORDER = (2, 1, 3)
BOTH = ("dom", "orient")


def along_first(value, step):
    return lax.ppermute(value, BOTH, turn(step, True))


def along_second(value, step):
    return lax.ppermute(value, BOTH, turn(step, False))


def cost(flops, moved):
    return pl.CostEstimate(flops=flops, bytes_accessed=moved, transcendentals=0)


def inside(kernel, arguments, out_shape, name, flops=0, scratch=(), mib=16):
    single = not isinstance(out_shape, list)
    return pl.pallas_call(
        kernel,
        in_specs=[INSIDE] * len(arguments),
        out_specs=INSIDE if single else [INSIDE] * len(out_shape),
        out_shape=out_shape,
        scratch_shapes=list(scratch),
        compiler_params=params(mib),
        cost_estimate=cost(flops, 2**20),
        name=name,
    )(*arguments)


def score_half(rc, images, lines, cosine, sine):
    part = shape((NTRANS, PART, SLOTS), F32)
    return inside(
        lambda *refs: scores_kernel(rc, *refs),
        [images, *lines, cosine, sine],
        [shape((NTRANS * HALF, K2), BF)]
        + ([part] * ZN if rc == 0 else [shape((ZN, NTRANS, PART, SLOTS), F32)]),
        "scores",
        flops=2 * NTRANS * HALF * K2 * YN * YB,
        scratch=[pltpu.VMEM((YN * YB, K2), BF)],
    )


def prepare(references, noise_weight, images, ids, mask):
    codes = pltpu.VMEM((PART, CAP, OWNERS), jnp.int32)
    return pl.pallas_call(
        prepare_kernel,
        in_specs=[pl.BlockSpec(memory_space=pl.ANY)] * 5,
        out_specs=[INSIDE] * 6,
        out_shape=[shape((OD, KE), BF)]
        + [shape((2, PART, KE), BF)] * ZN
        + [shape((PART, SLOTS), jnp.int32)],
        scratch_shapes=[
            pltpu.VMEM((OD, 2, KS), BF),
            pltpu.VMEM((1, KS), F32),
            pltpu.VMEM((PART, 2, K), BF),
            codes,
            codes,
            pltpu.SemaphoreType.DMA((5,)),
        ],
        compiler_params=params(56),
        name="prepare",
    )(
        references,
        noise_weight.reshape(1, K),
        images,
        jnp.swapaxes(ids, 1, 2),
        jnp.swapaxes(mask, 1, 2),
    )


def shards(images, references, noise_weight, candidate_ids, candidate_mask, shifts):
    scaled, *cuts, code = prepare(
        references, noise_weight, images, candidate_ids, candidate_mask
    )
    blocks = {0: scaled}
    for step in ORDER:
        blocks[(-step) % XN] = along_first(scaled, step)
    pieces = {0: cuts[0]}
    for step in ORDER:
        pieces[(-step) % ZN] = along_z(cuts[step], step)
    line = inside(
        gather_kernel, [blocks[b] for b in range(XN)], shape((YB, KE), BF), "gather"
    )
    lines = {0: line}
    for step in ORDER:
        lines[(-step) % YN] = along_second(line, step)
    lines = [lines[y] for y in range(YN)]
    near, far = inside(
        split_kernel,
        [pieces[rz] for rz in range(ZN)],
        [shape((ZN, PART, KE), BF)] * 2,
        "split_images",
    )
    far = lax.ppermute(far, "dom", dom_core())
    cosine, sine = pl.pallas_call(
        tables_kernel,
        in_specs=[pl.BlockSpec(memory_space=pltpu.SMEM)],
        out_specs=[INSIDE] * 2,
        out_shape=[shape((NTRANS, KS), F32)] * 2,
        compiler_params=params(8),
        name="tables",
    )(shifts.T)

    far_shift, far_slots = score_half(1, far, lines, cosine, sine)
    partner = lax.ppermute(far_slots, "dom", dom_core())
    near_shift, *near_slots = score_half(0, near, lines, cosine, sine)
    part = shape((NTRANS, PART, SLOTS), F32)
    slots = inside(add_kernel, [partner, *near_slots], [part] * ZN, "add_cores")
    arrived = [along_z(slots[step], step) for step in ORDER]
    near_inv, near_count, far_inv, far_count = inside(
        slots_kernel,
        [near, far],
        [shape((HALF, YN * YB), jnp.int32), shape((HALF, YN * YB), F32)] * 2,
        "slot_map",
    )
    code, near_inv, near_count, far_inv, far_count = lax.optimization_barrier(
        (code, near_inv, near_count, far_inv, far_count)
    )
    weights, evidence = inside(
        posterior_kernel,
        [slots[0], *arrived, code],
        [shape((NTRANS, PART, SLOTS), BF), shape((PART, SLOTS), F32)],
        "posterior",
    )

    mine = {0: weights}
    for step in ORDER:
        mine[(-step) % ZN] = along_z(weights, step)
    near_weights = [mine[rz] for rz in range(ZN)]
    stacked = inside(
        stack_kernel, near_weights, shape((ZN, NTRANS, PART, SLOTS), BF), "stack_weights"
    )
    far_weights = lax.ppermute(stacked, "dom", dom_core())
    flops = 2 * NTRANS * HALF * K2 * YN * YB
    acc = inside(
        near_kernel,
        [*near_weights, near_shift, near_inv, near_count],
        shape((YN * YB, KE), F32),
        "near_sums",
        flops=flops,
        scratch=[pltpu.VMEM((NTRANS * HALF, YN * YB), BF)],
    )
    outs = {}
    for targets in ((2, 1), (3,), (0,)):
        pair = inside(
            lambda *refs, targets=targets: far_kernel(targets, *refs),
            [far_weights, far_shift, far_inv, far_count, acc],
            [shape((YB, KE), F32 if target == 0 else BF) for target in targets],
            "far_sums",
            flops=flops * len(targets) // XN,
            scratch=[pltpu.VMEM((NTRANS * HALF, len(targets) * YB), BF)],
        )
        outs.update(zip(targets, pair))
    rows = inside(
        merge_kernel,
        [outs[0]] + [along_first(outs[step], step) for step in ORDER],
        [shape((OD, KE), F32 if b == 0 else BF) for b in range(YN)],
        "merge_first",
    )
    image_sums, totals = inside(
        final_kernel,
        [rows[0]] + [along_second(rows[step], step) for step in ORDER],
        [shape((OD, 2, KS), F32), shape((1, OD), F32)],
        "merge_second",
    )
    return image_sums, totals.reshape(OD), evidence[:, 0]


def solution(mesh):
    return jax.shard_map(
        shards,
        mesh=mesh,
        in_specs=(
            P(("dom", "orient"), None, None),
            P("orient", None, None),
            P(),
            P(("dom", "orient"), None, None),
            P(("dom", "orient"), None, None),
            P(),
        ),
        out_specs=(P("orient", None, "dom"), P("orient"), P(("dom", "orient"))),
        check_vma=False,
    )
```

```python
import math

import jax
import jax.numpy as jnp
from jax import lax
from jax.experimental import pallas as pl
from jax.experimental.pallas import tpu as pltpu
from jax.sharding import PartitionSpec as P

GRID = 64
K = 4096
BOX = 400
NTRANS = 25
CAP = 8
ZN = 4
YN = 4
XN = 4
DOM = 8
PART = 16
KS = K // DOM
K2 = 2 * KS
EXT = 128
KE = K2 + EXT
SLOTS = 128
OD = 32
YB = XN * OD
TC = 5
STEPS = NTRANS // TC
HALF = ZN * PART
ROWS = TC * HALF
BF = jnp.bfloat16
F32 = jnp.float32
BLOCK = 256
OWNERS = YN * XN
INSIDE = pl.BlockSpec(memory_space=pltpu.VMEM)


def nt(left, right):
    return lax.dot_general(
        left, right, (((1,), (1,)), ((), ())), preferred_element_type=F32
    )


def tn(left, right):
    return lax.dot_general(
        left, right, (((0,), (0,)), ((), ())), preferred_element_type=F32
    )


def params(mib=16):
    return pltpu.CompilerParams(vmem_limit_bytes=mib * 1024 * 1024)


def lanes(shape):
    return lax.broadcasted_iota(jnp.int32, shape, len(shape) - 1)


def split3(value):
    high = value.astype(BF)
    rest = value - high.astype(F32)
    mid = rest.astype(BF)
    low = (rest - mid.astype(F32)).astype(BF)
    return high, mid, low


def pack2(total, lane):
    high = total.astype(BF).astype(F32)
    return jnp.where(lane == 0, high, jnp.where(lane == 1, total - high, 0.0))


def phase_tables(d, shifts_ref, cos_ref, sin_ref):
    coefficient = d * KS + lanes((1, KS))
    row_freq = coefficient // GRID - GRID // 2
    col_freq = coefficient % GRID - GRID // 2
    turns = jnp.concatenate(
        [row_freq * shifts_ref[0, t] + col_freq * shifts_ref[1, t] for t in range(NTRANS)], axis=0
    )
    angles = turns.astype(F32) * (2.0 * math.pi / BOX)
    cos_ref[...] = jnp.cos(angles)
    sin_ref[...] = jnp.sin(angles)


def prepare_kernel(
    refs_hbm, noise_hbm, shifts_hbm, images_hbm, ids_hbm, mask_hbm,
    scaled_ref, near_ref, far_ref, code_ref, cos_ref, sin_ref,
    refs_ref, noise_ref, shifts_ref, images_ref, ids_ref, mask_ref, sems,
):
    d = lax.axis_index("dom")
    z = d // 2
    core = lax.rem(d, 2)
    span = pl.ds(pl.multiple_of(d * KS, KS), KS)
    copies = [
        pltpu.make_async_copy(refs_hbm.at[:, :, span], refs_ref, sems.at[0]),
        pltpu.make_async_copy(noise_hbm.at[:, span], noise_ref, sems.at[1]),
        pltpu.make_async_copy(shifts_hbm, shifts_ref, sems.at[2]),
        pltpu.make_async_copy(images_hbm, images_ref, sems.at[3]),
        pltpu.make_async_copy(ids_hbm, ids_ref, sems.at[4]),
        pltpu.make_async_copy(mask_hbm, mask_ref, sems.at[5]),
    ]
    for copy in copies:
        copy.start()
    copies[2].wait()
    phase_tables(d, shifts_ref, cos_ref, sin_ref)
    for copy in copies[:2]:
        copy.wait()
    noise = noise_ref[...]
    total = jnp.zeros((OD, 1), F32)
    for part in range(2):
        values = refs_ref[:, part, :].astype(F32)
        scaled_ref[:, part * KS : (part + 1) * KS] = (values * noise).astype(BF)
        total = total + jnp.sum(noise * values * values, axis=1, keepdims=True)
    high, mid, low = [term.astype(F32) for term in split3(0.5 * total)]
    lane = lanes((OD, EXT))
    norms = jnp.where(lane == 0, high, jnp.where(lane == 1, mid, jnp.where(lane == 2, low, 0.0)))
    scaled_ref[:, K2:] = norms.astype(BF)
    for copy in copies[3:]:
        copy.wait()
    marked = jnp.where(mask_ref[...] > 0, ids_ref[...] + OD, ids_ref[...])
    flat = jnp.concatenate([marked[:, c, :] for c in range(CAP)], axis=1)
    code_ref[...] = flat
    code = flat.astype(F32).astype(BF)
    for rz in range(ZN):
        for rc, out_ref in enumerate((near_ref, far_ref)):
            slot = lax.rem(z + rz, ZN) * 2 + (core if rc == 0 else 1 - core)
            span = pl.ds(pl.multiple_of(slot * KS, KS), KS)
            for part in range(2):
                out_ref[rz, :, part * KS : (part + 1) * KS] = images_ref[:, part, span]
            out_ref[rz, :, K2:] = code


def gather_kernel(b0_ref, b1_ref, b2_ref, b3_ref, line_ref):
    for place, ref in enumerate((b0_ref, b1_ref, b2_ref, b3_ref)):
        line_ref[place * OD : (place + 1) * OD, :] = ref[...]


def pair_kernel(near_ref, far_ref, *outs):
    for place, ref in enumerate(outs):
        ref[0] = near_ref[place]
        ref[1] = far_ref[place]


def stack_kernel(s0_ref, s1_ref, s2_ref, s3_ref, out_ref):
    for place, ref in enumerate((s0_ref, s1_ref, s2_ref, s3_ref)):
        out_ref[place] = ref[...]


def first_axis(core, along_x, along_y):
    return jnp.where(core == 0, along_x, along_y)


def slots_kernel(p0_ref, p1_ref, p2_ref, p3_ref, near_inv, near_count, far_inv, far_count):
    core = lax.rem(lax.axis_index("dom"), 2)
    j = lax.axis_index("orient")
    lane = lanes((HALF, SLOTS))
    pieces = (p0_ref, p1_ref, p2_ref, p3_ref)
    for rc, (inv_ref, count_ref) in enumerate(((near_inv, near_count), (far_inv, far_count))):
        code = jnp.concatenate([ref[rc, :, K2:].astype(F32) for ref in pieces], axis=0)
        code = code.astype(jnp.int32)
        for block in range(XN):
            along_x = first_axis(core, block, lane // OD)
            along_y = first_axis(core, lane // OD, block)
            owner = ((j // XN + along_y) % YN) * XN + (lax.rem(j, XN) + along_x) % XN
            inverse = jnp.zeros((HALF, YB), jnp.int32)
            count = jnp.zeros((HALF, YB), F32)
            for c in range(CAP):
                where_slot = c * OWNERS + owner
                seen = jnp.take_along_axis(code, where_slot, axis=1, mode="promise_in_bounds")
                match = seen == (lane % OD + OD)
                count = count + jnp.where(match, 1.0, 0.0)
                inverse = jnp.where(match, where_slot, inverse)
            inv_ref[:, block * YB : (block + 1) * YB] = inverse
            count_ref[:, block * YB : (block + 1) * YB] = count


def scores_kernel(rc, *refs):
    images = [ref[rc] for ref in refs[:ZN]]
    refs = refs[ZN:]
    refs_in = refs[:YN]
    cos_ref, sin_ref, shift_ref = refs[YN : YN + 3]
    outs = refs[YN + 3 : -1]
    weight_ref = refs[-1]
    core = lax.rem(lax.axis_index("dom"), 2)
    j = lax.axis_index("orient")
    lane8 = lanes((8, EXT))
    ones = jnp.where(lane8 < 3, 1.0, 0.0).astype(BF)
    norms = []
    for y in range(YN):
        weight_ref[y * YB : (y + 1) * YB, :] = refs_in[y][:, :K2]
        norms.append(nt(ones, refs_in[y][:, K2:])[0:1])
    lane = lanes((HALF, SLOTS))
    values = jnp.concatenate([part.astype(F32) for part in images], axis=0)
    code = values[:, K2:].astype(jnp.int32)
    owner = lane % OWNERS
    along_y = (owner // XN + YN - j // XN) % YN
    along_x = (owner % XN + XN - lax.rem(j, XN)) % XN
    line = first_axis(core, along_y, along_x)
    index = first_axis(core, along_x, along_y) * OD + code % OD
    real = values[:, :KS]
    imag = values[:, KS:K2]
    for step in range(STEPS):
        base = step * ROWS
        for t in range(TC):
            row = step * TC + t
            cosine = cos_ref[row : row + 1, :]
            sine = sin_ref[row : row + 1, :]
            rows = slice(base + t * HALF, base + (t + 1) * HALF)
            shift_ref[rows, :KS] = (real * cosine - imag * sine).astype(BF)
            shift_ref[rows, KS:] = (real * sine + imag * cosine).astype(BF)
        scores = nt(shift_ref[base : base + ROWS, :], weight_ref[...])
        for t in range(TC):
            found = jnp.zeros((HALF, SLOTS), F32)
            for y in range(YN):
                span = slice(y * YB, (y + 1) * YB)
                block = scores[t * HALF : (t + 1) * HALF, span] - norms[y]
                picked = jnp.take_along_axis(block, index, axis=1, mode="promise_in_bounds")
                found = jnp.where(line == y, picked, found)
            if rc == 0:
                for rz in range(ZN):
                    outs[rz][step * TC + t] = found[rz * PART : (rz + 1) * PART, :]
            else:
                outs[0][:, step * TC + t] = found.reshape(ZN, PART, SLOTS)


def add_kernel(partner_ref, *refs):
    for rz in range(ZN):
        refs[ZN + rz][...] = refs[rz][...] + partner_ref[rz]


def posterior_kernel(own_ref, one_ref, two_ref, three_ref, code_ref, weight_ref, evidence_ref):
    valid = code_ref[...] >= OD
    scores = own_ref[...] + one_ref[...] + two_ref[...] + three_ref[...]
    masked = jnp.where(valid[None], scores, -1e30)
    highest = jnp.max(jnp.max(masked, axis=0), axis=1, keepdims=True)
    terms = jnp.where(valid[None], jnp.exp(scores - highest[None]), 0.0)
    summed = jnp.sum(jnp.sum(terms, axis=0), axis=1, keepdims=True)
    evidence = highest + jnp.log(summed)
    weights = jnp.where(valid[None], jnp.exp(scores - evidence[None]), 0.0)
    weight_ref[...] = weights.astype(BF)
    evidence_ref[...] = jnp.broadcast_to(evidence, evidence_ref.shape)


def dense_rows(blocks, slots, inv_ref, count_ref, dense_ref):
    column = []
    ones = jnp.ones((HALF, EXT), BF)
    for place, block in enumerate(blocks):
        span = slice(block * YB, (block + 1) * YB)
        inverse = inv_ref[:, span]
        count = count_ref[:, span]
        total = jnp.zeros((HALF, YB), F32)
        for t in range(NTRANS):
            picked = jnp.take_along_axis(slots[t], inverse, axis=1, mode="promise_in_bounds")
            weight = (picked * count).astype(BF)
            dense_ref[t * HALF : (t + 1) * HALF, place * YB : (place + 1) * YB] = weight
            total = total + weight.astype(F32)
        summed = jnp.zeros((YB, EXT), F32)
        for term in split3(total):
            summed = summed + tn(term, ones)
        column.append(summed)
    return column


def near_kernel(s0_ref, s1_ref, s2_ref, s3_ref, shift_ref, inv_ref, count_ref, acc_ref, dense_ref):
    parts = (s0_ref, s1_ref, s2_ref, s3_ref)
    slots = [
        jnp.concatenate([ref[t].astype(F32) for ref in parts], axis=0) for t in range(NTRANS)
    ]
    column = dense_rows(range(XN), slots, inv_ref, count_ref, dense_ref)
    for block in range(XN):
        acc_ref[block * YB : (block + 1) * YB, K2:] = column[block]
    for block in range(K2 // BLOCK):
        span = slice(block * BLOCK, (block + 1) * BLOCK)
        acc_ref[:, span] = tn(dense_ref[...], shift_ref[:, span])


def far_kernel(blocks, slot_ref, shift_ref, inv_ref, count_ref, acc_ref, *refs):
    outs = refs[:-1]
    dense_ref = refs[-1]
    slots = [slot_ref[:, t].reshape(HALF, SLOTS).astype(F32) for t in range(NTRANS)]
    column = dense_rows(blocks, slots, inv_ref, count_ref, dense_ref)
    lane = lanes((YB, EXT))
    for place, block in enumerate(blocks):
        total = acc_ref[block * YB : (block + 1) * YB, K2:] + column[place]
        outs[place][:, K2:] = pack2(total, lane).astype(outs[place].dtype)
    for part in range(K2 // BLOCK):
        span = slice(part * BLOCK, (part + 1) * BLOCK)
        sums = tn(dense_ref[...], shift_ref[:, span])
        for place, block in enumerate(blocks):
            done = acc_ref[block * YB : (block + 1) * YB, span]
            done = done + sums[place * YB : (place + 1) * YB, :]
            outs[place][:, span] = done.astype(outs[place].dtype)


def merge_kernel(own_ref, one_ref, two_ref, three_ref, *outs):
    lane = lanes((OD, EXT))
    for b in range(YN):
        rows = slice(b * OD, (b + 1) * OD)
        block = own_ref[rows, :]
        for other in (one_ref, two_ref, three_ref):
            block = block + other[rows, :].astype(F32)
        total = jnp.sum(block[:, K2:], axis=1, keepdims=True)
        outs[b][:, :K2] = block[:, :K2].astype(outs[b].dtype)
        outs[b][:, K2:] = pack2(total, lane).astype(outs[b].dtype)


def final_kernel(own_ref, one_ref, two_ref, three_ref, sum_ref, total_ref):
    block = own_ref[...]
    for other in (one_ref, two_ref, three_ref):
        block = block + other[...].astype(F32)
    sum_ref[:, 0, :] = block[:, :KS]
    sum_ref[:, 1, :] = block[:, KS:K2]
    ones = jnp.ones((8, EXT), BF)
    row = jnp.zeros((8, OD), F32)
    for term in split3(block[:, K2:]):
        row = row + nt(ones, term)
    total_ref[...] = row[0:1]


def shape(dims, dtype):
    return jax.ShapeDtypeStruct(dims, dtype)


def dom_core():
    return [(d, d ^ 1) for d in range(DOM)]


def along_z(value, step):
    return lax.ppermute(value, "dom", [(d, (d + 2 * step) % DOM) for d in range(DOM)])


def turn(step, first):
    pairs = []
    for d in range(DOM):
        for y in range(YN):
            for x in range(XN):
                if (d % 2 == 0) == first:
                    owner = y * XN + (x + step) % XN
                else:
                    owner = ((y + step) % YN) * XN + x
                pairs.append((d * OWNERS + y * XN + x, d * OWNERS + owner))
    return pairs


ORDER = (2, 1, 3)
BOTH = ("dom", "orient")


def along_first(value, step):
    return lax.ppermute(value, BOTH, turn(step, True))


def along_second(value, step):
    return lax.ppermute(value, BOTH, turn(step, False))


def cost(flops, moved):
    return pl.CostEstimate(flops=flops, bytes_accessed=moved, transcendentals=0)


def inside(kernel, arguments, out_shape, name, flops=0, scratch=(), mib=16):
    single = not isinstance(out_shape, list)
    return pl.pallas_call(
        kernel,
        in_specs=[INSIDE] * len(arguments),
        out_specs=INSIDE if single else [INSIDE] * len(out_shape),
        out_shape=out_shape,
        scratch_shapes=list(scratch),
        compiler_params=params(mib),
        cost_estimate=cost(flops, 2**20),
        name=name,
    )(*arguments)


def score_half(rc, images, lines, cosine, sine):
    part = shape((NTRANS, PART, SLOTS), F32)
    return inside(
        lambda *refs: scores_kernel(rc, *refs),
        [*images, *lines, cosine, sine],
        [shape((NTRANS * HALF, K2), BF)]
        + ([part] * ZN if rc == 0 else [shape((ZN, NTRANS, PART, SLOTS), F32)]),
        "scores",
        flops=2 * NTRANS * HALF * K2 * YN * YB,
        scratch=[pltpu.VMEM((YN * YB, K2), BF)],
    )


def prepare(references, noise_weight, shifts, images, ids, mask):
    codes = pltpu.VMEM((PART, CAP, OWNERS), jnp.int32)
    arguments = (
        references,
        noise_weight.reshape(1, K),
        shifts.T,
        images,
        jnp.swapaxes(ids, 1, 2),
        jnp.swapaxes(mask, 1, 2),
    )
    return pl.pallas_call(
        prepare_kernel,
        in_specs=[pl.BlockSpec(memory_space=pltpu.HBM)] * len(arguments),
        out_specs=[INSIDE] * 6,
        out_shape=[shape((OD, KE), BF)]
        + [shape((ZN, PART, KE), BF)] * 2
        + [shape((PART, SLOTS), jnp.int32)]
        + [shape((NTRANS, KS), F32)] * 2,
        scratch_shapes=[
            pltpu.VMEM((OD, 2, KS), BF),
            pltpu.VMEM((1, KS), F32),
            pltpu.SMEM((2, NTRANS), jnp.int32),
            pltpu.VMEM((PART, 2, K), BF),
            codes,
            codes,
            pltpu.SemaphoreType.DMA((6,)),
        ],
        compiler_params=params(8),
        name="prepare",
    )(*[pltpu.with_memory_space_constraint(value, pltpu.HBM) for value in arguments])


def shards(images, references, noise_weight, candidate_ids, candidate_mask, shifts):
    scaled, near, far, code, cosine, sine = prepare(
        references, noise_weight, shifts, images, candidate_ids, candidate_mask
    )
    far = lax.ppermute(far, "dom", dom_core())
    blocks = {0: scaled}
    for step in ORDER:
        blocks[(-step) % XN] = along_first(scaled, step)
    pairs = inside(pair_kernel, [near, far], [shape((2, PART, KE), BF)] * ZN, "pair_images")
    pieces = {0: pairs[0]}
    for step in ORDER:
        pieces[(-step) % ZN] = along_z(pairs[step], step)
    pieces = [pieces[rz] for rz in range(ZN)]
    line = inside(
        gather_kernel, [blocks[b] for b in range(XN)], shape((YB, KE), BF), "gather"
    )
    lines = {0: line}
    for step in ORDER:
        lines[(-step) % YN] = along_second(line, step)
    lines = [lines[y] for y in range(YN)]
    far_shift, far_slots = score_half(1, pieces, lines, cosine, sine)
    partner = lax.ppermute(far_slots, "dom", dom_core())
    near_shift, *near_slots = score_half(0, pieces, lines, cosine, sine)
    part = shape((NTRANS, PART, SLOTS), F32)
    slots = inside(add_kernel, [partner, *near_slots], [part] * ZN, "add_cores")
    arrived = [along_z(slots[step], step) for step in ORDER]
    near_inv, near_count, far_inv, far_count = inside(
        slots_kernel,
        pieces,
        [shape((HALF, YN * YB), jnp.int32), shape((HALF, YN * YB), F32)] * 2,
        "slot_map",
    )
    code, near_inv, near_count, far_inv, far_count = lax.optimization_barrier(
        (code, near_inv, near_count, far_inv, far_count)
    )
    weights, evidence = inside(
        posterior_kernel,
        [slots[0], *arrived, code],
        [shape((NTRANS, PART, SLOTS), BF), shape((PART, SLOTS), F32)],
        "posterior",
    )

    mine = {0: weights}
    for step in ORDER:
        mine[(-step) % ZN] = along_z(weights, step)
    near_weights = [mine[rz] for rz in range(ZN)]
    stacked = inside(
        stack_kernel, near_weights, shape((ZN, NTRANS, PART, SLOTS), BF), "stack_weights"
    )
    far_weights = lax.ppermute(stacked, "dom", dom_core())
    flops = 2 * NTRANS * HALF * K2 * YN * YB
    acc = inside(
        near_kernel,
        [*near_weights, near_shift, near_inv, near_count],
        shape((YN * YB, KE), F32),
        "near_sums",
        flops=flops,
        scratch=[pltpu.VMEM((NTRANS * HALF, YN * YB), BF)],
    )
    outs = {}
    for targets in ((2, 1), (3,), (0,)):
        pair = inside(
            lambda *refs, targets=targets: far_kernel(targets, *refs),
            [far_weights, far_shift, far_inv, far_count, acc],
            [shape((YB, KE), F32 if target == 0 else BF) for target in targets],
            "far_sums",
            flops=flops * len(targets) // XN,
            scratch=[pltpu.VMEM((NTRANS * HALF, len(targets) * YB), BF)],
        )
        outs.update(zip(targets, pair))
    rows = inside(
        merge_kernel,
        [outs[0]] + [along_first(outs[step], step) for step in ORDER],
        [shape((OD, KE), F32 if b == 0 else BF) for b in range(YN)],
        "merge_first",
    )
    image_sums, totals = inside(
        final_kernel,
        [rows[0]] + [along_second(rows[step], step) for step in ORDER],
        [shape((OD, 2, KS), F32), shape((1, OD), F32)],
        "merge_second",
    )
    return image_sums, totals.reshape(OD), evidence[:, 0]


def solution(mesh):
    return jax.shard_map(
        shards,
        mesh=mesh,
        in_specs=(
            P(("dom", "orient"), None, None),
            P("orient", None, None),
            P(),
            P(("dom", "orient"), None, None),
            P(("dom", "orient"), None, None),
            P(),
        ),
        out_specs=(P("orient", None, "dom"), P("orient"), P(("dom", "orient"))),
        check_vma=False,
    )
```

```python
import math

import jax
import jax.numpy as jnp
from jax import lax
from jax.experimental import pallas as pl
from jax.experimental.pallas import tpu as pltpu
from jax.sharding import PartitionSpec as P

GRID = 64
K = 4096
BOX = 400
NTRANS = 25
CAP = 8
ZN = 4
YN = 4
XN = 4
DOM = 8
PART = 16
KS = K // DOM
K2 = 2 * KS
EXT = 128
KE = K2 + EXT
SLOTS = 128
OD = 32
YB = XN * OD
TC = 5
STEPS = NTRANS // TC
HALF = ZN * PART
ROWS = TC * HALF
BF = jnp.bfloat16
F32 = jnp.float32
BLOCK = 256
OWNERS = YN * XN
INSIDE = pl.BlockSpec(memory_space=pltpu.VMEM)


def nt(left, right):
    return lax.dot_general(
        left, right, (((1,), (1,)), ((), ())), preferred_element_type=F32
    )


def tn(left, right):
    return lax.dot_general(
        left, right, (((0,), (0,)), ((), ())), preferred_element_type=F32
    )


def params(mib=16):
    return pltpu.CompilerParams(vmem_limit_bytes=mib * 1024 * 1024)


def lanes(shape):
    return lax.broadcasted_iota(jnp.int32, shape, len(shape) - 1)


def split3(value):
    high = value.astype(BF)
    rest = value - high.astype(F32)
    mid = rest.astype(BF)
    low = (rest - mid.astype(F32)).astype(BF)
    return high, mid, low


def pack2(total, lane):
    high = total.astype(BF).astype(F32)
    return jnp.where(lane == 0, high, jnp.where(lane == 1, total - high, 0.0))


def phase_tables(d, shifts_ref, cos_ref, sin_ref):
    coefficient = d * KS + lanes((1, KS))
    row_freq = coefficient // GRID - GRID // 2
    col_freq = coefficient % GRID - GRID // 2
    turns = jnp.concatenate(
        [row_freq * shifts_ref[0, t] + col_freq * shifts_ref[1, t] for t in range(NTRANS)], axis=0
    )
    angles = turns.astype(F32) * (2.0 * math.pi / BOX)
    cos_ref[...] = jnp.cos(angles)
    sin_ref[...] = jnp.sin(angles)


def prepare_kernel(
    refs_hbm, noise_hbm, shifts_hbm, images_hbm, ids_hbm, mask_hbm,
    scaled_ref, o0_ref, o1_ref, o2_ref, o3_ref, code_ref, cos_ref, sin_ref,
    refs_ref, noise_ref, shifts_ref, images_ref, ids_ref, mask_ref, sems,
):
    d = lax.axis_index("dom")
    z = d // 2
    core = lax.rem(d, 2)
    span = pl.ds(pl.multiple_of(d * KS, KS), KS)
    copies = [
        pltpu.make_async_copy(refs_hbm.at[:, :, span], refs_ref, sems.at[0]),
        pltpu.make_async_copy(noise_hbm.at[:, span], noise_ref, sems.at[1]),
        pltpu.make_async_copy(shifts_hbm, shifts_ref, sems.at[2]),
        pltpu.make_async_copy(images_hbm, images_ref, sems.at[3]),
        pltpu.make_async_copy(ids_hbm, ids_ref, sems.at[4]),
        pltpu.make_async_copy(mask_hbm, mask_ref, sems.at[5]),
    ]
    for copy in copies:
        copy.start()
    copies[2].wait()
    phase_tables(d, shifts_ref, cos_ref, sin_ref)
    for copy in copies[:2]:
        copy.wait()
    noise = noise_ref[...]
    total = jnp.zeros((OD, 1), F32)
    for part in range(2):
        values = refs_ref[:, part, :].astype(F32)
        scaled_ref[:, part * KS : (part + 1) * KS] = (values * noise).astype(BF)
        total = total + jnp.sum(noise * values * values, axis=1, keepdims=True)
    high, mid, low = [term.astype(F32) for term in split3(0.5 * total)]
    lane = lanes((OD, EXT))
    norms = jnp.where(lane == 0, high, jnp.where(lane == 1, mid, jnp.where(lane == 2, low, 0.0)))
    scaled_ref[:, K2:] = norms.astype(BF)
    for copy in copies[3:]:
        copy.wait()
    marked = jnp.where(mask_ref[...] > 0, ids_ref[...] + OD, ids_ref[...])
    flat = jnp.concatenate([marked[:, c, :] for c in range(CAP)], axis=1)
    code_ref[...] = flat
    code = flat.astype(F32).astype(BF)
    for rz, out_ref in enumerate((o0_ref, o1_ref, o2_ref, o3_ref)):
        for rc in range(2):
            slot = lax.rem(z + rz, ZN) * 2 + (core if rc == 0 else 1 - core)
            span = pl.ds(pl.multiple_of(slot * KS, KS), KS)
            for part in range(2):
                out_ref[rc, :, part * KS : (part + 1) * KS] = images_ref[:, part, span]
            out_ref[rc, :, K2:] = code


def gather_kernel(b0_ref, b1_ref, b2_ref, b3_ref, line_ref):
    for place, ref in enumerate((b0_ref, b1_ref, b2_ref, b3_ref)):
        line_ref[place * OD : (place + 1) * OD, :] = ref[...]


def split_kernel(p0_ref, p1_ref, p2_ref, p3_ref, near_ref, far_ref):
    for place, ref in enumerate((p0_ref, p1_ref, p2_ref, p3_ref)):
        near_ref[place] = ref[0]
        far_ref[place] = ref[1]


def stack_kernel(s0_ref, s1_ref, s2_ref, s3_ref, out_ref):
    for place, ref in enumerate((s0_ref, s1_ref, s2_ref, s3_ref)):
        out_ref[place] = ref[...]


def first_axis(core, along_x, along_y):
    return jnp.where(core == 0, along_x, along_y)


def slots_kernel(near_ref, far_ref, near_inv, near_count, far_inv, far_count):
    core = lax.rem(lax.axis_index("dom"), 2)
    j = lax.axis_index("orient")
    lane = lanes((HALF, SLOTS))
    groups = ((near_ref, near_inv, near_count), (far_ref, far_inv, far_count))
    for images_ref, inv_ref, count_ref in groups:
        code = images_ref[:, :, K2:].reshape(HALF, EXT).astype(F32).astype(jnp.int32)
        for block in range(XN):
            along_x = first_axis(core, block, lane // OD)
            along_y = first_axis(core, lane // OD, block)
            owner = ((j // XN + along_y) % YN) * XN + (lax.rem(j, XN) + along_x) % XN
            inverse = jnp.zeros((HALF, YB), jnp.int32)
            count = jnp.zeros((HALF, YB), F32)
            for c in range(CAP):
                where_slot = c * OWNERS + owner
                seen = jnp.take_along_axis(code, where_slot, axis=1, mode="promise_in_bounds")
                match = seen == (lane % OD + OD)
                count = count + jnp.where(match, 1.0, 0.0)
                inverse = jnp.where(match, where_slot, inverse)
            inv_ref[:, block * YB : (block + 1) * YB] = inverse
            count_ref[:, block * YB : (block + 1) * YB] = count


def scores_kernel(rc, *refs):
    images_ref = refs[0]
    refs = refs[1:]
    refs_in = refs[:YN]
    cos_ref, sin_ref, shift_ref = refs[YN : YN + 3]
    outs = refs[YN + 3 : -1]
    weight_ref = refs[-1]
    core = lax.rem(lax.axis_index("dom"), 2)
    j = lax.axis_index("orient")
    lane8 = lanes((8, EXT))
    ones = jnp.where(lane8 < 3, 1.0, 0.0).astype(BF)
    norms = []
    for y in range(YN):
        weight_ref[y * YB : (y + 1) * YB, :] = refs_in[y][:, :K2]
        norms.append(nt(ones, refs_in[y][:, K2:])[0:1])
    lane = lanes((HALF, SLOTS))
    values = images_ref[...].reshape(HALF, KE).astype(F32)
    code = values[:, K2:].astype(jnp.int32)
    owner = lane % OWNERS
    along_y = (owner // XN + YN - j // XN) % YN
    along_x = (owner % XN + XN - lax.rem(j, XN)) % XN
    line = first_axis(core, along_y, along_x)
    index = first_axis(core, along_x, along_y) * OD + code % OD
    real = values[:, :KS]
    imag = values[:, KS:K2]
    for step in range(STEPS):
        base = step * ROWS
        for t in range(TC):
            row = step * TC + t
            cosine = cos_ref[row : row + 1, :]
            sine = sin_ref[row : row + 1, :]
            rows = slice(base + t * HALF, base + (t + 1) * HALF)
            shift_ref[rows, :KS] = (real * cosine - imag * sine).astype(BF)
            shift_ref[rows, KS:] = (real * sine + imag * cosine).astype(BF)
        scores = nt(shift_ref[base : base + ROWS, :], weight_ref[...])
        for t in range(TC):
            found = jnp.zeros((HALF, SLOTS), F32)
            for y in range(YN):
                span = slice(y * YB, (y + 1) * YB)
                block = scores[t * HALF : (t + 1) * HALF, span] - norms[y]
                picked = jnp.take_along_axis(block, index, axis=1, mode="promise_in_bounds")
                found = jnp.where(line == y, picked, found)
            if rc == 0:
                for rz in range(ZN):
                    outs[rz][step * TC + t] = found[rz * PART : (rz + 1) * PART, :]
            else:
                outs[0][:, step * TC + t] = found.reshape(ZN, PART, SLOTS)


def add_kernel(partner_ref, *refs):
    for rz in range(ZN):
        refs[ZN + rz][...] = refs[rz][...] + partner_ref[rz]


def posterior_kernel(own_ref, one_ref, two_ref, three_ref, code_ref, weight_ref, evidence_ref):
    valid = code_ref[...] >= OD
    scores = own_ref[...] + one_ref[...] + two_ref[...] + three_ref[...]
    masked = jnp.where(valid[None], scores, -1e30)
    highest = jnp.max(jnp.max(masked, axis=0), axis=1, keepdims=True)
    terms = jnp.where(valid[None], jnp.exp(scores - highest[None]), 0.0)
    summed = jnp.sum(jnp.sum(terms, axis=0), axis=1, keepdims=True)
    evidence = highest + jnp.log(summed)
    weights = jnp.where(valid[None], jnp.exp(scores - evidence[None]), 0.0)
    weight_ref[...] = weights.astype(BF)
    evidence_ref[...] = jnp.broadcast_to(evidence, evidence_ref.shape)


def dense_rows(blocks, slots, inv_ref, count_ref, dense_ref):
    column = []
    ones = jnp.ones((HALF, EXT), BF)
    for place, block in enumerate(blocks):
        span = slice(block * YB, (block + 1) * YB)
        inverse = inv_ref[:, span]
        count = count_ref[:, span]
        total = jnp.zeros((HALF, YB), F32)
        for t in range(NTRANS):
            picked = jnp.take_along_axis(slots[t], inverse, axis=1, mode="promise_in_bounds")
            weight = (picked * count).astype(BF)
            dense_ref[t * HALF : (t + 1) * HALF, place * YB : (place + 1) * YB] = weight
            total = total + weight.astype(F32)
        summed = jnp.zeros((YB, EXT), F32)
        for term in split3(total):
            summed = summed + tn(term, ones)
        column.append(summed)
    return column


def sums_kernel(blocks, groups, before, *refs):
    dense = refs[len(refs) - groups :]
    outs = refs[len(refs) - groups - (len(blocks) if before or groups == 2 else 1) :]
    columns, shifts = [], []
    for group in range(groups):
        stack_ref, shift_ref, inv_ref, count_ref = refs[4 * group : 4 * group + 4]
        slots = [stack_ref[:, t].reshape(HALF, SLOTS).astype(F32) for t in range(NTRANS)]
        columns.append(dense_rows(blocks, slots, inv_ref, count_ref, dense[group]))
        shifts.append(shift_ref)
    acc_ref = refs[4 * groups] if before else None
    finished = before or groups == 2
    lane = lanes((YB, EXT))
    for place in range(len(blocks)):
        rows = slice(place * YB, (place + 1) * YB)
        total = sum(column[place] for column in columns)
        if before:
            total = total + acc_ref[rows, K2:]
        if finished:
            outs[place][:, K2:] = pack2(total, lane).astype(outs[place].dtype)
        else:
            outs[0][rows, K2:] = total
    for part in range(K2 // BLOCK):
        span = slice(part * BLOCK, (part + 1) * BLOCK)
        sums = tn(dense[0][...], shifts[0][:, span])
        for group in range(1, groups):
            sums = sums + tn(dense[group][...], shifts[group][:, span])
        if before:
            sums = sums + acc_ref[:, span]
        if finished:
            for place in range(len(blocks)):
                rows = slice(place * YB, (place + 1) * YB)
                outs[place][:, span] = sums[rows, :].astype(outs[place].dtype)
        else:
            outs[0][:, span] = sums


def merge_kernel(own_ref, one_ref, two_ref, three_ref, *outs):
    lane = lanes((OD, EXT))
    for b in range(YN):
        rows = slice(b * OD, (b + 1) * OD)
        block = own_ref[rows, :]
        for other in (one_ref, two_ref, three_ref):
            block = block + other[rows, :].astype(F32)
        total = jnp.sum(block[:, K2:], axis=1, keepdims=True)
        outs[b][:, :K2] = block[:, :K2].astype(outs[b].dtype)
        outs[b][:, K2:] = pack2(total, lane).astype(outs[b].dtype)


def final_kernel(own_ref, one_ref, two_ref, three_ref, sum_ref, total_ref):
    block = own_ref[...]
    for other in (one_ref, two_ref, three_ref):
        block = block + other[...].astype(F32)
    sum_ref[:, 0, :] = block[:, :KS]
    sum_ref[:, 1, :] = block[:, KS:K2]
    ones = jnp.ones((8, EXT), BF)
    row = jnp.zeros((8, OD), F32)
    for term in split3(block[:, K2:]):
        row = row + nt(ones, term)
    total_ref[...] = row[0:1]


def shape(dims, dtype):
    return jax.ShapeDtypeStruct(dims, dtype)


def dom_core():
    return [(d, d ^ 1) for d in range(DOM)]


def along_z(value, step):
    return lax.ppermute(value, "dom", [(d, (d + 2 * step) % DOM) for d in range(DOM)])


def turn(step, first):
    pairs = []
    for d in range(DOM):
        for y in range(YN):
            for x in range(XN):
                if (d % 2 == 0) == first:
                    owner = y * XN + (x + step) % XN
                else:
                    owner = ((y + step) % YN) * XN + x
                pairs.append((d * OWNERS + y * XN + x, d * OWNERS + owner))
    return pairs


ORDER = (2, 1, 3)
BOTH = ("dom", "orient")


def along_first(value, step):
    return lax.ppermute(value, BOTH, turn(step, True))


def along_second(value, step):
    return lax.ppermute(value, BOTH, turn(step, False))


def cost(flops, moved):
    return pl.CostEstimate(flops=flops, bytes_accessed=moved, transcendentals=0)


def inside(kernel, arguments, out_shape, name, flops=0, scratch=(), mib=16):
    single = not isinstance(out_shape, list)
    return pl.pallas_call(
        kernel,
        in_specs=[INSIDE] * len(arguments),
        out_specs=INSIDE if single else [INSIDE] * len(out_shape),
        out_shape=out_shape,
        scratch_shapes=list(scratch),
        compiler_params=params(mib),
        cost_estimate=cost(flops, 2**20),
        name=name,
    )(*arguments)


def score_half(rc, images, lines, cosine, sine):
    part = shape((NTRANS, PART, SLOTS), F32)
    return inside(
        lambda *refs: scores_kernel(rc, *refs),
        [images, *lines, cosine, sine],
        [shape((NTRANS * HALF, K2), BF)]
        + ([part] * ZN if rc == 0 else [shape((ZN, NTRANS, PART, SLOTS), F32)]),
        "scores",
        flops=2 * NTRANS * HALF * K2 * YN * YB,
        scratch=[pltpu.VMEM((YN * YB, K2), BF)],
    )


def weighted_sums(blocks, groups, acc, name):
    arguments = [array for group in groups for array in group]
    if acc is not None:
        arguments.append(acc)
    if acc is not None or len(groups) == 2:
        out = [shape((YB, KE), F32 if block == 0 else BF) for block in blocks]
    else:
        out = [shape((len(blocks) * YB, KE), F32)]
    return inside(
        lambda *refs: sums_kernel(blocks, len(groups), acc is not None, *refs),
        arguments,
        out,
        name,
        flops=len(groups) * len(blocks) * 2 * NTRANS * HALF * K2 * YB,
        scratch=[pltpu.VMEM((NTRANS * HALF, len(blocks) * YB), BF)] * len(groups),
    )


def prepare(references, noise_weight, shifts, images, ids, mask):
    codes = pltpu.VMEM((PART, CAP, OWNERS), jnp.int32)
    arguments = (
        references,
        noise_weight.reshape(1, K),
        shifts.T,
        images,
        jnp.swapaxes(ids, 1, 2),
        jnp.swapaxes(mask, 1, 2),
    )
    return pl.pallas_call(
        prepare_kernel,
        in_specs=[pl.BlockSpec(memory_space=pltpu.HBM)] * len(arguments),
        out_specs=[INSIDE] * 8,
        out_shape=[shape((OD, KE), BF)]
        + [shape((2, PART, KE), BF)] * ZN
        + [shape((PART, SLOTS), jnp.int32)]
        + [shape((NTRANS, KS), F32)] * 2,
        scratch_shapes=[
            pltpu.VMEM((OD, 2, KS), BF),
            pltpu.VMEM((1, KS), F32),
            pltpu.SMEM((2, NTRANS), jnp.int32),
            pltpu.VMEM((PART, 2, K), BF),
            codes,
            codes,
            pltpu.SemaphoreType.DMA((6,)),
        ],
        compiler_params=params(8),
        name="prepare",
    )(*[pltpu.with_memory_space_constraint(value, pltpu.HBM) for value in arguments])


def shards(images, references, noise_weight, candidate_ids, candidate_mask, shifts):
    scaled, *cuts, code, cosine, sine = prepare(
        references, noise_weight, shifts, images, candidate_ids, candidate_mask
    )
    blocks = {0: scaled}
    for step in ORDER:
        blocks[(-step) % XN] = along_first(scaled, step)
    pieces = {0: cuts[0]}
    for step in ORDER:
        pieces[(-step) % ZN] = along_z(cuts[step], step)
    blocks[0], pieces[ZN - 1] = lax.optimization_barrier((blocks[0], pieces[ZN - 1]))
    line = inside(
        gather_kernel, [blocks[b] for b in range(XN)], shape((YB, KE), BF), "gather"
    )
    lines = {0: line}
    for step in ORDER:
        lines[(-step) % YN] = along_second(line, step)
    lines = [lines[y] for y in range(YN)]
    near, far = inside(
        split_kernel,
        [pieces[rz] for rz in range(ZN)],
        [shape((ZN, PART, KE), BF)] * 2,
        "split_images",
    )
    far = lax.ppermute(far, "dom", dom_core())
    far_shift, far_slots = score_half(1, far, lines, cosine, sine)
    partner = lax.ppermute(far_slots, "dom", dom_core())
    near_shift, *near_slots = score_half(0, near, lines, cosine, sine)
    part = shape((NTRANS, PART, SLOTS), F32)
    slots = inside(add_kernel, [partner, *near_slots], [part] * ZN, "add_cores")
    arrived = [along_z(slots[step], step) for step in ORDER]
    near_inv, near_count, far_inv, far_count = inside(
        slots_kernel,
        [near, far],
        [shape((HALF, YN * YB), jnp.int32), shape((HALF, YN * YB), F32)] * 2,
        "slot_map",
    )
    code, near_inv, near_count, far_inv, far_count = lax.optimization_barrier(
        (code, near_inv, near_count, far_inv, far_count)
    )
    weights, evidence = inside(
        posterior_kernel,
        [slots[0], *arrived, code],
        [shape((NTRANS, PART, SLOTS), BF), shape((PART, SLOTS), F32)],
        "posterior",
    )

    mine = {0: weights}
    for step in ORDER:
        mine[(-step) % ZN] = along_z(weights, step)
    near_weights = inside(
        stack_kernel,
        [mine[rz] for rz in range(ZN)],
        shape((ZN, NTRANS, PART, SLOTS), BF),
        "stack_weights",
    )
    far_weights = lax.ppermute(near_weights, "dom", dom_core())
    near_group = (near_weights, near_shift, near_inv, near_count)
    far_group = (far_weights, far_shift, far_inv, far_count)
    outs = {}
    (acc,) = weighted_sums((2, 1), [near_group], None, "near_sums")
    outs[2], outs[1] = weighted_sums((2, 1), [far_group], acc, "far_sums")
    for target in (3, 0):
        (outs[target],) = weighted_sums((target,), [near_group, far_group], None, "both_sums")
    rows = inside(
        merge_kernel,
        [outs[0]] + [along_first(outs[step], step) for step in ORDER],
        [shape((OD, KE), F32 if b == 0 else BF) for b in range(YN)],
        "merge_first",
    )
    image_sums, totals = inside(
        final_kernel,
        [rows[0]] + [along_second(rows[step], step) for step in ORDER],
        [shape((OD, 2, KS), F32), shape((1, OD), F32)],
        "merge_second",
    )
    return image_sums, totals.reshape(OD), evidence[:, 0]


def solution(mesh):
    return jax.shard_map(
        shards,
        mesh=mesh,
        in_specs=(
            P(("dom", "orient"), None, None),
            P("orient", None, None),
            P(),
            P(("dom", "orient"), None, None),
            P(("dom", "orient"), None, None),
            P(),
        ),
        out_specs=(P("orient", None, "dom"), P("orient"), P(("dom", "orient"))),
        check_vma=False,
    )
```

```python
import math

import jax
import jax.numpy as jnp
from jax import lax
from jax.experimental import pallas as pl
from jax.experimental.pallas import tpu as pltpu
from jax.sharding import PartitionSpec as P

GRID = 64
K = 4096
BOX = 400
NTRANS = 25
CAP = 8
ZN = 4
YN = 4
XN = 4
DOM = 8
PART = 16
KS = K // DOM
K2 = 2 * KS
EXT = 128
KE = K2 + EXT
SLOTS = 128
OD = 32
YB = XN * OD
TC = 5
STEPS = NTRANS // TC
HALF = ZN * PART
ROWS = TC * HALF
BF = jnp.bfloat16
F32 = jnp.float32
BLOCK = 256
TOP = 32767.0
STEP = 64.0
OWNERS = YN * XN
INSIDE = pl.BlockSpec(memory_space=pltpu.VMEM)


def nt(left, right):
    return lax.dot_general(
        left, right, (((1,), (1,)), ((), ())), preferred_element_type=F32
    )


def tn(left, right):
    return lax.dot_general(
        left, right, (((0,), (0,)), ((), ())), preferred_element_type=F32
    )


def params(mib=16):
    return pltpu.CompilerParams(vmem_limit_bytes=mib * 1024 * 1024)


def lanes(shape):
    return lax.broadcasted_iota(jnp.int32, shape, len(shape) - 1)


def split3(value):
    high = value.astype(BF)
    rest = value - high.astype(F32)
    mid = rest.astype(BF)
    low = (rest - mid.astype(F32)).astype(BF)
    return high, mid, low


def pack2(total, lane):
    high = total.astype(BF).astype(F32)
    return jnp.where(lane == 0, high, jnp.where(lane == 1, total - high, 0.0))


def phase_tables(d, shifts_ref, cos_ref, sin_ref):
    coefficient = d * KS + lanes((1, KS))
    row_freq = coefficient // GRID - GRID // 2
    col_freq = coefficient % GRID - GRID // 2
    turns = jnp.concatenate(
        [row_freq * shifts_ref[0, t] + col_freq * shifts_ref[1, t] for t in range(NTRANS)], axis=0
    )
    angles = turns.astype(F32) * (2.0 * math.pi / BOX)
    cos_ref[...] = jnp.cos(angles)
    sin_ref[...] = jnp.sin(angles)


def prepare_kernel(
    refs_hbm, noise_hbm, shifts_hbm, images_hbm, ids_hbm, mask_hbm,
    scaled_ref, near_ref, far_ref, code_ref, cos_ref, sin_ref,
    refs_ref, noise_ref, shifts_ref, images_ref, ids_ref, mask_ref, sems,
):
    d = lax.axis_index("dom")
    z = d // 2
    core = lax.rem(d, 2)
    span = pl.ds(pl.multiple_of(d * KS, KS), KS)
    copies = [
        pltpu.make_async_copy(refs_hbm.at[:, :, span], refs_ref, sems.at[0]),
        pltpu.make_async_copy(noise_hbm.at[:, span], noise_ref, sems.at[1]),
        pltpu.make_async_copy(shifts_hbm, shifts_ref, sems.at[2]),
        pltpu.make_async_copy(images_hbm, images_ref, sems.at[3]),
        pltpu.make_async_copy(ids_hbm, ids_ref, sems.at[4]),
        pltpu.make_async_copy(mask_hbm, mask_ref, sems.at[5]),
    ]
    for copy in copies:
        copy.start()
    copies[2].wait()
    phase_tables(d, shifts_ref, cos_ref, sin_ref)
    for copy in copies[:2]:
        copy.wait()
    noise = noise_ref[...]
    total = jnp.zeros((OD, 1), F32)
    for part in range(2):
        values = refs_ref[:, part, :].astype(F32)
        scaled_ref[:, part * KS : (part + 1) * KS] = (values * noise).astype(BF)
        total = total + jnp.sum(noise * values * values, axis=1, keepdims=True)
    high, mid, low = [term.astype(F32) for term in split3(0.5 * total)]
    lane = lanes((OD, EXT))
    norms = jnp.where(lane == 0, high, jnp.where(lane == 1, mid, jnp.where(lane == 2, low, 0.0)))
    scaled_ref[:, K2:] = norms.astype(BF)
    for copy in copies[3:]:
        copy.wait()
    marked = jnp.where(mask_ref[...] > 0, ids_ref[...] + OD, ids_ref[...])
    flat = jnp.concatenate([marked[:, c, :] for c in range(CAP)], axis=1)
    code_ref[...] = flat
    code = flat.astype(F32).astype(BF)
    for rz in range(ZN):
        for rc, out_ref in enumerate((near_ref, far_ref)):
            slot = lax.rem(z + rz, ZN) * 2 + (core if rc == 0 else 1 - core)
            span = pl.ds(pl.multiple_of(slot * KS, KS), KS)
            for part in range(2):
                out_ref[rz, :, part * KS : (part + 1) * KS] = images_ref[:, part, span]
            out_ref[rz, :, K2:] = code


def gather_kernel(b0_ref, b1_ref, b2_ref, b3_ref, line_ref):
    for place, ref in enumerate((b0_ref, b1_ref, b2_ref, b3_ref)):
        line_ref[place * OD : (place + 1) * OD, :] = ref[...]


def pair_kernel(near_ref, far_ref, *outs):
    for place, ref in enumerate(outs):
        ref[0] = near_ref[place]
        ref[1] = far_ref[place]


def stack_kernel(s0_ref, s1_ref, s2_ref, s3_ref, out_ref):
    for place, ref in enumerate((s0_ref, s1_ref, s2_ref, s3_ref)):
        out_ref[place] = ref[...]


def first_axis(core, along_x, along_y):
    return jnp.where(core == 0, along_x, along_y)


def slots_kernel(p0_ref, p1_ref, p2_ref, p3_ref, near_inv, near_count, far_inv, far_count):
    core = lax.rem(lax.axis_index("dom"), 2)
    j = lax.axis_index("orient")
    lane = lanes((HALF, SLOTS))
    pieces = (p0_ref, p1_ref, p2_ref, p3_ref)
    for rc, (inv_ref, count_ref) in enumerate(((near_inv, near_count), (far_inv, far_count))):
        code = jnp.concatenate([ref[rc, :, K2:].astype(F32) for ref in pieces], axis=0)
        code = code.astype(jnp.int32)
        for block in range(XN):
            along_x = first_axis(core, block, lane // OD)
            along_y = first_axis(core, lane // OD, block)
            owner = ((j // XN + along_y) % YN) * XN + (lax.rem(j, XN) + along_x) % XN
            inverse = jnp.zeros((HALF, YB), jnp.int32)
            count = jnp.zeros((HALF, YB), F32)
            for c in range(CAP):
                where_slot = c * OWNERS + owner
                seen = jnp.take_along_axis(code, where_slot, axis=1, mode="promise_in_bounds")
                match = seen == (lane % OD + OD)
                count = count + jnp.where(match, 1.0, 0.0)
                inverse = jnp.where(match, where_slot, inverse)
            inv_ref[:, block * YB : (block + 1) * YB] = inverse
            count_ref[:, block * YB : (block + 1) * YB] = count


def scores_kernel(rc, *refs):
    images = [ref[rc] for ref in refs[:ZN]]
    refs = refs[ZN:]
    refs_in = refs[:YN]
    cos_ref, sin_ref, shift_ref = refs[YN : YN + 3]
    outs = refs[YN + 3 : -1]
    weight_ref = refs[-1]
    core = lax.rem(lax.axis_index("dom"), 2)
    j = lax.axis_index("orient")
    lane8 = lanes((8, EXT))
    ones = jnp.where(lane8 < 3, 1.0, 0.0).astype(BF)
    norms = []
    for y in range(YN):
        weight_ref[y * YB : (y + 1) * YB, :] = refs_in[y][:, :K2]
        norms.append(nt(ones, refs_in[y][:, K2:])[0:1])
    lane = lanes((HALF, SLOTS))
    values = jnp.concatenate([part.astype(F32) for part in images], axis=0)
    code = values[:, K2:].astype(jnp.int32)
    owner = lane % OWNERS
    along_y = (owner // XN + YN - j // XN) % YN
    along_x = (owner % XN + XN - lax.rem(j, XN)) % XN
    line = first_axis(core, along_y, along_x)
    index = first_axis(core, along_x, along_y) * OD + code % OD
    real = values[:, :KS]
    imag = values[:, KS:K2]
    for step in range(STEPS):
        base = step * ROWS
        for t in range(TC):
            row = step * TC + t
            cosine = cos_ref[row : row + 1, :]
            sine = sin_ref[row : row + 1, :]
            rows = slice(base + t * HALF, base + (t + 1) * HALF)
            shift_ref[rows, :KS] = (real * cosine - imag * sine).astype(BF)
            shift_ref[rows, KS:] = (real * sine + imag * cosine).astype(BF)
        scores = nt(shift_ref[base : base + ROWS, :], weight_ref[...])
        for t in range(TC):
            found = jnp.zeros((HALF, SLOTS), F32)
            for y in range(YN):
                span = slice(y * YB, (y + 1) * YB)
                block = scores[t * HALF : (t + 1) * HALF, span] - norms[y]
                picked = jnp.take_along_axis(block, index, axis=1, mode="promise_in_bounds")
                found = jnp.where(line == y, picked, found)
            if rc == 0:
                for rz in range(ZN):
                    outs[rz][step * TC + t] = found[rz * PART : (rz + 1) * PART, :]
            else:
                outs[0][:, step * TC + t] = found.reshape(ZN, PART, SLOTS)


def scale_of(code):
    return jnp.exp(code * (math.log(2.0) / STEP)) * (1.0 / TOP)


def code_of(size):
    return jnp.floor(jnp.log(jnp.maximum(size, 1e-30)) * (STEP / math.log(2.0))) + 2.0


def add_kernel(partner_ref, *refs):
    lane = lanes((PART, SLOTS))
    refs[2 * ZN][...] = refs[0][...] + partner_ref[0]
    for rz in range(1, ZN):
        scores = refs[rz][...] + partner_ref[rz]
        valid = refs[ZN + rz][0, :, K2:].astype(F32) >= OD
        top = jnp.max(jnp.where(valid[None], scores, -1e30), axis=0)
        top = jnp.max(top, axis=1, keepdims=True)
        bottom = jnp.min(jnp.where(valid[None], scores, 1e30), axis=0)
        bottom = jnp.min(bottom, axis=1, keepdims=True)
        centre_code = code_of(jnp.maximum(jnp.abs(top), jnp.abs(bottom)))
        centre = jnp.floor(0.5 * (top + bottom) / scale_of(centre_code) + 0.5)
        offset = centre * scale_of(centre_code)
        size_code = code_of(jnp.maximum(top - offset, offset - bottom))
        whole = jnp.floor((scores - offset[None]) / scale_of(size_code)[None] + 0.5)
        whole = jnp.clip(whole, -TOP, TOP)
        row = jnp.where(lane == 0, centre_code, jnp.where(lane == 1, centre, size_code))
        out_ref = refs[2 * ZN + rz]
        out_ref[:NTRANS] = whole.astype(jnp.int32).astype(jnp.int16)
        out_ref[NTRANS] = row.astype(jnp.int32).astype(jnp.int16)


def sent_scores(ref):
    values = ref[...].astype(jnp.int32).astype(F32)
    row = values[NTRANS]
    offset = row[:, 1:2] * scale_of(row[:, 0:1])
    return values[:NTRANS] * scale_of(row[:, 2:3])[None] + offset[None]


def posterior_kernel(own_ref, one_ref, two_ref, three_ref, code_ref, weight_ref, evidence_ref):
    valid = code_ref[...] >= OD
    scores = own_ref[...]
    for ref in (one_ref, two_ref, three_ref):
        scores = scores + sent_scores(ref)
    masked = jnp.where(valid[None], scores, -1e30)
    highest = jnp.max(jnp.max(masked, axis=0), axis=1, keepdims=True)
    terms = jnp.where(valid[None], jnp.exp(scores - highest[None]), 0.0)
    summed = jnp.sum(jnp.sum(terms, axis=0), axis=1, keepdims=True)
    evidence = highest + jnp.log(summed)
    weights = jnp.where(valid[None], jnp.exp(scores - evidence[None]), 0.0)
    weight_ref[...] = weights.astype(BF)
    evidence_ref[...] = jnp.broadcast_to(evidence, evidence_ref.shape)


def dense_rows(blocks, slots, inv_ref, count_ref, dense_ref):
    column = []
    ones = jnp.ones((HALF, EXT), BF)
    for place, block in enumerate(blocks):
        span = slice(block * YB, (block + 1) * YB)
        inverse = inv_ref[:, span]
        count = count_ref[:, span]
        total = jnp.zeros((HALF, YB), F32)
        for t in range(NTRANS):
            picked = jnp.take_along_axis(slots[t], inverse, axis=1, mode="promise_in_bounds")
            weight = (picked * count).astype(BF)
            dense_ref[t * HALF : (t + 1) * HALF, place * YB : (place + 1) * YB] = weight
            total = total + weight.astype(F32)
        summed = jnp.zeros((YB, EXT), F32)
        for term in split3(total):
            summed = summed + tn(term, ones)
        column.append(summed)
    return column


def sums_kernel(blocks, groups, before, *refs):
    dense = refs[len(refs) - groups :]
    outs = refs[len(refs) - groups - (len(blocks) if before or groups == 2 else 1) :]
    columns, shifts = [], []
    for group in range(groups):
        stack_ref, shift_ref, inv_ref, count_ref = refs[4 * group : 4 * group + 4]
        slots = [stack_ref[:, t].reshape(HALF, SLOTS).astype(F32) for t in range(NTRANS)]
        columns.append(dense_rows(blocks, slots, inv_ref, count_ref, dense[group]))
        shifts.append(shift_ref)
    acc_ref = refs[4 * groups] if before else None
    finished = before or groups == 2
    lane = lanes((YB, EXT))
    for place in range(len(blocks)):
        rows = slice(place * YB, (place + 1) * YB)
        total = sum(column[place] for column in columns)
        if before:
            total = total + acc_ref[rows, K2:]
        if finished:
            outs[place][:, K2:] = pack2(total, lane).astype(outs[place].dtype)
        else:
            outs[0][rows, K2:] = total
    for part in range(K2 // BLOCK):
        span = slice(part * BLOCK, (part + 1) * BLOCK)
        sums = tn(dense[0][...], shifts[0][:, span])
        for group in range(1, groups):
            sums = sums + tn(dense[group][...], shifts[group][:, span])
        if before:
            sums = sums + acc_ref[:, span]
        if finished:
            for place in range(len(blocks)):
                rows = slice(place * YB, (place + 1) * YB)
                outs[place][:, span] = sums[rows, :].astype(outs[place].dtype)
        else:
            outs[0][:, span] = sums


def merge_kernel(own_ref, one_ref, two_ref, three_ref, *outs):
    lane = lanes((OD, EXT))
    for b in range(YN):
        rows = slice(b * OD, (b + 1) * OD)
        block = own_ref[rows, :]
        for other in (one_ref, two_ref, three_ref):
            block = block + other[rows, :].astype(F32)
        total = jnp.sum(block[:, K2:], axis=1, keepdims=True)
        outs[b][:, :K2] = block[:, :K2].astype(outs[b].dtype)
        outs[b][:, K2:] = pack2(total, lane).astype(outs[b].dtype)


def final_kernel(own_ref, one_ref, two_ref, three_ref, sum_ref, total_ref):
    block = own_ref[...]
    for other in (one_ref, two_ref, three_ref):
        block = block + other[...].astype(F32)
    sum_ref[:, 0, :] = block[:, :KS]
    sum_ref[:, 1, :] = block[:, KS:K2]
    ones = jnp.ones((8, EXT), BF)
    row = jnp.zeros((8, OD), F32)
    for term in split3(block[:, K2:]):
        row = row + nt(ones, term)
    total_ref[...] = row[0:1]


def shape(dims, dtype):
    return jax.ShapeDtypeStruct(dims, dtype)


def dom_core():
    return [(d, d ^ 1) for d in range(DOM)]


def along_z(value, step):
    return lax.ppermute(value, "dom", [(d, (d + 2 * step) % DOM) for d in range(DOM)])


def turn(step, first):
    pairs = []
    for d in range(DOM):
        for y in range(YN):
            for x in range(XN):
                if (d % 2 == 0) == first:
                    owner = y * XN + (x + step) % XN
                else:
                    owner = ((y + step) % YN) * XN + x
                pairs.append((d * OWNERS + y * XN + x, d * OWNERS + owner))
    return pairs


ORDER = (2, 1, 3)
BOTH = ("dom", "orient")


def along_first(value, step):
    return lax.ppermute(value, BOTH, turn(step, True))


def along_second(value, step):
    return lax.ppermute(value, BOTH, turn(step, False))


def cost(flops, moved):
    return pl.CostEstimate(flops=flops, bytes_accessed=moved, transcendentals=0)


def inside(kernel, arguments, out_shape, name, flops=0, scratch=(), mib=16):
    single = not isinstance(out_shape, list)
    return pl.pallas_call(
        kernel,
        in_specs=[INSIDE] * len(arguments),
        out_specs=INSIDE if single else [INSIDE] * len(out_shape),
        out_shape=out_shape,
        scratch_shapes=list(scratch),
        compiler_params=params(mib),
        cost_estimate=cost(flops, 2**20),
        name=name,
    )(*arguments)


def score_half(rc, images, lines, cosine, sine):
    part = shape((NTRANS, PART, SLOTS), F32)
    return inside(
        lambda *refs: scores_kernel(rc, *refs),
        [*images, *lines, cosine, sine],
        [shape((NTRANS * HALF, K2), BF)]
        + ([part] * ZN if rc == 0 else [shape((ZN, NTRANS, PART, SLOTS), F32)]),
        "scores",
        flops=2 * NTRANS * HALF * K2 * YN * YB,
        scratch=[pltpu.VMEM((YN * YB, K2), BF)],
    )


def weighted_sums(blocks, groups, acc, name):
    arguments = [array for group in groups for array in group]
    if acc is not None:
        arguments.append(acc)
    if acc is not None or len(groups) == 2:
        out = [shape((YB, KE), F32 if block == 0 else BF) for block in blocks]
    else:
        out = [shape((len(blocks) * YB, KE), F32)]
    return inside(
        lambda *refs: sums_kernel(blocks, len(groups), acc is not None, *refs),
        arguments,
        out,
        name,
        flops=len(groups) * len(blocks) * 2 * NTRANS * HALF * K2 * YB,
        scratch=[pltpu.VMEM((NTRANS * HALF, len(blocks) * YB), BF)] * len(groups),
    )


def prepare(references, noise_weight, shifts, images, ids, mask):
    codes = pltpu.VMEM((PART, CAP, OWNERS), jnp.int32)
    arguments = (
        references,
        noise_weight.reshape(1, K),
        shifts.T,
        images,
        jnp.swapaxes(ids, 1, 2),
        jnp.swapaxes(mask, 1, 2),
    )
    return pl.pallas_call(
        prepare_kernel,
        in_specs=[pl.BlockSpec(memory_space=pltpu.HBM)] * len(arguments),
        out_specs=[INSIDE] * 6,
        out_shape=[shape((OD, KE), BF)]
        + [shape((ZN, PART, KE), BF)] * 2
        + [shape((PART, SLOTS), jnp.int32)]
        + [shape((NTRANS, KS), F32)] * 2,
        scratch_shapes=[
            pltpu.VMEM((OD, 2, KS), BF),
            pltpu.VMEM((1, KS), F32),
            pltpu.SMEM((2, NTRANS), jnp.int32),
            pltpu.VMEM((PART, 2, K), BF),
            codes,
            codes,
            pltpu.SemaphoreType.DMA((6,)),
        ],
        compiler_params=params(8),
        name="prepare",
    )(*[pltpu.with_memory_space_constraint(value, pltpu.HBM) for value in arguments])


def shards(images, references, noise_weight, candidate_ids, candidate_mask, shifts):
    scaled, near, far, code, cosine, sine = prepare(
        references, noise_weight, shifts, images, candidate_ids, candidate_mask
    )
    far = lax.ppermute(far, "dom", dom_core())
    blocks = {0: scaled}
    for step in ORDER:
        blocks[(-step) % XN] = along_first(scaled, step)
    pairs = inside(pair_kernel, [near, far], [shape((2, PART, KE), BF)] * ZN, "pair_images")
    pieces = {0: pairs[0]}
    for step in ORDER:
        pieces[(-step) % ZN] = along_z(pairs[step], step)
    pieces = [pieces[rz] for rz in range(ZN)]
    line = inside(
        gather_kernel, [blocks[b] for b in range(XN)], shape((YB, KE), BF), "gather"
    )
    lines = {0: line}
    for step in ORDER:
        lines[(-step) % YN] = along_second(line, step)
    lines = [lines[y] for y in range(YN)]
    far_shift, far_slots = score_half(1, pieces, lines, cosine, sine)
    partner = lax.ppermute(far_slots, "dom", dom_core())
    near_shift, *near_slots = score_half(0, pieces, lines, cosine, sine)
    part = shape((NTRANS, PART, SLOTS), F32)
    sent = shape((NTRANS + 1, PART, SLOTS), jnp.int16)
    slots = inside(add_kernel, [partner, *near_slots, *pieces], [part] + [sent] * (ZN - 1), "add_cores")
    arrived = [along_z(slots[step], step) for step in ORDER]
    near_inv, near_count, far_inv, far_count = inside(
        slots_kernel,
        pieces,
        [shape((HALF, YN * YB), jnp.int32), shape((HALF, YN * YB), F32)] * 2,
        "slot_map",
    )
    code, near_inv, near_count, far_inv, far_count = lax.optimization_barrier(
        (code, near_inv, near_count, far_inv, far_count)
    )
    weights, evidence = inside(
        posterior_kernel,
        [slots[0], *arrived, code],
        [shape((NTRANS, PART, SLOTS), BF), shape((PART, SLOTS), F32)],
        "posterior",
    )

    mine = {0: weights}
    for step in ORDER:
        mine[(-step) % ZN] = along_z(weights, step)
    near_weights = inside(
        stack_kernel,
        [mine[rz] for rz in range(ZN)],
        shape((ZN, NTRANS, PART, SLOTS), BF),
        "stack_weights",
    )
    far_weights = lax.ppermute(near_weights, "dom", dom_core())
    near_group = (near_weights, near_shift, near_inv, near_count)
    far_group = (far_weights, far_shift, far_inv, far_count)
    outs = {}
    (acc,) = weighted_sums((2, 1), [near_group], None, "near_sums")
    outs[2], outs[1] = weighted_sums((2, 1), [far_group], acc, "far_sums")
    for target in (3, 0):
        (outs[target],) = weighted_sums((target,), [near_group, far_group], None, "both_sums")
    rows = inside(
        merge_kernel,
        [outs[0]] + [along_first(outs[step], step) for step in ORDER],
        [shape((OD, KE), F32 if b == 0 else BF) for b in range(YN)],
        "merge_first",
    )
    image_sums, totals = inside(
        final_kernel,
        [rows[0]] + [along_second(rows[step], step) for step in ORDER],
        [shape((OD, 2, KS), F32), shape((1, OD), F32)],
        "merge_second",
    )
    return image_sums, totals.reshape(OD), evidence[:, 0]


def solution(mesh):
    return jax.shard_map(
        shards,
        mesh=mesh,
        in_specs=(
            P(("dom", "orient"), None, None),
            P("orient", None, None),
            P(),
            P(("dom", "orient"), None, None),
            P(("dom", "orient"), None, None),
            P(),
        ),
        out_specs=(P("orient", None, "dom"), P("orient"), P(("dom", "orient"))),
        check_vma=False,
    )
```

```python
import math

import jax
import jax.numpy as jnp
from jax import lax
from jax.experimental import pallas as pl
from jax.experimental.pallas import tpu as pltpu
from jax.sharding import PartitionSpec as P

GRID = 64
K = 4096
BOX = 400
NTRANS = 25
CAP = 8
ZN = 4
YN = 4
XN = 4
DOM = 8
PART = 16
KS = K // DOM
K2 = 2 * KS
EXT = 128
KE = K2 + EXT
SLOTS = 128
OD = 32
YB = XN * OD
HALF = ZN * PART
PIECE = NTRANS * PART
BF = jnp.bfloat16
F32 = jnp.float32
BLOCK = 256
TOP = 32767.0
STEP = 64.0
OWNERS = YN * XN
INSIDE = pl.BlockSpec(memory_space=pltpu.VMEM)


def nt(left, right):
    return lax.dot_general(
        left, right, (((1,), (1,)), ((), ())), preferred_element_type=F32
    )


def tn(left, right):
    return lax.dot_general(
        left, right, (((0,), (0,)), ((), ())), preferred_element_type=F32
    )


def params(mib=16):
    return pltpu.CompilerParams(vmem_limit_bytes=mib * 1024 * 1024)


def lanes(shape):
    return lax.broadcasted_iota(jnp.int32, shape, len(shape) - 1)


def split3(value):
    high = value.astype(BF)
    rest = value - high.astype(F32)
    mid = rest.astype(BF)
    low = (rest - mid.astype(F32)).astype(BF)
    return high, mid, low


def pack2(total, lane):
    high = total.astype(BF).astype(F32)
    return jnp.where(lane == 0, high, jnp.where(lane == 1, total - high, 0.0))


def phase_tables(d, shifts_ref, cos_ref, sin_ref):
    coefficient = d * KS + lanes((1, KS))
    row_freq = coefficient // GRID - GRID // 2
    col_freq = coefficient % GRID - GRID // 2
    turns = jnp.concatenate(
        [row_freq * shifts_ref[0, t] + col_freq * shifts_ref[1, t] for t in range(NTRANS)], axis=0
    )
    angles = turns.astype(F32) * (2.0 * math.pi / BOX)
    cos_ref[...] = jnp.cos(angles)
    sin_ref[...] = jnp.sin(angles)


def prepare_kernel(
    refs_hbm, noise_hbm, shifts_hbm, images_hbm, ids_hbm, mask_hbm,
    scaled_ref, near_ref, far_ref, code_ref, cos_ref, sin_ref,
    refs_ref, noise_ref, shifts_ref, images_ref, ids_ref, mask_ref, sems,
):
    d = lax.axis_index("dom")
    z = d // 2
    core = lax.rem(d, 2)
    span = pl.ds(pl.multiple_of(d * KS, KS), KS)
    copies = [
        pltpu.make_async_copy(refs_hbm.at[:, :, span], refs_ref, sems.at[0]),
        pltpu.make_async_copy(noise_hbm.at[:, span], noise_ref, sems.at[1]),
        pltpu.make_async_copy(shifts_hbm, shifts_ref, sems.at[2]),
        pltpu.make_async_copy(images_hbm, images_ref, sems.at[3]),
        pltpu.make_async_copy(ids_hbm, ids_ref, sems.at[4]),
        pltpu.make_async_copy(mask_hbm, mask_ref, sems.at[5]),
    ]
    for copy in copies:
        copy.start()
    copies[2].wait()
    phase_tables(d, shifts_ref, cos_ref, sin_ref)
    for copy in copies[:2]:
        copy.wait()
    noise = noise_ref[...]
    total = jnp.zeros((OD, 1), F32)
    for part in range(2):
        values = refs_ref[:, part, :].astype(F32)
        scaled_ref[:, part * KS : (part + 1) * KS] = (values * noise).astype(BF)
        total = total + jnp.sum(noise * values * values, axis=1, keepdims=True)
    high, mid, low = [term.astype(F32) for term in split3(0.5 * total)]
    lane = lanes((OD, EXT))
    norms = jnp.where(lane == 0, high, jnp.where(lane == 1, mid, jnp.where(lane == 2, low, 0.0)))
    scaled_ref[:, K2:] = norms.astype(BF)
    for copy in copies[3:]:
        copy.wait()
    marked = jnp.where(mask_ref[...] > 0, ids_ref[...] + OD, ids_ref[...])
    flat = jnp.concatenate([marked[:, c, :] for c in range(CAP)], axis=1)
    code_ref[...] = flat
    code = flat.astype(F32).astype(BF)
    for rz in range(ZN):
        for rc, out_ref in enumerate((near_ref, far_ref)):
            slot = lax.rem(z + rz, ZN) * 2 + (core if rc == 0 else 1 - core)
            span = pl.ds(pl.multiple_of(slot * KS, KS), KS)
            for part in range(2):
                out_ref[rz, :, part * KS : (part + 1) * KS] = images_ref[:, part, span]
            out_ref[rz, :, K2:] = code


def gather_kernel(b0_ref, b1_ref, b2_ref, b3_ref, line_ref):
    for place, ref in enumerate((b0_ref, b1_ref, b2_ref, b3_ref)):
        line_ref[place * OD : (place + 1) * OD, :] = ref[...]


def pair_kernel(near_ref, far_ref, *outs):
    for place, ref in enumerate(outs):
        ref[0] = near_ref[place]
        ref[1] = far_ref[place]


def stack_kernel(acc_ref, s1_ref, s2_ref, s3_ref, out_ref):
    del acc_ref
    for place, ref in enumerate((s1_ref, s2_ref, s3_ref)):
        out_ref[place] = ref[...]


def first_axis(core, along_x, along_y):
    return jnp.where(core == 0, along_x, along_y)


def slots_kernel(p0_ref, p1_ref, p2_ref, p3_ref, near_inv, near_count, far_inv, far_count):
    core = lax.rem(lax.axis_index("dom"), 2)
    j = lax.axis_index("orient")
    lane = lanes((HALF, SLOTS))
    pieces = (p0_ref, p1_ref, p2_ref, p3_ref)
    for rc, (inv_ref, count_ref) in enumerate(((near_inv, near_count), (far_inv, far_count))):
        code = jnp.concatenate([ref[rc, :, K2:].astype(F32) for ref in pieces], axis=0)
        code = code.astype(jnp.int32)
        for block in range(XN):
            along_x = first_axis(core, block, lane // OD)
            along_y = first_axis(core, lane // OD, block)
            owner = ((j // XN + along_y) % YN) * XN + (lax.rem(j, XN) + along_x) % XN
            inverse = jnp.zeros((HALF, YB), jnp.int32)
            count = jnp.zeros((HALF, YB), F32)
            for c in range(CAP):
                where_slot = c * OWNERS + owner
                seen = jnp.take_along_axis(code, where_slot, axis=1, mode="promise_in_bounds")
                match = seen == (lane % OD + OD)
                count = count + jnp.where(match, 1.0, 0.0)
                inverse = jnp.where(match, where_slot, inverse)
            inv_ref[:, block * YB : (block + 1) * YB] = inverse
            count_ref[:, block * YB : (block + 1) * YB] = count


def scores_kernel(rc, *refs):
    images = [ref[rc] for ref in refs[:ZN]]
    refs = refs[ZN:]
    refs_in = refs[:YN]
    cos_ref, sin_ref, shift_ref = refs[YN : YN + 3]
    outs = refs[YN + 3 : -1]
    weight_ref = refs[-1]
    core = lax.rem(lax.axis_index("dom"), 2)
    j = lax.axis_index("orient")
    lane8 = lanes((8, EXT))
    ones = jnp.where(lane8 < 3, 1.0, 0.0).astype(BF)
    norms = []
    for y in range(YN):
        weight_ref[y * YB : (y + 1) * YB, :] = refs_in[y][:, :K2]
        norms.append(nt(ones, refs_in[y][:, K2:])[0:1])
    lane = lanes((HALF, SLOTS))
    values = jnp.concatenate([part.astype(F32) for part in images], axis=0)
    code = values[:, K2:].astype(jnp.int32)
    owner = lane % OWNERS
    along_y = (owner // XN + YN - j // XN) % YN
    along_x = (owner % XN + XN - lax.rem(j, XN)) % XN
    line = first_axis(core, along_y, along_x)
    index = first_axis(core, along_x, along_y) * OD + code % OD
    real = values[:, :KS]
    imag = values[:, KS:K2]
    for rz in range(ZN):
        part = slice(rz * PART, (rz + 1) * PART)
        base = rz * PIECE
        for t in range(NTRANS):
            cosine = cos_ref[t : t + 1, :]
            sine = sin_ref[t : t + 1, :]
            rows = slice(base + t * PART, base + (t + 1) * PART)
            shift_ref[rows, :KS] = (real[part] * cosine - imag[part] * sine).astype(BF)
            shift_ref[rows, KS:] = (real[part] * sine + imag[part] * cosine).astype(BF)
        scores = nt(shift_ref[base : base + PIECE, :], weight_ref[...])
        for t in range(NTRANS):
            found = jnp.zeros((PART, SLOTS), F32)
            for y in range(YN):
                span = slice(y * YB, (y + 1) * YB)
                block = scores[t * PART : (t + 1) * PART, span] - norms[y]
                picked = jnp.take_along_axis(
                    block, index[part], axis=1, mode="promise_in_bounds"
                )
                found = jnp.where(line[part] == y, picked, found)
            if rc == 0:
                outs[rz][t] = found
            else:
                outs[0][rz, t] = found


def scale_of(code):
    return jnp.exp(code * (math.log(2.0) / STEP)) * (1.0 / TOP)


def code_of(size):
    return jnp.floor(jnp.log(jnp.maximum(size, 1e-30)) * (STEP / math.log(2.0))) + 2.0


def add_kernel(partner_ref, *refs):
    lane = lanes((PART, SLOTS))
    refs[2 * ZN][...] = refs[0][...] + partner_ref[0]
    for rz in range(1, ZN):
        scores = refs[rz][...] + partner_ref[rz]
        valid = refs[ZN + rz][0, :, K2:].astype(F32) >= OD
        top = jnp.max(jnp.where(valid[None], scores, -1e30), axis=0)
        top = jnp.max(top, axis=1, keepdims=True)
        bottom = jnp.min(jnp.where(valid[None], scores, 1e30), axis=0)
        bottom = jnp.min(bottom, axis=1, keepdims=True)
        centre_code = code_of(jnp.maximum(jnp.abs(top), jnp.abs(bottom)))
        centre = jnp.floor(0.5 * (top + bottom) / scale_of(centre_code) + 0.5)
        offset = centre * scale_of(centre_code)
        size_code = code_of(jnp.maximum(top - offset, offset - bottom))
        whole = jnp.floor((scores - offset[None]) / scale_of(size_code)[None] + 0.5)
        whole = jnp.clip(whole, -TOP, TOP)
        row = jnp.where(lane == 0, centre_code, jnp.where(lane == 1, centre, size_code))
        out_ref = refs[2 * ZN + rz]
        out_ref[:NTRANS] = whole.astype(jnp.int32).astype(jnp.int16)
        out_ref[NTRANS] = row.astype(jnp.int32).astype(jnp.int16)


def sent_scores(ref):
    values = ref[...].astype(jnp.int32).astype(F32)
    row = values[NTRANS]
    offset = row[:, 1:2] * scale_of(row[:, 0:1])
    return values[:NTRANS] * scale_of(row[:, 2:3])[None] + offset[None]


def posterior_kernel(own_ref, one_ref, two_ref, three_ref, code_ref, weight_ref, evidence_ref):
    valid = code_ref[...] >= OD
    scores = own_ref[...]
    for ref in (one_ref, two_ref, three_ref):
        scores = scores + sent_scores(ref)
    masked = jnp.where(valid[None], scores, -1e30)
    highest = jnp.max(jnp.max(masked, axis=0), axis=1, keepdims=True)
    terms = jnp.where(valid[None], jnp.exp(scores - highest[None]), 0.0)
    summed = jnp.sum(jnp.sum(terms, axis=0), axis=1, keepdims=True)
    evidence = highest + jnp.log(summed)
    weights = jnp.where(valid[None], jnp.exp(scores - evidence[None]), 0.0)
    weight_ref[...] = weights.astype(BF)
    evidence_ref[...] = jnp.broadcast_to(evidence, evidence_ref.shape)


def dense_rows(blocks, stack_ref, first, inv_ref, count_ref, dense_ref):
    column = []
    ones = jnp.ones((PART, EXT), BF)
    for place, block in enumerate(blocks):
        span = slice(block * YB, (block + 1) * YB)
        columns = slice(place * YB, (place + 1) * YB)
        total = jnp.zeros((PART, YB), F32)
        for r in range(stack_ref.shape[0]):
            part = slice((first + r) * PART, (first + r + 1) * PART)
            inverse = inv_ref[part, span]
            count = count_ref[part, span]
            for t in range(NTRANS):
                slots = stack_ref[r, t].astype(F32)
                picked = jnp.take_along_axis(slots, inverse, axis=1, mode="promise_in_bounds")
                weight = (picked * count).astype(BF)
                start = r * PIECE + t * PART
                dense_ref[start : start + PART, columns] = weight
                total = total + weight.astype(F32)
        summed = jnp.zeros((YB, EXT), F32)
        for term in split3(total):
            summed = summed + tn(term, ones)
        column.append(summed)
    return column


def sums_kernel(blocks, firsts, offset, finished, *refs):
    groups = len(firsts)
    dense = refs[len(refs) - groups :]
    refs = refs[: len(refs) - groups]
    columns, shifts = [], []
    for group, first in enumerate(firsts):
        stack_ref, shift_ref, inv_ref, count_ref = refs[4 * group : 4 * group + 4]
        columns.append(dense_rows(blocks, stack_ref, first, inv_ref, count_ref, dense[group]))
        shifts.append((shift_ref, slice(first * PIECE, (first + stack_ref.shape[0]) * PIECE)))
    refs = refs[4 * groups :]
    before = offset is not None
    if before:
        acc_ref = refs[0]
        refs = refs[1:]
        held = slice(offset * YB, (offset + len(blocks)) * YB)
    lane = lanes((YB, EXT))
    for place in range(len(blocks)):
        rows = slice(place * YB, (place + 1) * YB)
        total = sum(column[place] for column in columns)
        if before:
            total = total + acc_ref[(offset + place) * YB : (offset + place + 1) * YB, K2:]
        if finished:
            refs[place][:, K2:] = pack2(total, lane).astype(refs[place].dtype)
        else:
            refs[0][rows, K2:] = total
    for part in range(K2 // BLOCK):
        span = slice(part * BLOCK, (part + 1) * BLOCK)
        sums = tn(dense[0][...], shifts[0][0][shifts[0][1], span])
        for group in range(1, groups):
            sums = sums + tn(dense[group][...], shifts[group][0][shifts[group][1], span])
        if before:
            sums = sums + acc_ref[held, span]
        if finished:
            for place in range(len(blocks)):
                rows = slice(place * YB, (place + 1) * YB)
                refs[place][:, span] = sums[rows, :].astype(refs[place].dtype)
        else:
            refs[0][:, span] = sums


def merge_kernel(own_ref, one_ref, two_ref, three_ref, *outs):
    lane = lanes((OD, EXT))
    for b in range(YN):
        rows = slice(b * OD, (b + 1) * OD)
        block = own_ref[rows, :]
        for other in (one_ref, two_ref, three_ref):
            block = block + other[rows, :].astype(F32)
        total = jnp.sum(block[:, K2:], axis=1, keepdims=True)
        outs[b][:, :K2] = block[:, :K2].astype(outs[b].dtype)
        outs[b][:, K2:] = pack2(total, lane).astype(outs[b].dtype)


def final_kernel(own_ref, one_ref, two_ref, three_ref, sum_ref, total_ref):
    block = own_ref[...]
    for other in (one_ref, two_ref, three_ref):
        block = block + other[...].astype(F32)
    sum_ref[:, 0, :] = block[:, :KS]
    sum_ref[:, 1, :] = block[:, KS:K2]
    ones = jnp.ones((8, EXT), BF)
    row = jnp.zeros((8, OD), F32)
    for term in split3(block[:, K2:]):
        row = row + nt(ones, term)
    total_ref[...] = row[0:1]


def shape(dims, dtype):
    return jax.ShapeDtypeStruct(dims, dtype)


def dom_core():
    return [(d, d ^ 1) for d in range(DOM)]


def along_z(value, step):
    return lax.ppermute(value, "dom", [(d, (d + 2 * step) % DOM) for d in range(DOM)])


def turn(step, first):
    pairs = []
    for d in range(DOM):
        for y in range(YN):
            for x in range(XN):
                if (d % 2 == 0) == first:
                    owner = y * XN + (x + step) % XN
                else:
                    owner = ((y + step) % YN) * XN + x
                pairs.append((d * OWNERS + y * XN + x, d * OWNERS + owner))
    return pairs


ORDER = (2, 1, 3)
BOTH = ("dom", "orient")


def along_first(value, step):
    return lax.ppermute(value, BOTH, turn(step, True))


def along_second(value, step):
    return lax.ppermute(value, BOTH, turn(step, False))


def cost(flops, moved):
    return pl.CostEstimate(flops=flops, bytes_accessed=moved, transcendentals=0)


def inside(kernel, arguments, out_shape, name, flops=0, scratch=(), mib=16):
    single = not isinstance(out_shape, list)
    return pl.pallas_call(
        kernel,
        in_specs=[INSIDE] * len(arguments),
        out_specs=INSIDE if single else [INSIDE] * len(out_shape),
        out_shape=out_shape,
        scratch_shapes=list(scratch),
        compiler_params=params(mib),
        cost_estimate=cost(flops, 2**20),
        name=name,
    )(*arguments)


def score_half(rc, images, lines, cosine, sine):
    part = shape((NTRANS, PART, SLOTS), F32)
    return inside(
        lambda *refs: scores_kernel(rc, *refs),
        [*images, *lines, cosine, sine],
        [shape((NTRANS * HALF, K2), BF)]
        + ([part] * ZN if rc == 0 else [shape((ZN, NTRANS, PART, SLOTS), F32)]),
        "scores",
        flops=2 * NTRANS * HALF * K2 * YN * YB,
        scratch=[pltpu.VMEM((YN * YB, K2), BF)],
    )


def weighted_sums(blocks, groups, first, acc, offset, finished, name):
    arguments = [array for group in groups for array in group]
    if acc is not None:
        arguments.append(acc)
    if finished:
        out = [shape((YB, KE), F32 if block == 0 else BF) for block in blocks]
    else:
        out = [shape((len(blocks) * YB, KE), F32)]
    rows = groups[0][0].shape[0] * PIECE
    return inside(
        lambda *refs: sums_kernel(blocks, [first] * len(groups), offset, finished, *refs),
        arguments,
        out,
        name,
        flops=len(groups) * len(blocks) * 2 * rows * K2 * YB,
        scratch=[pltpu.VMEM((rows, len(blocks) * YB), BF)] * len(groups),
    )


def prepare(references, noise_weight, shifts, images, ids, mask):
    codes = pltpu.VMEM((PART, CAP, OWNERS), jnp.int32)
    arguments = (
        references,
        noise_weight.reshape(1, K),
        shifts.T,
        images,
        jnp.swapaxes(ids, 1, 2),
        jnp.swapaxes(mask, 1, 2),
    )
    return pl.pallas_call(
        prepare_kernel,
        in_specs=[pl.BlockSpec(memory_space=pltpu.HBM)] * len(arguments),
        out_specs=[INSIDE] * 6,
        out_shape=[shape((OD, KE), BF)]
        + [shape((ZN, PART, KE), BF)] * 2
        + [shape((PART, SLOTS), jnp.int32)]
        + [shape((NTRANS, KS), F32)] * 2,
        scratch_shapes=[
            pltpu.VMEM((OD, 2, KS), BF),
            pltpu.VMEM((1, KS), F32),
            pltpu.SMEM((2, NTRANS), jnp.int32),
            pltpu.VMEM((PART, 2, K), BF),
            codes,
            codes,
            pltpu.SemaphoreType.DMA((6,)),
        ],
        compiler_params=params(8),
        name="prepare",
    )(*[pltpu.with_memory_space_constraint(value, pltpu.HBM) for value in arguments])


def shards(images, references, noise_weight, candidate_ids, candidate_mask, shifts):
    scaled, near, far, code, cosine, sine = prepare(
        references, noise_weight, shifts, images, candidate_ids, candidate_mask
    )
    far = lax.ppermute(far, "dom", dom_core())
    blocks = {0: scaled}
    for step in ORDER:
        blocks[(-step) % XN] = along_first(scaled, step)
    pairs = inside(pair_kernel, [near, far], [shape((2, PART, KE), BF)] * ZN, "pair_images")
    pieces = {0: pairs[0]}
    for step in ORDER:
        pieces[(-step) % ZN] = along_z(pairs[step], step)
    pieces = [pieces[rz] for rz in range(ZN)]
    line = inside(
        gather_kernel, [blocks[b] for b in range(XN)], shape((YB, KE), BF), "gather"
    )
    lines = {0: line}
    for step in ORDER:
        lines[(-step) % YN] = along_second(line, step)
    lines = [lines[y] for y in range(YN)]
    far_shift, far_slots = score_half(1, pieces, lines, cosine, sine)
    partner = lax.ppermute(far_slots, "dom", dom_core())
    near_shift, *near_slots = score_half(0, pieces, lines, cosine, sine)
    part = shape((NTRANS, PART, SLOTS), F32)
    sent = shape((NTRANS + 1, PART, SLOTS), jnp.int16)
    slots = inside(add_kernel, [partner, *near_slots, *pieces], [part] + [sent] * (ZN - 1), "add_cores")
    arrived = [along_z(slots[step], step) for step in ORDER]
    near_inv, near_count, far_inv, far_count = inside(
        slots_kernel,
        pieces,
        [shape((HALF, YN * YB), jnp.int32), shape((HALF, YN * YB), F32)] * 2,
        "slot_map",
    )
    code, near_inv, near_count, far_inv, far_count = lax.optimization_barrier(
        (code, near_inv, near_count, far_inv, far_count)
    )
    weights, evidence = inside(
        posterior_kernel,
        [slots[0], *arrived, code],
        [shape((NTRANS, PART, SLOTS), BF), shape((PART, SLOTS), F32)],
        "posterior",
    )

    mine = {}
    for step in ORDER:
        mine[(-step) % ZN] = along_z(weights, step)
    own = weights.reshape(1, NTRANS, PART, SLOTS)
    other = lax.ppermute(own, "dom", dom_core())
    near_maps = (near_shift, near_inv, near_count)
    far_maps = (far_shift, far_inv, far_count)
    targets = (2, 1, 3, 0)
    (acc,) = weighted_sums(
        targets, [(own, *near_maps), (other, *far_maps)], 0, None, None, False, "own_sums"
    )
    near_rest = inside(
        stack_kernel,
        [acc] + [mine[rz] for rz in range(1, ZN)],
        shape((ZN - 1, NTRANS, PART, SLOTS), BF),
        "stack_weights",
    )
    far_rest = lax.ppermute(near_rest, "dom", dom_core())
    near_group = (near_rest, *near_maps)
    far_group = (far_rest, *far_maps)
    outs = {}
    (pair,) = weighted_sums((2, 1, 3), [near_group], 1, acc, 0, False, "near_sums")
    outs[2], outs[1], outs[3] = weighted_sums((2, 1, 3), [far_group], 1, pair, 0, True, "far_sums")
    acc, outs[2] = lax.optimization_barrier((acc, outs[2]))
    for place in (3,):
        target = targets[place]
        (outs[target],) = weighted_sums(
            (target,), [near_group, far_group], 1, acc, place, True, "both_sums"
        )
    rows = inside(
        merge_kernel,
        [outs[0]] + [along_first(outs[step], step) for step in ORDER],
        [shape((OD, KE), F32 if b == 0 else BF) for b in range(YN)],
        "merge_first",
    )
    image_sums, totals = inside(
        final_kernel,
        [rows[0]] + [along_second(rows[step], step) for step in ORDER],
        [shape((OD, 2, KS), F32), shape((1, OD), F32)],
        "merge_second",
    )
    return image_sums, totals.reshape(OD), evidence[:, 0]


def solution(mesh):
    return jax.shard_map(
        shards,
        mesh=mesh,
        in_specs=(
            P(("dom", "orient"), None, None),
            P("orient", None, None),
            P(),
            P(("dom", "orient"), None, None),
            P(("dom", "orient"), None, None),
            P(),
        ),
        out_specs=(P("orient", None, "dom"), P("orient"), P(("dom", "orient"))),
        check_vma=False,
    )
```

```python
import math

import jax
import jax.numpy as jnp
from jax import lax
from jax.experimental import pallas as pl
from jax.experimental.pallas import tpu as pltpu
from jax.sharding import PartitionSpec as P

GRID = 64
K = 4096
BOX = 400
NTRANS = 25
CAP = 8
ZN = 4
YN = 4
XN = 4
DOM = 8
PART = 16
KS = K // DOM
K2 = 2 * KS
EXT = 128
KE = K2 + EXT
SLOTS = 128
OD = 32
YB = XN * OD
HALF = ZN * PART
PIECE = NTRANS * PART
BF = jnp.bfloat16
F32 = jnp.float32
BLOCK = 256
TOP = 32767.0
STEP = 64.0
OWNERS = YN * XN
INSIDE = pl.BlockSpec(memory_space=pltpu.VMEM)


def nt(left, right):
    return lax.dot_general(
        left, right, (((1,), (1,)), ((), ())), preferred_element_type=F32
    )


def tn(left, right):
    return lax.dot_general(
        left, right, (((0,), (0,)), ((), ())), preferred_element_type=F32
    )


def params(mib=16):
    return pltpu.CompilerParams(vmem_limit_bytes=mib * 1024 * 1024)


def lanes(shape):
    return lax.broadcasted_iota(jnp.int32, shape, len(shape) - 1)


def split3(value):
    high = value.astype(BF)
    rest = value - high.astype(F32)
    mid = rest.astype(BF)
    low = (rest - mid.astype(F32)).astype(BF)
    return high, mid, low


def pack2(total, lane):
    high = total.astype(BF).astype(F32)
    return jnp.where(lane == 0, high, jnp.where(lane == 1, total - high, 0.0))


def phase_tables(d, shifts_ref, cos_ref, sin_ref):
    coefficient = d * KS + lanes((1, KS))
    row_freq = coefficient // GRID - GRID // 2
    col_freq = coefficient % GRID - GRID // 2
    turns = jnp.concatenate(
        [row_freq * shifts_ref[0, t] + col_freq * shifts_ref[1, t] for t in range(NTRANS)], axis=0
    )
    angles = turns.astype(F32) * (2.0 * math.pi / BOX)
    cos_ref[...] = jnp.cos(angles)
    sin_ref[...] = jnp.sin(angles)


def scale_kernel(refs_hbm, noise_hbm, scaled_ref, refs_ref, noise_ref, sems):
    d = lax.axis_index("dom")
    span = pl.ds(pl.multiple_of(d * KS, KS), KS)
    copies = [
        pltpu.make_async_copy(refs_hbm.at[:, :, span], refs_ref, sems.at[0]),
        pltpu.make_async_copy(noise_hbm.at[:, span], noise_ref, sems.at[1]),
    ]
    for copy in copies:
        copy.start()
    for copy in copies:
        copy.wait()
    noise = noise_ref[...]
    total = jnp.zeros((OD, 1), F32)
    for part in range(2):
        values = refs_ref[:, part, :].astype(F32)
        scaled_ref[:, part * KS : (part + 1) * KS] = (values * noise).astype(BF)
        total = total + jnp.sum(noise * values * values, axis=1, keepdims=True)
    high, mid, low = [term.astype(F32) for term in split3(0.5 * total)]
    lane = lanes((OD, EXT))
    norms = jnp.where(lane == 0, high, jnp.where(lane == 1, mid, jnp.where(lane == 2, low, 0.0)))
    scaled_ref[:, K2:] = norms.astype(BF)


def prepare_kernel(
    shifts_hbm, images_hbm, ids_hbm, mask_hbm,
    near_ref, far_ref, code_ref, cos_ref, sin_ref,
    shifts_ref, images_ref, ids_ref, mask_ref, sems,
):
    d = lax.axis_index("dom")
    z = d // 2
    core = lax.rem(d, 2)
    copies = [
        pltpu.make_async_copy(shifts_hbm, shifts_ref, sems.at[0]),
        pltpu.make_async_copy(images_hbm, images_ref, sems.at[1]),
        pltpu.make_async_copy(ids_hbm, ids_ref, sems.at[2]),
        pltpu.make_async_copy(mask_hbm, mask_ref, sems.at[3]),
    ]
    for copy in copies:
        copy.start()
    copies[0].wait()
    phase_tables(d, shifts_ref, cos_ref, sin_ref)
    for copy in copies[1:]:
        copy.wait()
    marked = jnp.where(mask_ref[...] > 0, ids_ref[...] + OD, ids_ref[...])
    flat = jnp.concatenate([marked[:, c, :] for c in range(CAP)], axis=1)
    code_ref[...] = flat
    code = flat.astype(F32).astype(BF)
    for rz in range(ZN):
        for rc, out_ref in enumerate((near_ref, far_ref)):
            slot = lax.rem(z + rz, ZN) * 2 + (core if rc == 0 else 1 - core)
            span = pl.ds(pl.multiple_of(slot * KS, KS), KS)
            for part in range(2):
                out_ref[rz, :, part * KS : (part + 1) * KS] = images_ref[:, part, span]
            out_ref[rz, :, K2:] = code


def gather_kernel(b0_ref, b1_ref, b2_ref, b3_ref, line_ref):
    for place, ref in enumerate((b0_ref, b1_ref, b2_ref, b3_ref)):
        line_ref[place * OD : (place + 1) * OD, :] = ref[...]


def pair_kernel(near_ref, far_ref, *outs):
    for place, ref in enumerate(outs):
        ref[0] = near_ref[place]
        ref[1] = far_ref[place]


def stack_kernel(acc_ref, s1_ref, s2_ref, s3_ref, out_ref):
    del acc_ref
    for place, ref in enumerate((s1_ref, s2_ref, s3_ref)):
        out_ref[place] = ref[...]


def first_axis(core, along_x, along_y):
    return jnp.where(core == 0, along_x, along_y)


def slots_kernel(p0_ref, p1_ref, p2_ref, p3_ref, near_inv, near_count, far_inv, far_count):
    core = lax.rem(lax.axis_index("dom"), 2)
    j = lax.axis_index("orient")
    lane = lanes((HALF, SLOTS))
    pieces = (p0_ref, p1_ref, p2_ref, p3_ref)
    for rc, (inv_ref, count_ref) in enumerate(((near_inv, near_count), (far_inv, far_count))):
        code = jnp.concatenate([ref[rc, :, K2:].astype(F32) for ref in pieces], axis=0)
        code = code.astype(jnp.int32)
        for block in range(XN):
            along_x = first_axis(core, block, lane // OD)
            along_y = first_axis(core, lane // OD, block)
            owner = ((j // XN + along_y) % YN) * XN + (lax.rem(j, XN) + along_x) % XN
            inverse = jnp.zeros((HALF, YB), jnp.int32)
            count = jnp.zeros((HALF, YB), F32)
            for c in range(CAP):
                where_slot = c * OWNERS + owner
                seen = jnp.take_along_axis(code, where_slot, axis=1, mode="promise_in_bounds")
                match = seen == (lane % OD + OD)
                count = count + jnp.where(match, 1.0, 0.0)
                inverse = jnp.where(match, where_slot, inverse)
            inv_ref[:, block * YB : (block + 1) * YB] = inverse
            count_ref[:, block * YB : (block + 1) * YB] = count


def scores_kernel(rc, *refs):
    images = [ref[rc] for ref in refs[:ZN]]
    refs = refs[ZN:]
    refs_in = refs[:YN]
    cos_ref, sin_ref, shift_ref = refs[YN : YN + 3]
    outs = refs[YN + 3 : -1]
    weight_ref = refs[-1]
    core = lax.rem(lax.axis_index("dom"), 2)
    j = lax.axis_index("orient")
    lane8 = lanes((8, EXT))
    ones = jnp.where(lane8 < 3, 1.0, 0.0).astype(BF)
    norms = []
    for y in range(YN):
        weight_ref[y * YB : (y + 1) * YB, :] = refs_in[y][:, :K2]
        norms.append(nt(ones, refs_in[y][:, K2:])[0:1])
    lane = lanes((HALF, SLOTS))
    values = jnp.concatenate([part.astype(F32) for part in images], axis=0)
    code = values[:, K2:].astype(jnp.int32)
    owner = lane % OWNERS
    along_y = (owner // XN + YN - j // XN) % YN
    along_x = (owner % XN + XN - lax.rem(j, XN)) % XN
    line = first_axis(core, along_y, along_x)
    index = first_axis(core, along_x, along_y) * OD + code % OD
    real = values[:, :KS]
    imag = values[:, KS:K2]
    for rz in range(ZN):
        part = slice(rz * PART, (rz + 1) * PART)
        base = rz * PIECE
        for t in range(NTRANS):
            cosine = cos_ref[t : t + 1, :]
            sine = sin_ref[t : t + 1, :]
            rows = slice(base + t * PART, base + (t + 1) * PART)
            shift_ref[rows, :KS] = (real[part] * cosine - imag[part] * sine).astype(BF)
            shift_ref[rows, KS:] = (real[part] * sine + imag[part] * cosine).astype(BF)
        scores = nt(shift_ref[base : base + PIECE, :], weight_ref[...])
        for t in range(NTRANS):
            found = jnp.zeros((PART, SLOTS), F32)
            for y in range(YN):
                span = slice(y * YB, (y + 1) * YB)
                block = scores[t * PART : (t + 1) * PART, span] - norms[y]
                picked = jnp.take_along_axis(
                    block, index[part], axis=1, mode="promise_in_bounds"
                )
                found = jnp.where(line[part] == y, picked, found)
            if rc == 0:
                outs[rz][t] = found
            else:
                outs[0][rz, t] = found


def scale_of(code):
    return jnp.exp(code * (math.log(2.0) / STEP)) * (1.0 / TOP)


def code_of(size):
    return jnp.floor(jnp.log(jnp.maximum(size, 1e-30)) * (STEP / math.log(2.0))) + 2.0


def add_kernel(partner_ref, *refs):
    lane = lanes((PART, SLOTS))
    refs[2 * ZN][...] = refs[0][...] + partner_ref[0]
    for rz in range(1, ZN):
        scores = refs[rz][...] + partner_ref[rz]
        valid = refs[ZN + rz][0, :, K2:].astype(F32) >= OD
        top = jnp.max(jnp.where(valid[None], scores, -1e30), axis=0)
        top = jnp.max(top, axis=1, keepdims=True)
        bottom = jnp.min(jnp.where(valid[None], scores, 1e30), axis=0)
        bottom = jnp.min(bottom, axis=1, keepdims=True)
        centre_code = code_of(jnp.maximum(jnp.abs(top), jnp.abs(bottom)))
        centre = jnp.floor(0.5 * (top + bottom) / scale_of(centre_code) + 0.5)
        offset = centre * scale_of(centre_code)
        size_code = code_of(jnp.maximum(top - offset, offset - bottom))
        whole = jnp.floor((scores - offset[None]) / scale_of(size_code)[None] + 0.5)
        whole = jnp.clip(whole, -TOP, TOP)
        row = jnp.where(lane == 0, centre_code, jnp.where(lane == 1, centre, size_code))
        out_ref = refs[2 * ZN + rz]
        out_ref[:NTRANS] = whole.astype(jnp.int32).astype(jnp.int16)
        out_ref[NTRANS] = row.astype(jnp.int32).astype(jnp.int16)


def sent_scores(ref):
    values = ref[...].astype(jnp.int32).astype(F32)
    row = values[NTRANS]
    offset = row[:, 1:2] * scale_of(row[:, 0:1])
    return values[:NTRANS] * scale_of(row[:, 2:3])[None] + offset[None]


def posterior_kernel(own_ref, one_ref, two_ref, three_ref, code_ref, weight_ref, evidence_ref):
    valid = code_ref[...] >= OD
    scores = own_ref[...]
    for ref in (one_ref, two_ref, three_ref):
        scores = scores + sent_scores(ref)
    masked = jnp.where(valid[None], scores, -1e30)
    highest = jnp.max(jnp.max(masked, axis=0), axis=1, keepdims=True)
    terms = jnp.where(valid[None], jnp.exp(scores - highest[None]), 0.0)
    summed = jnp.sum(jnp.sum(terms, axis=0), axis=1, keepdims=True)
    evidence = highest + jnp.log(summed)
    weights = jnp.where(valid[None], jnp.exp(scores - evidence[None]), 0.0)
    weight_ref[...] = weights.astype(BF)
    evidence_ref[...] = jnp.broadcast_to(evidence, evidence_ref.shape)


def dense_rows(blocks, stack_ref, first, inv_ref, count_ref, dense_ref):
    column = []
    ones = jnp.ones((PART, EXT), BF)
    for place, block in enumerate(blocks):
        span = slice(block * YB, (block + 1) * YB)
        columns = slice(place * YB, (place + 1) * YB)
        total = jnp.zeros((PART, YB), F32)
        for r in range(stack_ref.shape[0]):
            part = slice((first + r) * PART, (first + r + 1) * PART)
            inverse = inv_ref[part, span]
            count = count_ref[part, span]
            for t in range(NTRANS):
                slots = stack_ref[r, t].astype(F32)
                picked = jnp.take_along_axis(slots, inverse, axis=1, mode="promise_in_bounds")
                weight = (picked * count).astype(BF)
                start = r * PIECE + t * PART
                dense_ref[start : start + PART, columns] = weight
                total = total + weight.astype(F32)
        summed = jnp.zeros((YB, EXT), F32)
        for term in split3(total):
            summed = summed + tn(term, ones)
        column.append(summed)
    return column


def sums_kernel(blocks, firsts, offset, finished, *refs):
    groups = len(firsts)
    dense = refs[len(refs) - groups :]
    refs = refs[: len(refs) - groups]
    columns, shifts = [], []
    for group, first in enumerate(firsts):
        stack_ref, shift_ref, inv_ref, count_ref = refs[4 * group : 4 * group + 4]
        columns.append(dense_rows(blocks, stack_ref, first, inv_ref, count_ref, dense[group]))
        shifts.append((shift_ref, slice(first * PIECE, (first + stack_ref.shape[0]) * PIECE)))
    refs = refs[4 * groups :]
    before = offset is not None
    if before:
        acc_ref = refs[0]
        refs = refs[1:]
        held = slice(offset * YB, (offset + len(blocks)) * YB)
    lane = lanes((YB, EXT))
    for place in range(len(blocks)):
        rows = slice(place * YB, (place + 1) * YB)
        total = sum(column[place] for column in columns)
        if before:
            total = total + acc_ref[(offset + place) * YB : (offset + place + 1) * YB, K2:]
        if finished:
            refs[place][:, K2:] = pack2(total, lane).astype(refs[place].dtype)
        else:
            refs[0][rows, K2:] = total
    for part in range(K2 // BLOCK):
        span = slice(part * BLOCK, (part + 1) * BLOCK)
        sums = tn(dense[0][...], shifts[0][0][shifts[0][1], span])
        for group in range(1, groups):
            sums = sums + tn(dense[group][...], shifts[group][0][shifts[group][1], span])
        if before:
            sums = sums + acc_ref[held, span]
        if finished:
            for place in range(len(blocks)):
                rows = slice(place * YB, (place + 1) * YB)
                refs[place][:, span] = sums[rows, :].astype(refs[place].dtype)
        else:
            refs[0][:, span] = sums


def merge_kernel(own_ref, one_ref, two_ref, three_ref, *outs):
    lane = lanes((OD, EXT))
    for b in range(YN):
        rows = slice(b * OD, (b + 1) * OD)
        block = own_ref[rows, :]
        for other in (one_ref, two_ref, three_ref):
            block = block + other[rows, :].astype(F32)
        total = jnp.sum(block[:, K2:], axis=1, keepdims=True)
        outs[b][:, :K2] = block[:, :K2].astype(outs[b].dtype)
        outs[b][:, K2:] = pack2(total, lane).astype(outs[b].dtype)


def final_kernel(own_ref, one_ref, two_ref, three_ref, sum_ref, total_ref):
    block = own_ref[...]
    for other in (one_ref, two_ref, three_ref):
        block = block + other[...].astype(F32)
    sum_ref[:, 0, :] = block[:, :KS]
    sum_ref[:, 1, :] = block[:, KS:K2]
    ones = jnp.ones((8, EXT), BF)
    row = jnp.zeros((8, OD), F32)
    for term in split3(block[:, K2:]):
        row = row + nt(ones, term)
    total_ref[...] = row[0:1]


def shape(dims, dtype):
    return jax.ShapeDtypeStruct(dims, dtype)


def dom_core():
    return [(d, d ^ 1) for d in range(DOM)]


def along_z(value, step):
    return lax.ppermute(value, "dom", [(d, (d + 2 * step) % DOM) for d in range(DOM)])


def turn(step, first):
    pairs = []
    for d in range(DOM):
        for y in range(YN):
            for x in range(XN):
                if (d % 2 == 0) == first:
                    owner = y * XN + (x + step) % XN
                else:
                    owner = ((y + step) % YN) * XN + x
                pairs.append((d * OWNERS + y * XN + x, d * OWNERS + owner))
    return pairs


ORDER = (2, 1, 3)
BOTH = ("dom", "orient")


def along_first(value, step):
    return lax.ppermute(value, BOTH, turn(step, True))


def along_second(value, step):
    return lax.ppermute(value, BOTH, turn(step, False))


def cost(flops, moved):
    return pl.CostEstimate(flops=flops, bytes_accessed=moved, transcendentals=0)


def inside(kernel, arguments, out_shape, name, flops=0, scratch=(), mib=16):
    single = not isinstance(out_shape, list)
    return pl.pallas_call(
        kernel,
        in_specs=[INSIDE] * len(arguments),
        out_specs=INSIDE if single else [INSIDE] * len(out_shape),
        out_shape=out_shape,
        scratch_shapes=list(scratch),
        compiler_params=params(mib),
        cost_estimate=cost(flops, 2**20),
        name=name,
    )(*arguments)


def score_half(rc, images, lines, cosine, sine):
    part = shape((NTRANS, PART, SLOTS), F32)
    return inside(
        lambda *refs: scores_kernel(rc, *refs),
        [*images, *lines, cosine, sine],
        [shape((NTRANS * HALF, K2), BF)]
        + ([part] * ZN if rc == 0 else [shape((ZN, NTRANS, PART, SLOTS), F32)]),
        "scores",
        flops=2 * NTRANS * HALF * K2 * YN * YB,
        scratch=[pltpu.VMEM((YN * YB, K2), BF)],
    )


def weighted_sums(blocks, groups, first, acc, offset, finished, name):
    arguments = [array for group in groups for array in group]
    if acc is not None:
        arguments.append(acc)
    if finished:
        out = [shape((YB, KE), F32 if block == 0 else BF) for block in blocks]
    else:
        out = [shape((len(blocks) * YB, KE), F32)]
    rows = groups[0][0].shape[0] * PIECE
    return inside(
        lambda *refs: sums_kernel(blocks, [first] * len(groups), offset, finished, *refs),
        arguments,
        out,
        name,
        flops=len(groups) * len(blocks) * 2 * rows * K2 * YB,
        scratch=[pltpu.VMEM((rows, len(blocks) * YB), BF)] * len(groups),
    )


def loader(kernel, arguments, out_shape, scratch, name):
    return pl.pallas_call(
        kernel,
        in_specs=[pl.BlockSpec(memory_space=pltpu.HBM)] * len(arguments),
        out_specs=[INSIDE] * len(out_shape),
        out_shape=out_shape,
        scratch_shapes=scratch + [pltpu.SemaphoreType.DMA((len(arguments),))],
        compiler_params=params(8),
        name=name,
    )(*[pltpu.with_memory_space_constraint(value, pltpu.HBM) for value in arguments])


def shards(images, references, noise_weight, candidate_ids, candidate_mask, shifts):
    (scaled,) = loader(
        scale_kernel,
        [references, noise_weight.reshape(1, K)],
        [shape((OD, KE), BF)],
        [pltpu.VMEM((OD, 2, KS), BF), pltpu.VMEM((1, KS), F32)],
        "scale",
    )
    codes = pltpu.VMEM((PART, CAP, OWNERS), jnp.int32)
    near, far, code, cosine, sine = loader(
        prepare_kernel,
        [
            shifts.T,
            images,
            jnp.swapaxes(candidate_ids, 1, 2),
            jnp.swapaxes(candidate_mask, 1, 2),
        ],
        [shape((ZN, PART, KE), BF)] * 2
        + [shape((PART, SLOTS), jnp.int32)]
        + [shape((NTRANS, KS), F32)] * 2,
        [pltpu.SMEM((2, NTRANS), jnp.int32), pltpu.VMEM((PART, 2, K), BF), codes, codes],
        "prepare",
    )
    far = lax.ppermute(far, "dom", dom_core())
    blocks = {0: scaled}
    for step in ORDER:
        blocks[(-step) % XN] = along_first(scaled, step)
    pairs = inside(pair_kernel, [near, far], [shape((2, PART, KE), BF)] * ZN, "pair_images")
    pieces = {0: pairs[0]}
    for step in ORDER:
        pieces[(-step) % ZN] = along_z(pairs[step], step)
    pieces = [pieces[rz] for rz in range(ZN)]
    line = inside(
        gather_kernel, [blocks[b] for b in range(XN)], shape((YB, KE), BF), "gather"
    )
    lines = {0: line}
    for step in ORDER:
        lines[(-step) % YN] = along_second(line, step)
    lines = [lines[y] for y in range(YN)]
    far_shift, far_slots = score_half(1, pieces, lines, cosine, sine)
    partner = lax.ppermute(far_slots, "dom", dom_core())
    near_shift, *near_slots = score_half(0, pieces, lines, cosine, sine)
    part = shape((NTRANS, PART, SLOTS), F32)
    sent = shape((NTRANS + 1, PART, SLOTS), jnp.int16)
    slots = inside(add_kernel, [partner, *near_slots, *pieces], [part] + [sent] * (ZN - 1), "add_cores")
    arrived = [along_z(slots[step], step) for step in ORDER]
    near_inv, near_count, far_inv, far_count = inside(
        slots_kernel,
        pieces,
        [shape((HALF, YN * YB), jnp.int32), shape((HALF, YN * YB), F32)] * 2,
        "slot_map",
    )
    code, near_inv, near_count, far_inv, far_count = lax.optimization_barrier(
        (code, near_inv, near_count, far_inv, far_count)
    )
    weights, evidence = inside(
        posterior_kernel,
        [slots[0], *arrived, code],
        [shape((NTRANS, PART, SLOTS), BF), shape((PART, SLOTS), F32)],
        "posterior",
    )

    mine = {}
    for step in ORDER:
        mine[(-step) % ZN] = along_z(weights, step)
    own = weights.reshape(1, NTRANS, PART, SLOTS)
    other = lax.ppermute(own, "dom", dom_core())
    near_maps = (near_shift, near_inv, near_count)
    far_maps = (far_shift, far_inv, far_count)
    targets = (2, 1, 3, 0)
    (acc,) = weighted_sums(
        targets, [(own, *near_maps), (other, *far_maps)], 0, None, None, False, "own_sums"
    )
    near_rest = inside(
        stack_kernel,
        [acc] + [mine[rz] for rz in range(1, ZN)],
        shape((ZN - 1, NTRANS, PART, SLOTS), BF),
        "stack_weights",
    )
    far_rest = lax.ppermute(near_rest, "dom", dom_core())
    near_group = (near_rest, *near_maps)
    far_group = (far_rest, *far_maps)
    outs = {}
    (pair,) = weighted_sums((2, 1, 3), [near_group], 1, acc, 0, False, "near_sums")
    outs[2], outs[1], outs[3] = weighted_sums((2, 1, 3), [far_group], 1, pair, 0, True, "far_sums")
    acc, outs[2] = lax.optimization_barrier((acc, outs[2]))
    for place in (3,):
        target = targets[place]
        (outs[target],) = weighted_sums(
            (target,), [near_group, far_group], 1, acc, place, True, "both_sums"
        )
    rows = inside(
        merge_kernel,
        [outs[0]] + [along_first(outs[step], step) for step in ORDER],
        [shape((OD, KE), F32 if b == 0 else BF) for b in range(YN)],
        "merge_first",
    )
    image_sums, totals = inside(
        final_kernel,
        [rows[0]] + [along_second(rows[step], step) for step in ORDER],
        [shape((OD, 2, KS), F32), shape((1, OD), F32)],
        "merge_second",
    )
    return image_sums, totals.reshape(OD), evidence[:, 0]


def solution(mesh):
    return jax.shard_map(
        shards,
        mesh=mesh,
        in_specs=(
            P(("dom", "orient"), None, None),
            P("orient", None, None),
            P(),
            P(("dom", "orient"), None, None),
            P(("dom", "orient"), None, None),
            P(),
        ),
        out_specs=(P("orient", None, "dom"), P("orient"), P(("dom", "orient"))),
        check_vma=False,
    )
```

```python
import math

import jax
import jax.numpy as jnp
from jax import lax
from jax.experimental import pallas as pl
from jax.experimental.pallas import tpu as pltpu
from jax.sharding import PartitionSpec as P

GRID = 64
K = 4096
BOX = 400
NTRANS = 25
CAP = 8
ZN = 4
YN = 4
XN = 4
DOM = 8
PART = 16
KS = K // DOM
K2 = 2 * KS
EXT = 128
KE = K2 + EXT
SLOTS = 128
OD = 32
YB = XN * OD
HALF = ZN * PART
PIECE = NTRANS * PART
BF = jnp.bfloat16
F32 = jnp.float32
BLOCK = 256
TOP = 32767.0
STEP = 64.0
OWNERS = YN * XN
INSIDE = pl.BlockSpec(memory_space=pltpu.VMEM)


def nt(left, right):
    return lax.dot_general(
        left, right, (((1,), (1,)), ((), ())), preferred_element_type=F32
    )


def tn(left, right):
    return lax.dot_general(
        left, right, (((0,), (0,)), ((), ())), preferred_element_type=F32
    )


def params(mib=16):
    return pltpu.CompilerParams(vmem_limit_bytes=mib * 1024 * 1024)


def lanes(shape):
    return lax.broadcasted_iota(jnp.int32, shape, len(shape) - 1)


def split3(value):
    high = value.astype(BF)
    rest = value - high.astype(F32)
    mid = rest.astype(BF)
    low = (rest - mid.astype(F32)).astype(BF)
    return high, mid, low


def pack2(total, lane):
    high = total.astype(BF).astype(F32)
    return jnp.where(lane == 0, high, jnp.where(lane == 1, total - high, 0.0))


def phase_tables(d, shifts_ref, cos_ref, sin_ref):
    coefficient = d * KS + lanes((1, KS))
    row_freq = coefficient // GRID - GRID // 2
    col_freq = coefficient % GRID - GRID // 2
    turns = jnp.concatenate(
        [row_freq * shifts_ref[0, t] + col_freq * shifts_ref[1, t] for t in range(NTRANS)], axis=0
    )
    angles = turns.astype(F32) * (2.0 * math.pi / BOX)
    cos_ref[...] = jnp.cos(angles)
    sin_ref[...] = jnp.sin(angles)


def scale_kernel(refs_hbm, noise_hbm, scaled_ref, refs_ref, noise_ref, sems):
    d = lax.axis_index("dom")
    span = pl.ds(pl.multiple_of(d * KS, KS), KS)
    copies = [
        pltpu.make_async_copy(refs_hbm.at[:, :, span], refs_ref, sems.at[0]),
        pltpu.make_async_copy(noise_hbm.at[:, span], noise_ref, sems.at[1]),
    ]
    for copy in copies:
        copy.start()
    for copy in copies:
        copy.wait()
    noise = noise_ref[...]
    total = jnp.zeros((OD, 1), F32)
    for part in range(2):
        values = refs_ref[:, part, :].astype(F32)
        scaled_ref[:, part * KS : (part + 1) * KS] = (values * noise).astype(BF)
        total = total + jnp.sum(noise * values * values, axis=1, keepdims=True)
    high, mid, low = [term.astype(F32) for term in split3(0.5 * total)]
    lane = lanes((OD, EXT))
    norms = jnp.where(lane == 0, high, jnp.where(lane == 1, mid, jnp.where(lane == 2, low, 0.0)))
    scaled_ref[:, K2:] = norms.astype(BF)


def prepare_kernel(
    shifts_hbm, images_hbm, ids_hbm, mask_hbm,
    near_ref, far_ref, code_ref, cos_ref, sin_ref,
    shifts_ref, images_ref, ids_ref, mask_ref, sems,
):
    d = lax.axis_index("dom")
    z = d // 2
    core = lax.rem(d, 2)
    copies = [
        pltpu.make_async_copy(shifts_hbm, shifts_ref, sems.at[0]),
        pltpu.make_async_copy(images_hbm, images_ref, sems.at[1]),
        pltpu.make_async_copy(ids_hbm, ids_ref, sems.at[2]),
        pltpu.make_async_copy(mask_hbm, mask_ref, sems.at[3]),
    ]
    for copy in copies:
        copy.start()
    copies[0].wait()
    phase_tables(d, shifts_ref, cos_ref, sin_ref)
    for copy in copies[1:]:
        copy.wait()
    marked = jnp.where(mask_ref[...] > 0, ids_ref[...] + OD, ids_ref[...])
    flat = jnp.concatenate([marked[:, c, :] for c in range(CAP)], axis=1)
    code_ref[...] = flat
    code = flat.astype(F32).astype(BF)
    for rz in range(ZN):
        for rc, out_ref in enumerate((near_ref, far_ref)):
            slot = lax.rem(z + rz, ZN) * 2 + (core if rc == 0 else 1 - core)
            span = pl.ds(pl.multiple_of(slot * KS, KS), KS)
            for part in range(2):
                out_ref[rz, :, part * KS : (part + 1) * KS] = images_ref[:, part, span]
            out_ref[rz, :, K2:] = code


def gather_kernel(b0_ref, b1_ref, b2_ref, b3_ref, line_ref):
    for place, ref in enumerate((b0_ref, b1_ref, b2_ref, b3_ref)):
        line_ref[place * OD : (place + 1) * OD, :] = ref[...]


def pair_kernel(near_ref, far_ref, *outs):
    for place, ref in enumerate(outs):
        ref[0] = near_ref[place]
        ref[1] = far_ref[place]


def stack_kernel(acc_ref, s1_ref, s2_ref, s3_ref, out_ref):
    del acc_ref
    for place, ref in enumerate((s1_ref, s2_ref, s3_ref)):
        out_ref[place] = ref[...]


def first_axis(core, along_x, along_y):
    return jnp.where(core == 0, along_x, along_y)


def slots_kernel(p0_ref, p1_ref, p2_ref, p3_ref, near_inv, near_count, far_inv, far_count):
    core = lax.rem(lax.axis_index("dom"), 2)
    j = lax.axis_index("orient")
    lane = lanes((HALF, SLOTS))
    pieces = (p0_ref, p1_ref, p2_ref, p3_ref)
    for rc, (inv_ref, count_ref) in enumerate(((near_inv, near_count), (far_inv, far_count))):
        code = jnp.concatenate([ref[rc, :, K2:].astype(F32) for ref in pieces], axis=0)
        code = code.astype(jnp.int32)
        for block in range(XN):
            along_x = first_axis(core, block, lane // OD)
            along_y = first_axis(core, lane // OD, block)
            owner = ((j // XN + along_y) % YN) * XN + (lax.rem(j, XN) + along_x) % XN
            inverse = jnp.zeros((HALF, YB), jnp.int32)
            count = jnp.zeros((HALF, YB), F32)
            for c in range(CAP):
                where_slot = c * OWNERS + owner
                seen = jnp.take_along_axis(code, where_slot, axis=1, mode="promise_in_bounds")
                match = seen == (lane % OD + OD)
                count = count + jnp.where(match, 1.0, 0.0)
                inverse = jnp.where(match, where_slot, inverse)
            inv_ref[:, block * YB : (block + 1) * YB] = inverse
            count_ref[:, block * YB : (block + 1) * YB] = count


def scores_kernel(rc, *refs):
    images = [ref[rc] for ref in refs[:ZN]]
    refs = refs[ZN:]
    refs_in = refs[:YN]
    cos_ref, sin_ref, shift_ref = refs[YN : YN + 3]
    outs = refs[YN + 3 : -1]
    weight_ref = refs[-1]
    core = lax.rem(lax.axis_index("dom"), 2)
    j = lax.axis_index("orient")
    lane8 = lanes((8, EXT))
    ones = jnp.where(lane8 < 3, 1.0, 0.0).astype(BF)
    norms = []
    for y in range(YN):
        weight_ref[y * YB : (y + 1) * YB, :] = refs_in[y][:, :K2]
        norms.append(nt(ones, refs_in[y][:, K2:])[0:1])
    lane = lanes((HALF, SLOTS))
    values = jnp.concatenate([part.astype(F32) for part in images], axis=0)
    code = values[:, K2:].astype(jnp.int32)
    owner = lane % OWNERS
    along_y = (owner // XN + YN - j // XN) % YN
    along_x = (owner % XN + XN - lax.rem(j, XN)) % XN
    line = first_axis(core, along_y, along_x)
    index = first_axis(core, along_x, along_y) * OD + code % OD
    real = values[:, :KS]
    imag = values[:, KS:K2]
    waiting = None
    for rz in range(ZN + 1):
        done = waiting
        if rz < ZN:
            part = slice(rz * PART, (rz + 1) * PART)
            base = rz * PIECE
            for t in range(NTRANS):
                cosine = cos_ref[t : t + 1, :]
                sine = sin_ref[t : t + 1, :]
                rows = slice(base + t * PART, base + (t + 1) * PART)
                shift_ref[rows, :KS] = (real[part] * cosine - imag[part] * sine).astype(BF)
                shift_ref[rows, KS:] = (real[part] * sine + imag[part] * cosine).astype(BF)
            waiting = nt(shift_ref[base : base + PIECE, :], weight_ref[...])
        if rz == 0:
            continue
        part = slice((rz - 1) * PART, rz * PART)
        for t in range(NTRANS):
            found = jnp.zeros((PART, SLOTS), F32)
            for y in range(YN):
                span = slice(y * YB, (y + 1) * YB)
                block = done[t * PART : (t + 1) * PART, span] - norms[y]
                picked = jnp.take_along_axis(
                    block, index[part], axis=1, mode="promise_in_bounds"
                )
                found = jnp.where(line[part] == y, picked, found)
            if rc == 0:
                outs[rz - 1][t] = found
            else:
                outs[0][rz - 1, t] = found


def scale_of(code):
    return jnp.exp(code * (math.log(2.0) / STEP)) * (1.0 / TOP)


def code_of(size):
    return jnp.floor(jnp.log(jnp.maximum(size, 1e-30)) * (STEP / math.log(2.0))) + 2.0


def add_kernel(partner_ref, *refs):
    lane = lanes((PART, SLOTS))
    refs[2 * ZN][...] = refs[0][...] + partner_ref[0]
    for rz in range(1, ZN):
        scores = refs[rz][...] + partner_ref[rz]
        valid = refs[ZN + rz][0, :, K2:].astype(F32) >= OD
        top = jnp.max(jnp.where(valid[None], scores, -1e30), axis=0)
        top = jnp.max(top, axis=1, keepdims=True)
        bottom = jnp.min(jnp.where(valid[None], scores, 1e30), axis=0)
        bottom = jnp.min(bottom, axis=1, keepdims=True)
        centre_code = code_of(jnp.maximum(jnp.abs(top), jnp.abs(bottom)))
        centre = jnp.floor(0.5 * (top + bottom) / scale_of(centre_code) + 0.5)
        offset = centre * scale_of(centre_code)
        size_code = code_of(jnp.maximum(top - offset, offset - bottom))
        whole = jnp.floor((scores - offset[None]) / scale_of(size_code)[None] + 0.5)
        whole = jnp.clip(whole, -TOP, TOP)
        row = jnp.where(lane == 0, centre_code, jnp.where(lane == 1, centre, size_code))
        out_ref = refs[2 * ZN + rz]
        out_ref[:NTRANS] = whole.astype(jnp.int32).astype(jnp.int16)
        out_ref[NTRANS] = row.astype(jnp.int32).astype(jnp.int16)


def sent_scores(ref):
    values = ref[...].astype(jnp.int32).astype(F32)
    row = values[NTRANS]
    offset = row[:, 1:2] * scale_of(row[:, 0:1])
    return values[:NTRANS] * scale_of(row[:, 2:3])[None] + offset[None]


def posterior_kernel(own_ref, one_ref, two_ref, three_ref, code_ref, weight_ref, evidence_ref):
    valid = code_ref[...] >= OD
    scores = own_ref[...]
    for ref in (one_ref, two_ref, three_ref):
        scores = scores + sent_scores(ref)
    masked = jnp.where(valid[None], scores, -1e30)
    highest = jnp.max(jnp.max(masked, axis=0), axis=1, keepdims=True)
    terms = jnp.where(valid[None], jnp.exp(scores - highest[None]), 0.0)
    summed = jnp.sum(jnp.sum(terms, axis=0), axis=1, keepdims=True)
    evidence = highest + jnp.log(summed)
    weights = jnp.where(valid[None], jnp.exp(scores - evidence[None]), 0.0)
    weight_ref[...] = weights.astype(BF)
    evidence_ref[...] = jnp.broadcast_to(evidence, evidence_ref.shape)


def dense_rows(blocks, stack_ref, first, inv_ref, count_ref, dense_ref):
    column = []
    ones = jnp.ones((PART, EXT), BF)
    for place, block in enumerate(blocks):
        span = slice(block * YB, (block + 1) * YB)
        columns = slice(place * YB, (place + 1) * YB)
        total = jnp.zeros((PART, YB), F32)
        for r in range(stack_ref.shape[0]):
            part = slice((first + r) * PART, (first + r + 1) * PART)
            inverse = inv_ref[part, span]
            count = count_ref[part, span]
            for t in range(NTRANS):
                slots = stack_ref[r, t].astype(F32)
                picked = jnp.take_along_axis(slots, inverse, axis=1, mode="promise_in_bounds")
                weight = (picked * count).astype(BF)
                start = r * PIECE + t * PART
                dense_ref[start : start + PART, columns] = weight
                total = total + weight.astype(F32)
        summed = jnp.zeros((YB, EXT), F32)
        for term in split3(total):
            summed = summed + tn(term, ones)
        column.append(summed)
    return column


def sums_kernel(blocks, firsts, offset, finished, *refs):
    groups = len(firsts)
    dense = refs[len(refs) - groups :]
    refs = refs[: len(refs) - groups]
    columns, shifts = [], []
    for group, first in enumerate(firsts):
        stack_ref, shift_ref, inv_ref, count_ref = refs[4 * group : 4 * group + 4]
        columns.append(dense_rows(blocks, stack_ref, first, inv_ref, count_ref, dense[group]))
        shifts.append((shift_ref, slice(first * PIECE, (first + stack_ref.shape[0]) * PIECE)))
    refs = refs[4 * groups :]
    before = offset is not None
    if before:
        acc_ref = refs[0]
        refs = refs[1:]
        held = slice(offset * YB, (offset + len(blocks)) * YB)
    lane = lanes((YB, EXT))
    for place in range(len(blocks)):
        rows = slice(place * YB, (place + 1) * YB)
        total = sum(column[place] for column in columns)
        if before:
            total = total + acc_ref[(offset + place) * YB : (offset + place + 1) * YB, K2:]
        if finished:
            refs[place][:, K2:] = pack2(total, lane).astype(refs[place].dtype)
        else:
            refs[0][rows, K2:] = total
    for part in range(K2 // BLOCK):
        span = slice(part * BLOCK, (part + 1) * BLOCK)
        sums = tn(dense[0][...], shifts[0][0][shifts[0][1], span])
        for group in range(1, groups):
            sums = sums + tn(dense[group][...], shifts[group][0][shifts[group][1], span])
        if before:
            sums = sums + acc_ref[held, span]
        if finished:
            for place in range(len(blocks)):
                rows = slice(place * YB, (place + 1) * YB)
                refs[place][:, span] = sums[rows, :].astype(refs[place].dtype)
        else:
            refs[0][:, span] = sums


def merge_kernel(own_ref, one_ref, two_ref, three_ref, *outs):
    lane = lanes((OD, EXT))
    for b in range(YN):
        rows = slice(b * OD, (b + 1) * OD)
        block = own_ref[rows, :]
        for other in (one_ref, two_ref, three_ref):
            block = block + other[rows, :].astype(F32)
        total = jnp.sum(block[:, K2:], axis=1, keepdims=True)
        outs[b][:, :K2] = block[:, :K2].astype(outs[b].dtype)
        outs[b][:, K2:] = pack2(total, lane).astype(outs[b].dtype)


def final_kernel(own_ref, one_ref, two_ref, three_ref, sum_ref, total_ref):
    block = own_ref[...]
    for other in (one_ref, two_ref, three_ref):
        block = block + other[...].astype(F32)
    sum_ref[:, 0, :] = block[:, :KS]
    sum_ref[:, 1, :] = block[:, KS:K2]
    ones = jnp.ones((8, EXT), BF)
    row = jnp.zeros((8, OD), F32)
    for term in split3(block[:, K2:]):
        row = row + nt(ones, term)
    total_ref[...] = row[0:1]


def shape(dims, dtype):
    return jax.ShapeDtypeStruct(dims, dtype)


def dom_core():
    return [(d, d ^ 1) for d in range(DOM)]


def along_z(value, step):
    return lax.ppermute(value, "dom", [(d, (d + 2 * step) % DOM) for d in range(DOM)])


def turn(step, first):
    pairs = []
    for d in range(DOM):
        for y in range(YN):
            for x in range(XN):
                if (d % 2 == 0) == first:
                    owner = y * XN + (x + step) % XN
                else:
                    owner = ((y + step) % YN) * XN + x
                pairs.append((d * OWNERS + y * XN + x, d * OWNERS + owner))
    return pairs


ORDER = (2, 1, 3)
BOTH = ("dom", "orient")


def along_first(value, step):
    return lax.ppermute(value, BOTH, turn(step, True))


def along_second(value, step):
    return lax.ppermute(value, BOTH, turn(step, False))


def cost(flops, moved):
    return pl.CostEstimate(flops=flops, bytes_accessed=moved, transcendentals=0)


def inside(kernel, arguments, out_shape, name, flops=0, scratch=(), mib=16):
    single = not isinstance(out_shape, list)
    return pl.pallas_call(
        kernel,
        in_specs=[INSIDE] * len(arguments),
        out_specs=INSIDE if single else [INSIDE] * len(out_shape),
        out_shape=out_shape,
        scratch_shapes=list(scratch),
        compiler_params=params(mib),
        cost_estimate=cost(flops, 2**20),
        name=name,
    )(*arguments)


def score_half(rc, images, lines, cosine, sine):
    part = shape((NTRANS, PART, SLOTS), F32)
    return inside(
        lambda *refs: scores_kernel(rc, *refs),
        [*images, *lines, cosine, sine],
        [shape((NTRANS * HALF, K2), BF)]
        + ([part] * ZN if rc == 0 else [shape((ZN, NTRANS, PART, SLOTS), F32)]),
        "scores",
        flops=2 * NTRANS * HALF * K2 * YN * YB,
        scratch=[pltpu.VMEM((YN * YB, K2), BF)],
    )


def weighted_sums(blocks, groups, first, acc, offset, finished, name):
    arguments = [array for group in groups for array in group]
    if acc is not None:
        arguments.append(acc)
    if finished:
        out = [shape((YB, KE), F32 if block == 0 else BF) for block in blocks]
    else:
        out = [shape((len(blocks) * YB, KE), F32)]
    rows = groups[0][0].shape[0] * PIECE
    return inside(
        lambda *refs: sums_kernel(blocks, [first] * len(groups), offset, finished, *refs),
        arguments,
        out,
        name,
        flops=len(groups) * len(blocks) * 2 * rows * K2 * YB,
        scratch=[pltpu.VMEM((rows, len(blocks) * YB), BF)] * len(groups),
    )


def loader(kernel, arguments, out_shape, scratch, name):
    return pl.pallas_call(
        kernel,
        in_specs=[pl.BlockSpec(memory_space=pltpu.HBM)] * len(arguments),
        out_specs=[INSIDE] * len(out_shape),
        out_shape=out_shape,
        scratch_shapes=scratch + [pltpu.SemaphoreType.DMA((len(arguments),))],
        compiler_params=params(8),
        name=name,
    )(*[pltpu.with_memory_space_constraint(value, pltpu.HBM) for value in arguments])


def shards(images, references, noise_weight, candidate_ids, candidate_mask, shifts):
    (scaled,) = loader(
        scale_kernel,
        [references, noise_weight.reshape(1, K)],
        [shape((OD, KE), BF)],
        [pltpu.VMEM((OD, 2, KS), BF), pltpu.VMEM((1, KS), F32)],
        "scale",
    )
    codes = pltpu.VMEM((PART, CAP, OWNERS), jnp.int32)
    near, far, code, cosine, sine = loader(
        prepare_kernel,
        [
            shifts.T,
            images,
            jnp.swapaxes(candidate_ids, 1, 2),
            jnp.swapaxes(candidate_mask, 1, 2),
        ],
        [shape((ZN, PART, KE), BF)] * 2
        + [shape((PART, SLOTS), jnp.int32)]
        + [shape((NTRANS, KS), F32)] * 2,
        [pltpu.SMEM((2, NTRANS), jnp.int32), pltpu.VMEM((PART, 2, K), BF), codes, codes],
        "prepare",
    )
    far = lax.ppermute(far, "dom", dom_core())
    blocks = {0: scaled}
    for step in ORDER:
        blocks[(-step) % XN] = along_first(scaled, step)
    pairs = inside(pair_kernel, [near, far], [shape((2, PART, KE), BF)] * ZN, "pair_images")
    pieces = {0: pairs[0]}
    for step in ORDER:
        pieces[(-step) % ZN] = along_z(pairs[step], step)
    pieces = [pieces[rz] for rz in range(ZN)]
    line = inside(
        gather_kernel, [blocks[b] for b in range(XN)], shape((YB, KE), BF), "gather"
    )
    lines = {0: line}
    for step in ORDER:
        lines[(-step) % YN] = along_second(line, step)
    lines = [lines[y] for y in range(YN)]
    far_shift, far_slots = score_half(1, pieces, lines, cosine, sine)
    partner = lax.ppermute(far_slots, "dom", dom_core())
    near_shift, *near_slots = score_half(0, pieces, lines, cosine, sine)
    part = shape((NTRANS, PART, SLOTS), F32)
    sent = shape((NTRANS + 1, PART, SLOTS), jnp.int16)
    slots = inside(add_kernel, [partner, *near_slots, *pieces], [part] + [sent] * (ZN - 1), "add_cores")
    arrived = [along_z(slots[step], step) for step in ORDER]
    near_inv, near_count, far_inv, far_count = inside(
        slots_kernel,
        pieces,
        [shape((HALF, YN * YB), jnp.int32), shape((HALF, YN * YB), F32)] * 2,
        "slot_map",
    )
    code, near_inv, near_count, far_inv, far_count = lax.optimization_barrier(
        (code, near_inv, near_count, far_inv, far_count)
    )
    weights, evidence = inside(
        posterior_kernel,
        [slots[0], *arrived, code],
        [shape((NTRANS, PART, SLOTS), BF), shape((PART, SLOTS), F32)],
        "posterior",
    )

    mine = {}
    for step in ORDER:
        mine[(-step) % ZN] = along_z(weights, step)
    own = weights.reshape(1, NTRANS, PART, SLOTS)
    other = lax.ppermute(own, "dom", dom_core())
    near_inv, evidence = lax.optimization_barrier((near_inv, evidence[:, 0]))
    near_maps = (near_shift, near_inv, near_count)
    far_maps = (far_shift, far_inv, far_count)
    targets = (2, 1, 3, 0)
    (acc,) = weighted_sums(
        targets, [(own, *near_maps), (other, *far_maps)], 0, None, None, False, "own_sums"
    )
    near_rest = inside(
        stack_kernel,
        [acc] + [mine[rz] for rz in range(1, ZN)],
        shape((ZN - 1, NTRANS, PART, SLOTS), BF),
        "stack_weights",
    )
    far_rest = lax.ppermute(near_rest, "dom", dom_core())
    near_group = (near_rest, *near_maps)
    far_group = (far_rest, *far_maps)
    outs = {}
    (pair,) = weighted_sums((2, 1, 3), [near_group], 1, acc, 0, False, "near_sums")
    outs[2], outs[1], outs[3] = weighted_sums((2, 1, 3), [far_group], 1, pair, 0, True, "far_sums")
    acc, outs[2] = lax.optimization_barrier((acc, outs[2]))
    for place in (3,):
        target = targets[place]
        (outs[target],) = weighted_sums(
            (target,), [near_group, far_group], 1, acc, place, True, "both_sums"
        )
    rows = inside(
        merge_kernel,
        [outs[0]] + [along_first(outs[step], step) for step in ORDER],
        [shape((OD, KE), F32 if b == 0 else BF) for b in range(YN)],
        "merge_first",
    )
    image_sums, totals = inside(
        final_kernel,
        [rows[0]] + [along_second(rows[step], step) for step in ORDER],
        [shape((OD, 2, KS), F32), shape((1, OD), F32)],
        "merge_second",
    )
    return image_sums, totals.reshape(OD), evidence


def solution(mesh):
    return jax.shard_map(
        shards,
        mesh=mesh,
        in_specs=(
            P(("dom", "orient"), None, None),
            P("orient", None, None),
            P(),
            P(("dom", "orient"), None, None),
            P(("dom", "orient"), None, None),
            P(),
        ),
        out_specs=(P("orient", None, "dom"), P("orient"), P(("dom", "orient"))),
        check_vma=False,
    )
```

```python
import math

import jax
import jax.numpy as jnp
from jax import lax
from jax.experimental import pallas as pl
from jax.experimental.pallas import tpu as pltpu
from jax.sharding import PartitionSpec as P

GRID = 64
K = 4096
BOX = 400
NTRANS = 25
CAP = 8
ZN = 4
YN = 4
XN = 4
DOM = 8
PART = 16
KS = K // DOM
K2 = 2 * KS
EXT = 128
KE = K2 + EXT
SLOTS = 128
OD = 32
YB = XN * OD
HALF = ZN * PART
PIECE = NTRANS * PART
BF = jnp.bfloat16
F32 = jnp.float32
BLOCK = 256
TOP = 32767.0
STEP = 64.0
OWNERS = YN * XN
INSIDE = pl.BlockSpec(memory_space=pltpu.VMEM)


def nt(left, right):
    return lax.dot_general(
        left, right, (((1,), (1,)), ((), ())), preferred_element_type=F32
    )


def tn(left, right):
    return lax.dot_general(
        left, right, (((0,), (0,)), ((), ())), preferred_element_type=F32
    )


def params(mib=16):
    return pltpu.CompilerParams(vmem_limit_bytes=mib * 1024 * 1024)


def lanes(shape):
    return lax.broadcasted_iota(jnp.int32, shape, len(shape) - 1)


def split3(value):
    high = value.astype(BF)
    rest = value - high.astype(F32)
    mid = rest.astype(BF)
    low = (rest - mid.astype(F32)).astype(BF)
    return high, mid, low


def pack2(total, lane):
    high = total.astype(BF).astype(F32)
    return jnp.where(lane == 0, high, jnp.where(lane == 1, total - high, 0.0))


def phase_tables(d, shifts_ref, cos_ref, sin_ref):
    coefficient = d * KS + lanes((1, KS))
    row_freq = coefficient // GRID - GRID // 2
    col_freq = coefficient % GRID - GRID // 2
    turns = jnp.concatenate(
        [row_freq * shifts_ref[0, t] + col_freq * shifts_ref[1, t] for t in range(NTRANS)], axis=0
    )
    angles = turns.astype(F32) * (2.0 * math.pi / BOX)
    cos_ref[...] = jnp.cos(angles)
    sin_ref[...] = jnp.sin(angles)


def scale_kernel(refs_hbm, noise_hbm, scaled_ref, refs_ref, noise_ref, sems):
    d = lax.axis_index("dom")
    span = pl.ds(pl.multiple_of(d * KS, KS), KS)
    copies = [
        pltpu.make_async_copy(refs_hbm.at[:, :, span], refs_ref, sems.at[0]),
        pltpu.make_async_copy(noise_hbm.at[:, span], noise_ref, sems.at[1]),
    ]
    for copy in copies:
        copy.start()
    for copy in copies:
        copy.wait()
    noise = noise_ref[...]
    total = jnp.zeros((OD, 1), F32)
    for part in range(2):
        values = refs_ref[:, part, :].astype(F32)
        scaled_ref[:, part * KS : (part + 1) * KS] = (values * noise).astype(BF)
        total = total + jnp.sum(noise * values * values, axis=1, keepdims=True)
    high, mid, low = [term.astype(F32) for term in split3(0.5 * total)]
    lane = lanes((OD, EXT))
    norms = jnp.where(lane == 0, high, jnp.where(lane == 1, mid, jnp.where(lane == 2, low, 0.0)))
    scaled_ref[:, K2:] = norms.astype(BF)


def prepare_kernel(
    shifts_hbm, images_hbm, ids_hbm, mask_hbm,
    near_ref, far_ref, code_ref, cos_ref, sin_ref,
    shifts_ref, images_ref, ids_ref, mask_ref, sems,
):
    d = lax.axis_index("dom")
    z = d // 2
    core = lax.rem(d, 2)
    copies = [
        pltpu.make_async_copy(shifts_hbm, shifts_ref, sems.at[0]),
        pltpu.make_async_copy(images_hbm, images_ref, sems.at[1]),
        pltpu.make_async_copy(ids_hbm, ids_ref, sems.at[2]),
        pltpu.make_async_copy(mask_hbm, mask_ref, sems.at[3]),
    ]
    for copy in copies:
        copy.start()
    copies[0].wait()
    phase_tables(d, shifts_ref, cos_ref, sin_ref)
    for copy in copies[1:]:
        copy.wait()
    marked = jnp.where(mask_ref[...] > 0, ids_ref[...] + OD, ids_ref[...])
    flat = jnp.concatenate([marked[:, c, :] for c in range(CAP)], axis=1)
    code_ref[...] = flat
    code = flat.astype(F32).astype(BF)
    for rz in range(ZN):
        for rc, out_ref in enumerate((near_ref, far_ref)):
            slot = lax.rem(z + rz, ZN) * 2 + (core if rc == 0 else 1 - core)
            span = pl.ds(pl.multiple_of(slot * KS, KS), KS)
            for part in range(2):
                out_ref[rz, :, part * KS : (part + 1) * KS] = images_ref[:, part, span]
            out_ref[rz, :, K2:] = code


def gather_kernel(b0_ref, b1_ref, b2_ref, b3_ref, line_ref):
    for place, ref in enumerate((b0_ref, b1_ref, b2_ref, b3_ref)):
        line_ref[place * OD : (place + 1) * OD, :] = ref[...]


def pair_kernel(near_ref, far_ref, *outs):
    for place, ref in enumerate(outs):
        ref[0] = near_ref[place]
        ref[1] = far_ref[place]


def stack_kernel(acc_ref, s1_ref, s2_ref, s3_ref, out_ref):
    del acc_ref
    for place, ref in enumerate((s1_ref, s2_ref, s3_ref)):
        out_ref[place] = ref[...]


def first_axis(core, along_x, along_y):
    return jnp.where(core == 0, along_x, along_y)


def slots_kernel(p0_ref, p1_ref, p2_ref, p3_ref, near_inv, near_count, far_inv, far_count):
    core = lax.rem(lax.axis_index("dom"), 2)
    j = lax.axis_index("orient")
    lane = lanes((HALF, SLOTS))
    pieces = (p0_ref, p1_ref, p2_ref, p3_ref)
    for rc, (inv_ref, count_ref) in enumerate(((near_inv, near_count), (far_inv, far_count))):
        code = jnp.concatenate([ref[rc, :, K2:].astype(F32) for ref in pieces], axis=0)
        code = code.astype(jnp.int32)
        for block in range(XN):
            along_x = first_axis(core, block, lane // OD)
            along_y = first_axis(core, lane // OD, block)
            owner = ((j // XN + along_y) % YN) * XN + (lax.rem(j, XN) + along_x) % XN
            inverse = jnp.zeros((HALF, YB), jnp.int32)
            count = jnp.zeros((HALF, YB), F32)
            for c in range(CAP):
                where_slot = c * OWNERS + owner
                seen = jnp.take_along_axis(code, where_slot, axis=1, mode="promise_in_bounds")
                match = seen == (lane % OD + OD)
                count = count + jnp.where(match, 1.0, 0.0)
                inverse = jnp.where(match, where_slot, inverse)
            inv_ref[:, block * YB : (block + 1) * YB] = inverse
            count_ref[:, block * YB : (block + 1) * YB] = count


def scores_kernel(rc, *refs):
    images = [ref[rc] for ref in refs[:ZN]]
    refs = refs[ZN:]
    refs_in = refs[:YN]
    cos_ref, sin_ref, shift_ref = refs[YN : YN + 3]
    outs = refs[YN + 3 : -1]
    weight_ref = refs[-1]
    core = lax.rem(lax.axis_index("dom"), 2)
    j = lax.axis_index("orient")
    lane8 = lanes((8, EXT))
    ones = jnp.where(lane8 < 3, 1.0, 0.0).astype(BF)
    norms = []
    for y in range(YN):
        weight_ref[y * YB : (y + 1) * YB, :] = refs_in[y][:, :K2]
        norms.append(nt(ones, refs_in[y][:, K2:])[0:1])
    lane = lanes((HALF, SLOTS))
    values = jnp.concatenate([part.astype(F32) for part in images], axis=0)
    code = values[:, K2:].astype(jnp.int32)
    owner = lane % OWNERS
    along_y = (owner // XN + YN - j // XN) % YN
    along_x = (owner % XN + XN - lax.rem(j, XN)) % XN
    line = first_axis(core, along_y, along_x)
    index = first_axis(core, along_x, along_y) * OD + code % OD
    real = values[:, :KS]
    imag = values[:, KS:K2]
    waiting = None
    for rz in range(ZN + 1):
        done = waiting
        if rz < ZN:
            part = slice(rz * PART, (rz + 1) * PART)
            base = rz * PIECE
            for t in range(NTRANS):
                cosine = cos_ref[t : t + 1, :]
                sine = sin_ref[t : t + 1, :]
                rows = slice(base + t * PART, base + (t + 1) * PART)
                shift_ref[rows, :KS] = (real[part] * cosine - imag[part] * sine).astype(BF)
                shift_ref[rows, KS:] = (real[part] * sine + imag[part] * cosine).astype(BF)
            waiting = nt(shift_ref[base : base + PIECE, :], weight_ref[...])
        if rz == 0:
            continue
        part = slice((rz - 1) * PART, rz * PART)
        for t in range(NTRANS):
            found = jnp.zeros((PART, SLOTS), F32)
            for y in range(YN):
                span = slice(y * YB, (y + 1) * YB)
                block = done[t * PART : (t + 1) * PART, span] - norms[y]
                picked = jnp.take_along_axis(
                    block, index[part], axis=1, mode="promise_in_bounds"
                )
                found = jnp.where(line[part] == y, picked, found)
            if rc == 0:
                outs[rz - 1][t] = found
            else:
                outs[0][rz - 1, t] = found


def scale_of(code):
    return jnp.exp(code * (math.log(2.0) / STEP)) * (1.0 / TOP)


def code_of(size):
    return jnp.floor(jnp.log(jnp.maximum(size, 1e-30)) * (STEP / math.log(2.0))) + 2.0


def add_kernel(partner_ref, *refs):
    lane = lanes((PART, SLOTS))
    refs[2 * ZN][...] = refs[0][...] + partner_ref[0]
    for rz in range(1, ZN):
        scores = refs[rz][...] + partner_ref[rz]
        valid = refs[ZN + rz][0, :, K2:].astype(F32) >= OD
        top = jnp.max(jnp.where(valid[None], scores, -1e30), axis=0)
        top = jnp.max(top, axis=1, keepdims=True)
        bottom = jnp.min(jnp.where(valid[None], scores, 1e30), axis=0)
        bottom = jnp.min(bottom, axis=1, keepdims=True)
        centre_code = code_of(jnp.maximum(jnp.abs(top), jnp.abs(bottom)))
        centre = jnp.floor(0.5 * (top + bottom) / scale_of(centre_code) + 0.5)
        offset = centre * scale_of(centre_code)
        size_code = code_of(jnp.maximum(top - offset, offset - bottom))
        whole = jnp.floor((scores - offset[None]) / scale_of(size_code)[None] + 0.5)
        whole = jnp.clip(whole, -TOP, TOP)
        row = jnp.where(lane == 0, centre_code, jnp.where(lane == 1, centre, size_code))
        out_ref = refs[2 * ZN + rz]
        out_ref[:NTRANS] = whole.astype(jnp.int32).astype(jnp.int16)
        out_ref[NTRANS] = row.astype(jnp.int32).astype(jnp.int16)


def sent_scores(ref):
    values = ref[...].astype(jnp.int32).astype(F32)
    row = values[NTRANS]
    offset = row[:, 1:2] * scale_of(row[:, 0:1])
    return values[:NTRANS] * scale_of(row[:, 2:3])[None] + offset[None]


def posterior_kernel(own_ref, one_ref, two_ref, three_ref, code_ref, weight_ref, evidence_ref):
    valid = code_ref[...] >= OD
    scores = own_ref[...]
    for ref in (one_ref, two_ref, three_ref):
        scores = scores + sent_scores(ref)
    masked = jnp.where(valid[None], scores, -1e30)
    highest = jnp.max(jnp.max(masked, axis=0), axis=1, keepdims=True)
    terms = jnp.where(valid[None], jnp.exp(scores - highest[None]), 0.0)
    summed = jnp.sum(jnp.sum(terms, axis=0), axis=1, keepdims=True)
    evidence = highest + jnp.log(summed)
    weights = jnp.where(valid[None], jnp.exp(scores - evidence[None]), 0.0)
    weight_ref[...] = weights.astype(BF)
    evidence_ref[...] = jnp.broadcast_to(evidence, evidence_ref.shape)


def dense_rows(blocks, stack_ref, first, inv_ref, count_ref, dense_ref):
    column = []
    ones = jnp.ones((PART, EXT), BF)
    for place, block in enumerate(blocks):
        span = slice(block * YB, (block + 1) * YB)
        columns = slice(place * YB, (place + 1) * YB)
        total = jnp.zeros((PART, YB), F32)
        for r in range(stack_ref.shape[0]):
            part = slice((first + r) * PART, (first + r + 1) * PART)
            inverse = inv_ref[part, span]
            count = count_ref[part, span]
            for t in range(NTRANS):
                slots = stack_ref[r, t].astype(F32)
                picked = jnp.take_along_axis(slots, inverse, axis=1, mode="promise_in_bounds")
                weight = (picked * count).astype(BF)
                start = r * PIECE + t * PART
                dense_ref[start : start + PART, columns] = weight
                total = total + weight.astype(F32)
        summed = jnp.zeros((YB, EXT), F32)
        for term in split3(total):
            summed = summed + tn(term, ones)
        column.append(summed)
    return column


def sums_kernel(blocks, firsts, offset, finished, *refs):
    groups = len(firsts)
    dense = refs[len(refs) - groups :]
    refs = refs[: len(refs) - groups]
    columns, shifts = [], []
    for group, first in enumerate(firsts):
        stack_ref, shift_ref, inv_ref, count_ref = refs[4 * group : 4 * group + 4]
        columns.append(dense_rows(blocks, stack_ref, first, inv_ref, count_ref, dense[group]))
        shifts.append((shift_ref, slice(first * PIECE, (first + stack_ref.shape[0]) * PIECE)))
    refs = refs[4 * groups :]
    before = offset is not None
    if before:
        acc_ref = refs[0]
        refs = refs[1:]
        held = slice(offset * YB, (offset + len(blocks)) * YB)
    lane = lanes((YB, EXT))
    for place in range(len(blocks)):
        rows = slice(place * YB, (place + 1) * YB)
        total = sum(column[place] for column in columns)
        if before:
            total = total + acc_ref[(offset + place) * YB : (offset + place + 1) * YB, K2:]
        if finished:
            refs[place][:, K2:] = pack2(total, lane).astype(refs[place].dtype)
        else:
            refs[0][rows, K2:] = total
    for part in range(K2 // BLOCK):
        span = slice(part * BLOCK, (part + 1) * BLOCK)
        sums = tn(dense[0][...], shifts[0][0][shifts[0][1], span])
        for group in range(1, groups):
            sums = sums + tn(dense[group][...], shifts[group][0][shifts[group][1], span])
        if before:
            sums = sums + acc_ref[held, span]
        if finished:
            for place in range(len(blocks)):
                rows = slice(place * YB, (place + 1) * YB)
                refs[place][:, span] = sums[rows, :].astype(refs[place].dtype)
        else:
            refs[0][:, span] = sums


def merge_kernel(own_ref, one_ref, two_ref, three_ref, *outs):
    lane = lanes((OD, EXT))
    for b in range(YN):
        rows = slice(b * OD, (b + 1) * OD)
        block = own_ref[rows, :]
        for other in (one_ref, two_ref, three_ref):
            block = block + other[rows, :].astype(F32)
        total = jnp.sum(block[:, K2:], axis=1, keepdims=True)
        outs[b][:, :K2] = block[:, :K2].astype(outs[b].dtype)
        outs[b][:, K2:] = pack2(total, lane).astype(outs[b].dtype)


def final_kernel(own_ref, one_ref, two_ref, three_ref, sum_ref, total_ref):
    block = own_ref[...]
    for other in (one_ref, two_ref, three_ref):
        block = block + other[...].astype(F32)
    sum_ref[:, 0, :] = block[:, :KS]
    sum_ref[:, 1, :] = block[:, KS:K2]
    ones = jnp.ones((8, EXT), BF)
    row = jnp.zeros((8, OD), F32)
    for term in split3(block[:, K2:]):
        row = row + nt(ones, term)
    total_ref[...] = row[0:1]


def shape(dims, dtype):
    return jax.ShapeDtypeStruct(dims, dtype)


def dom_core():
    return [(d, d ^ 1) for d in range(DOM)]


def along_z(value, step):
    return lax.ppermute(value, "dom", [(d, (d + 2 * step) % DOM) for d in range(DOM)])


def turn(step, first):
    pairs = []
    for d in range(DOM):
        for y in range(YN):
            for x in range(XN):
                if (d % 2 == 0) == first:
                    owner = y * XN + (x + step) % XN
                else:
                    owner = ((y + step) % YN) * XN + x
                pairs.append((d * OWNERS + y * XN + x, d * OWNERS + owner))
    return pairs


ORDER = (2, 1, 3)
BOTH = ("dom", "orient")


def along_first(value, step):
    return lax.ppermute(value, BOTH, turn(step, True))


def along_second(value, step):
    return lax.ppermute(value, BOTH, turn(step, False))


def cost(flops, moved):
    return pl.CostEstimate(flops=flops, bytes_accessed=moved, transcendentals=0)


def inside(kernel, arguments, out_shape, name, flops=0, scratch=(), mib=16):
    single = not isinstance(out_shape, list)
    return pl.pallas_call(
        kernel,
        in_specs=[INSIDE] * len(arguments),
        out_specs=INSIDE if single else [INSIDE] * len(out_shape),
        out_shape=out_shape,
        scratch_shapes=list(scratch),
        compiler_params=params(mib),
        cost_estimate=cost(flops, 2**20),
        name=name,
    )(*arguments)


def score_half(rc, images, lines, cosine, sine):
    part = shape((NTRANS, PART, SLOTS), F32)
    return inside(
        lambda *refs: scores_kernel(rc, *refs),
        [*images, *lines, cosine, sine],
        [shape((NTRANS * HALF, K2), BF)]
        + ([part] * ZN if rc == 0 else [shape((ZN, NTRANS, PART, SLOTS), F32)]),
        "scores",
        flops=2 * NTRANS * HALF * K2 * YN * YB,
        scratch=[pltpu.VMEM((YN * YB, K2), BF)],
    )


def weighted_sums(blocks, groups, first, acc, offset, finished, name):
    arguments = [array for group in groups for array in group]
    if acc is not None:
        arguments.append(acc)
    if finished:
        out = [shape((YB, KE), F32 if block == 0 else BF) for block in blocks]
    else:
        out = [shape((len(blocks) * YB, KE), F32)]
    rows = groups[0][0].shape[0] * PIECE
    return inside(
        lambda *refs: sums_kernel(blocks, [first] * len(groups), offset, finished, *refs),
        arguments,
        out,
        name,
        flops=len(groups) * len(blocks) * 2 * rows * K2 * YB,
        scratch=[pltpu.VMEM((rows, len(blocks) * YB), BF)] * len(groups),
    )


def loader(kernel, arguments, out_shape, scratch, name):
    return pl.pallas_call(
        kernel,
        in_specs=[pl.BlockSpec(memory_space=pltpu.HBM)] * len(arguments),
        out_specs=[INSIDE] * len(out_shape),
        out_shape=out_shape,
        scratch_shapes=scratch + [pltpu.SemaphoreType.DMA((len(arguments),))],
        compiler_params=params(8),
        name=name,
    )(*[pltpu.with_memory_space_constraint(value, pltpu.HBM) for value in arguments])


def shards(images, references, noise_weight, candidate_ids, candidate_mask, shifts):
    (scaled,) = loader(
        scale_kernel,
        [references, noise_weight.reshape(1, K)],
        [shape((OD, KE), BF)],
        [pltpu.VMEM((OD, 2, KS), BF), pltpu.VMEM((1, KS), F32)],
        "scale",
    )
    codes = pltpu.VMEM((PART, CAP, OWNERS), jnp.int32)
    near, far, code, cosine, sine = loader(
        prepare_kernel,
        [
            shifts.T,
            images,
            jnp.swapaxes(candidate_ids, 1, 2),
            jnp.swapaxes(candidate_mask, 1, 2),
        ],
        [shape((ZN, PART, KE), BF)] * 2
        + [shape((PART, SLOTS), jnp.int32)]
        + [shape((NTRANS, KS), F32)] * 2,
        [pltpu.SMEM((2, NTRANS), jnp.int32), pltpu.VMEM((PART, 2, K), BF), codes, codes],
        "prepare",
    )
    far = lax.ppermute(far, "dom", dom_core())
    blocks = {0: scaled}
    for step in ORDER:
        blocks[(-step) % XN] = along_first(scaled, step)
    pairs = inside(pair_kernel, [near, far], [shape((2, PART, KE), BF)] * ZN, "pair_images")
    pieces = {0: pairs[0]}
    for step in ORDER:
        pieces[(-step) % ZN] = along_z(pairs[step], step)
    pieces = [pieces[rz] for rz in range(ZN)]
    line = inside(
        gather_kernel, [blocks[b] for b in range(XN)], shape((YB, KE), BF), "gather"
    )
    lines = {0: line}
    for step in ORDER:
        lines[(-step) % YN] = along_second(line, step)
    lines = [lines[y] for y in range(YN)]
    far_shift, far_slots = score_half(1, pieces, lines, cosine, sine)
    partner = lax.ppermute(far_slots, "dom", dom_core())
    near_shift, *near_slots = score_half(0, pieces, lines, cosine, sine)
    part = shape((NTRANS, PART, SLOTS), F32)
    sent = shape((NTRANS + 1, PART, SLOTS), jnp.int16)
    slots = inside(add_kernel, [partner, *near_slots, *pieces], [part] + [sent] * (ZN - 1), "add_cores")
    arrived = [along_z(slots[step], step) for step in ORDER]
    near_inv, near_count, far_inv, far_count = inside(
        slots_kernel,
        pieces,
        [shape((HALF, YN * YB), jnp.int32), shape((HALF, YN * YB), F32)] * 2,
        "slot_map",
    )
    code, near_inv, near_count, far_inv, far_count = lax.optimization_barrier(
        (code, near_inv, near_count, far_inv, far_count)
    )
    weights, evidence = inside(
        posterior_kernel,
        [slots[0], *arrived, code],
        [shape((NTRANS, PART, SLOTS), BF), shape((PART, SLOTS), F32)],
        "posterior",
    )

    mine = {}
    for step in (3, 1, 2):
        mine[(-step) % ZN] = along_z(weights, step)
    own = weights.reshape(1, NTRANS, PART, SLOTS)
    other = lax.ppermute(own, "dom", dom_core())
    near_inv, evidence = lax.optimization_barrier((near_inv, evidence[:, 0]))
    near_maps = (near_shift, near_inv, near_count)
    far_maps = (far_shift, far_inv, far_count)
    targets = (2, 1, 3, 0)
    (acc,) = weighted_sums(
        targets, [(own, *near_maps), (other, *far_maps)], 0, None, None, False, "own_sums"
    )
    near_rest = inside(
        stack_kernel,
        [acc] + [mine[rz] for rz in range(1, ZN)],
        shape((ZN - 1, NTRANS, PART, SLOTS), BF),
        "stack_weights",
    )
    far_rest = lax.ppermute(near_rest, "dom", dom_core())
    near_group = (near_rest, *near_maps)
    far_group = (far_rest, *far_maps)
    outs = {}
    (pair,) = weighted_sums((2, 1, 3), [near_group], 1, acc, 0, False, "near_sums")
    outs[2], outs[1], outs[3] = weighted_sums((2, 1, 3), [far_group], 1, pair, 0, True, "far_sums")
    acc, outs[2] = lax.optimization_barrier((acc, outs[2]))
    for place in (3,):
        target = targets[place]
        (outs[target],) = weighted_sums(
            (target,), [near_group, far_group], 1, acc, place, True, "both_sums"
        )
    rows = inside(
        merge_kernel,
        [outs[0]] + [along_first(outs[step], step) for step in ORDER],
        [shape((OD, KE), F32 if b == 0 else BF) for b in range(YN)],
        "merge_first",
    )
    image_sums, totals = inside(
        final_kernel,
        [rows[0]] + [along_second(rows[step], step) for step in ORDER],
        [shape((OD, 2, KS), F32), shape((1, OD), F32)],
        "merge_second",
    )
    return image_sums, totals.reshape(OD), evidence


def solution(mesh):
    return jax.shard_map(
        shards,
        mesh=mesh,
        in_specs=(
            P(("dom", "orient"), None, None),
            P("orient", None, None),
            P(),
            P(("dom", "orient"), None, None),
            P(("dom", "orient"), None, None),
            P(),
        ),
        out_specs=(P("orient", None, "dom"), P("orient"), P(("dom", "orient"))),
        check_vma=False,
    )
```
